32 devices in a mesh: seq: 16 (over z, y, core), head: 2 (over x).
Axes of the slice: x: 2, y: 2, z: 4, core: 2. Of those that a mesh axis runs over, the one named last changes fastest.
Arguments:
- tokens: bfloat16 [8192, 768], P('seq'), may hold values from -6 to 6
- norm1_gain: float32 [768], replicated, may hold values from 0.5 to 1.5
- norm1_shift: float32 [768], replicated, may hold values from -0.18 to 0.18
- w_query: bfloat16 [768, 768], P(None, 'head'), may hold values from -1.9453125 to 1.9453125
- w_key: bfloat16 [768, 768], P(None, 'head'), may hold values from -0.21875 to 0.21875
- w_value: bfloat16 [768, 768], P(None, 'head'), may hold values from -0.21875 to 0.21875
- w_output: bfloat16 [768, 768], P('head'), may hold values from -11.75 to 11.75
- norm2_gain: float32 [768], replicated, may hold values from 0.5 to 1.5
- norm2_shift: float32 [768], replicated, may hold values from -1.8 to 1.8
- w_in: bfloat16 [768, 3072], P(None, 'head'), may hold values from -0.21875 to 0.21875
- w_out: bfloat16 [3072, 768], P('head'), may hold values from -0.109375 to 0.109375
- cluster_ids: int32 [8192, 12], P('seq', 'head'), may hold values from 0 to 99
- masked_keys: int32 [1024], replicated, may hold values from 0 to 8191
- cotangent: bfloat16 [8192, 768], P('seq'), may hold values from -6 to 6
Outputs:
- block_out: bfloat16 [8192, 768], P('seq')
- grad_tokens: float32 [8192, 768], P('seq')
- grad_norm1_gain: float32 [768], replicated
- grad_norm1_shift: float32 [768], replicated
- grad_query: float32 [768, 768], P(None, 'head')
- grad_key: float32 [768, 768], P(None, 'head')
- grad_value: float32 [768, 768], P(None, 'head')
- grad_output: float32 [768, 768], P('head')
- grad_norm2_gain: float32 [768], replicated
- grad_norm2_shift: float32 [768], replicated
- grad_in: float32 [768, 3072], P(None, 'head')
- grad_out: float32 [3072, 768], P('head')
The draws below stay inside these ranges and needn't reach their ends.
Inputs may be any that keep to these rules, and one draw needn't show every extreme that they name: `masked_keys`: key positions, possibly repeated.
All inputs are finite; a program needn't handle non-finite values.
Results may differ from the reference program's by a relative error of at most 0.01.
Values may be sent and summed in bfloat16 or wider, within the bound.
A program may use at most 128 MiB of HBM per device.

```python
import jax
import jax.numpy as jnp
from jax import lax

D = 768
HEADS = 12
HDIM = 64
FF = 3072
CLUSTERS = 100
TOKENS = 8192
MASKED = 1024


def set_ends(array, own_key, smallest, top_value):
    index_at = [jax.random.randint(jax.random.fold_in(own_key, axis), (), 0, length) for axis, length in enumerate(array.shape)]
    main_axis = array.shape.index(max(array.shape))
    next_to = index_at[:main_axis] + [(index_at[main_axis] + 1) % array.shape[main_axis]] + index_at[main_axis + 1:]
    return array.at[tuple(index_at)].set(smallest).at[tuple(next_to)].set(top_value)


def shard_levels(own_key, dims, split, least, top_value):
    factor_of, own = 1.0, jax.random.fold_in(own_key, 6)
    for position, blocks in split:
        draws = jnp.exp(jax.random.uniform(jax.random.fold_in(own, position), (blocks,), jnp.float32, least / len(split), top_value / len(split)))
        factor_of = factor_of * jnp.repeat(draws, dims[position] // blocks).reshape([-1 if axis == position else 1 for axis in range(len(dims))])
    return factor_of


def bell_draw(stream_key, shape, deviation, most, cuts=(), kind=jnp.bfloat16):
    values = deviation * jax.random.normal(stream_key, shape, jnp.float32)
    if cuts:
        values = values * shard_levels(stream_key, shape, cuts, -0.22, 0.18)
    return jnp.clip(values, -most, most).astype(kind)


def setup_inputs(seed: int = 0) -> dict:
    splits = jax.random.split(jax.random.key(seed), 15)
    tokens = bell_draw(splits[0], (TOKENS, D), 1.0, 6.0, ((0, 16),))
    norm1_gain = jnp.clip(1.0 + 0.1 * jax.random.normal(splits[1], (D,), jnp.float32), 0.5, 1.5)
    norm1_shift = bell_draw(splits[2], (D,), 0.03, 0.18, (), jnp.float32)
    w_query = bell_draw(splits[3], (D, D), ((TOKENS // CLUSTERS) ** 0.5 * D ** -0.5), 1.9453125, ((1, 2),))
    w_key = bell_draw(splits[4], (D, D), D ** -0.5, 0.21875, ((1, 2),))
    w_value = bell_draw(splits[5], (D, D), D ** -0.5, 0.21875, ((1, 2),))
    w_output = bell_draw(splits[6], (D, D), (0.6 * TOKENS ** 0.5 * D ** -0.5), 11.75, ((0, 2),))
    norm2_gain = jnp.clip(1.0 + 0.1 * jax.random.normal(splits[7], (D,), jnp.float32), 0.5, 1.5)
    norm2_shift = bell_draw(splits[8], (D,), 0.3, 1.8, (), jnp.float32)
    w_in = bell_draw(splits[9], (D, FF), D ** -0.5, 0.21875, ((1, 2),))
    w_out = bell_draw(splits[10], (FF, D), FF ** -0.5, 0.109375, ((0, 2),))
    cluster_ids = set_ends(jax.random.randint(splits[11], (TOKENS, HEADS), 0, CLUSTERS), jax.random.fold_in(splits[11], 1), 0, CLUSTERS - 1).astype(jnp.int32)
    masked_keys = set_ends(jax.random.randint(splits[12], (MASKED,), 0, TOKENS), jax.random.fold_in(splits[12], 1), 0, TOKENS - 1).astype(jnp.int32)
    cotangent = bell_draw(splits[13], (TOKENS, D), 1.0, 6.0, ((0, 16),))
    return {"tokens": tokens, "norm1_gain": norm1_gain, "norm1_shift": norm1_shift, "w_query": w_query, "w_key": w_key, "w_value": w_value, "w_output": w_output, "norm2_gain": norm2_gain, "norm2_shift": norm2_shift, "w_in": w_in, "w_out": w_out, "cluster_ids": cluster_ids, "masked_keys": masked_keys, "cotangent": cotangent}


HIGHEST_PRECISION = lax.Precision.HIGHEST
EPSILON = 1e-05

@jax.custom_vjp
def low(v):
    return lax.optimization_barrier(v.astype(jnp.bfloat16)).astype(jnp.float32)

@jax.custom_vjp
def low_back(v):
    return v

def low_keep(v):
    return (low(v), None)

def low_pass(kept, grad):
    return (grad,)

def back_keep(v):
    return (v, None)

def back_low(kept, grad):
    return (low(grad),)
low.defvjp(low_keep, low_pass)
low_back.defvjp(back_keep, back_low)

def layer_norm(values, gain, shift):
    mean = lax.optimization_barrier(jnp.mean(values, axis=-1, keepdims=True))
    centred = values - mean
    inverse = lax.rsqrt(lax.optimization_barrier(jnp.mean(centred * centred, axis=-1, keepdims=True)) + EPSILON)
    return centred * inverse * gain + shift

def reference(tokens, norm1_gain, norm1_shift, w_query, w_key, w_value, w_output, norm2_gain, norm2_shift, w_in, w_out, cluster_ids, masked_keys, cotangent):
    scale = HDIM ** (-0.5)
    onehot = (cluster_ids[:, :, None] == jnp.arange(CLUSTERS, dtype=jnp.int32)[None, None, :]).astype(jnp.float32)
    blocked = jnp.zeros((TOKENS,), jnp.bool_).at[masked_keys].set(True)
    keep = jnp.logical_not(blocked)

    def forward(inputs, gain1, shift1, wq, wk, wv, wo, gain2, shift2, wi, wout):
        normed = low(layer_norm(inputs, gain1, shift1))

        def project(weight):
            product = jnp.dot(normed, weight, precision=HIGHEST_PRECISION)
            return low(low_back(product)).reshape(TOKENS, HEADS, HDIM)
        query = project(wq)
        keys = project(wk)
        values = project(wv)
        sums = jnp.einsum('thc,thd->hcd', onehot, query, precision=HIGHEST_PRECISION)
        counts = lax.optimization_barrier(jnp.sum(onehot, axis=0))
        centroid = low(sums / jnp.maximum(counts, 1.0)[:, :, None])
        raw = jnp.einsum('hcd,thd->hct', centroid, keys, precision=HIGHEST_PRECISION)
        scores = jnp.where(keep[None, None, :], low_back(raw * scale), -1e+30)
        top = lax.optimization_barrier(jnp.max(scores, axis=-1, keepdims=True))
        lse = top + jnp.log(lax.optimization_barrier(jnp.sum(jnp.exp(scores - top), axis=-1, keepdims=True)))
        probs = low(jnp.exp(scores - lse))
        cluster_out = low(low_back(jnp.einsum('hct,thd->hcd', probs, values, precision=HIGHEST_PRECISION)))
        gathered = jnp.einsum('thc,hcd->thd', onehot, cluster_out, precision=HIGHEST_PRECISION).reshape(TOKENS, D)
        attn = low_back(jnp.dot(gathered, wo, precision=HIGHEST_PRECISION))
        resid = inputs + attn
        normed2 = low(layer_norm(resid, gain2, shift2))
        upper = low_back(jnp.dot(normed2, wi, precision=HIGHEST_PRECISION))
        act = low(jax.nn.gelu(upper, approximate=False))
        return resid + jnp.dot(act, wout, precision=HIGHEST_PRECISION)
    primals = (tokens.astype(jnp.float32), norm1_gain, norm1_shift, w_query.astype(jnp.float32), w_key.astype(jnp.float32), w_value.astype(jnp.float32), w_output.astype(jnp.float32), norm2_gain, norm2_shift, w_in.astype(jnp.float32), w_out.astype(jnp.float32))
    result, pullback = jax.vjp(forward, *primals)
    grads = pullback(cotangent.astype(jnp.float32))
    return (result.astype(jnp.bfloat16), grads[0], grads[1], grads[2], grads[3], grads[4], grads[5], grads[6], grads[7], grads[8], grads[9], grads[10])
```

```python
import functools
from types import SimpleNamespace

import jax
import jax.numpy as jnp
from jax import lax
from jax.experimental import pallas as pl
from jax.experimental.pallas import tpu as pltpu
from jax.sharding import PartitionSpec as P

CLUSTERS = 100
EPSILON = 1e-05
MESH = pl.DeviceIdType.MESH
F32 = jnp.float32
BF16 = jnp.bfloat16
SLOT = 128
GROUP = 16
GROUPS = -(-CLUSTERS // GROUP)
SENT = GROUPS * GROUP
STREAMS = 8


def mm(a, b):
    return lax.dot_general(a, b, (((1,), (0,)), ((), ())), preferred_element_type=F32)


def mm_nt(a, b):
    return lax.dot_general(a, b, (((1,), (1,)), ((), ())), preferred_element_type=F32)


def mm_tn(a, b):
    return lax.dot_general(a, b, (((0,), (0,)), ((), ())), preferred_element_type=F32)


def aligned(index, size):
    return pl.ds(pl.multiple_of(index, size), size)


def remote(src, dst, send_sem, recv_sem, device):
    return pltpu.make_async_remote_copy(
        src_ref=src, dst_ref=dst, send_sem=send_sem, recv_sem=recv_sem, device_id=device, device_id_type=MESH
    )


def loop(count, body):
    def step(i, carry):
        body(i)
        return carry

    lax.fori_loop(0, count, step, 0)


def normalize(values):
    centred = values - jnp.mean(values, axis=-1, keepdims=True)
    inverse = lax.rsqrt(jnp.mean(centred * centred, axis=-1, keepdims=True) + EPSILON)
    return centred * inverse, inverse


def normalize_back(grad, gain, scaled, inverse):
    inner = grad * gain
    return inverse * (
        inner - jnp.mean(inner, axis=-1, keepdims=True) - scaled * jnp.mean(inner * scaled, axis=-1, keepdims=True)
    )


def fold_rows(values):
    return jnp.sum(values.reshape(values.shape[0] // 8, 8, values.shape[1]), axis=0)


def kernel(cfg, names, *all_refs):
    r = SimpleNamespace(**dict(zip(names, all_refs)))
    S, T, D, W, LH, F = cfg.S, cfg.T, cfg.D, cfg.W, cfg.LH, cfg.F
    pairs = LH // 2
    half = T // 2
    scale = (W // LH) ** (-0.5)
    ring = cfg.ring
    n = S // 2
    s = lax.axis_index("seq")
    h = lax.axis_index("head")
    oh = 1 - h
    core = lax.rem(s, 2)
    chip = lax.div(s, 2)
    me = s * 2 + h
    x_dev = (s, oh)
    sib_dev = (s + 1 - 2 * core, h)
    first = S // 4
    is_owner = jnp.logical_and(s >= first, s < first + GROUPS)
    group = s - first
    lanes = lax.broadcasted_iota(jnp.int32, (1, 128), 1)
    left = lanes < 64

    def fold(block):
        return jnp.where(left, block[:SLOT], block[SLOT:])

    def unfold(block):
        zero = jnp.zeros_like(block)
        return jnp.concatenate([jnp.where(left, block, zero), jnp.where(left, zero, block)], axis=0)

    def expand(stats):
        return jnp.concatenate(
            [jnp.where(left, stats[:, 2 * p : 2 * p + 1], stats[:, 2 * p + 1 : 2 * p + 2]) for p in range(pairs)], axis=1
        )

    def column(stats, p, at=0):
        return jnp.concatenate(
            [stats[:, at + 2 * p : at + 2 * p + 1], stats[:, at + 2 * p + 1 : at + 2 * p + 2]], axis=0
        )

    def place(columns, p, at=0):
        rows = columns.shape[0] // 2
        return jnp.where(lanes == at + 2 * p, columns[:rows], 0.0) + jnp.where(
            lanes == at + 2 * p + 1, columns[rows:], 0.0
        )

    def pair(p):
        return slice(p * 128, (p + 1) * 128)

    def pair_rows(p):
        return slice(p * 2 * SLOT, (p + 1) * 2 * SLOT)

    at_end = []

    loads = {}
    for i, name in enumerate(
        ["g1", "b1", "ids", "tok", "wq", "keep", "wk", "wv", "cot", "wout", "wo", "win", "g2", "b2"]
    ):
        dst = getattr(r, "v_" + name)
        dst = {"cot": lambda d: d.at[0], "wq": lambda d: d.at[h], "wo": lambda d: d.at[h], "ids": lambda d: d.at[h]}.get(
            name, lambda d: d
        )(dst)
        loads[name] = pltpu.make_async_copy(getattr(r, name), dst, r.load_sem.at[i])

    barrier = pltpu.get_barrier_semaphore()

    def greet(k):
        other = lax.rem(me + k + 1, 2 * S)
        pl.semaphore_signal(
            barrier, inc=1, device_id=(lax.div(other, 2), lax.rem(other, 2)), device_id_type=MESH
        )

    loop(2 * S - 1, greet)
    for load in loads.values():
        load.start()

    exchanges = {}

    def send(name, src, dst, device):
        i = len(exchanges)
        copy = remote(src, dst, r.ex_send.at[i], r.ex_recv.at[i], device)
        copy.start()
        exchanges[name] = copy
        at_end.append(copy.wait_send)

    def arrive(name):
        exchanges[name].wait_recv()

    counters = {"scatter": 0, "spread": 0}

    def scatter(src, dst, slot, plane):
        i = counters["scatter"]
        counters["scatter"] += 1

        def at(g):
            rows = pl.ds(g * GROUP, GROUP)
            mine = jnp.logical_and(s == first + g, h == plane)
            copy = remote(src.at[rows], dst.at[slot], r.sc_send.at[i, g], r.sc_recv.at[cfg.scatter_of[i]], (first + g, plane))
            return rows, mine, copy

        for g in range(GROUPS):
            rows, mine, copy = at(g)

            @pl.when(jnp.logical_not(mine))
            def _():
                copy.start()

            @pl.when(mine)
            def _():
                dst[slot] = src[rows, :]

        def finish():
            for g in range(GROUPS):
                rows, mine, copy = at(g)

                @pl.when(jnp.logical_not(mine))
                def _():
                    copy.wait_send()

        at_end.append(finish)

    def gathered_at_owner(buf, count, i):
        block = buf.at[pl.ds(0, count - 1)]
        remote(block, block, r.sc_send.at[0, 0], r.sc_recv.at[i], x_dev).wait_recv()

    def spread(buf, i, planes, like):
        rows = aligned(group * GROUP, GROUP)
        block = buf.at[rows]

        def to(k):
            copy = remote(block, block, r.sp_send.at[i], r.sp_recv.at[i, h, group], (lax.rem(s + k + 1, S), h))
            copy.start()

        def across(k):
            copy = remote(block, block, r.sp_send.at[i], r.sp_recv.at[i, h, group], (lax.rem(s + k, S), oh))
            copy.start()

        loop(S - 1, to)
        if planes == 2:
            loop(S, across)

        def finish():
            @pl.when(is_owner)
            def _():
                block = like.at[pl.ds(0, S * planes - 1)]
                remote(block, block, r.sp_send.at[i], r.sp_recv.at[i, 0, 0], x_dev).wait_send()

        at_end.append(finish)

    def spread_arrive(buf, i, from_plane=None):
        for g in range(GROUPS):
            mine = s == first + g
            plane = h
            if from_plane is not None:
                mine = jnp.logical_and(mine, h == from_plane)
                plane = from_plane

            @pl.when(jnp.logical_not(mine))
            def _():
                block = buf.at[pl.ds(g * GROUP, GROUP)]
                remote(block, block, r.sp_send.at[i], r.sp_recv.at[i, plane, g], x_dev).wait_recv()

    def total_of(buf, count):
        def add(i, acc):
            return acc + buf[i].astype(F32)

        return lax.fori_loop(0, count, add, jnp.zeros((GROUP, buf.shape[-1]), F32))

    r.ag1[...] = jnp.zeros_like(r.ag1)
    r.ag3[...] = jnp.zeros_like(r.ag3)
    r.ag2[...] = jnp.zeros_like(r.ag2)
    r.ag4[...] = jnp.zeros_like(r.ag4)
    r.aglse[...] = jnp.zeros_like(r.aglse)
    r.agdelta[...] = jnp.zeros_like(r.agdelta)
    r.norm_grads[...] = jnp.zeros_like(r.norm_grads)

    def onehot_t(x):
        ids = r.v_ids[x]
        rows = lax.broadcasted_iota(jnp.int32, (SLOT, T), 0)
        for j in range(LH):
            r.oht[x, j * SLOT : (j + 1) * SLOT, :] = jnp.where(rows == ids[j : j + 1, :], 1.0, 0.0).astype(BF16)

    def onehot(x):
        for p in range(pairs):
            r.oh[x, :, pair_rows(p)] = r.oht[x, pair_rows(p), :].T

    loads["ids"].wait()
    onehot_t(h)
    for name in ["g1", "b1", "tok"]:
        loads[name].wait()

    def first_norm(i):
        rows = aligned(i * 64, 64)
        scaled, _ = normalize(r.v_tok[rows, :].astype(F32))
        r.nrm[rows, :] = (scaled * r.v_g1[...] + r.v_b1[...]).astype(BF16)

    loop(T // 64, first_norm)
    loads["wq"].wait()

    def project(weight, out):
        def tile(i):
            rows = aligned(i * 256, 256)
            out[rows, :] = mm(r.nrm[rows, :], weight).astype(BF16)

        loop(T // 256, tile)

    project(r.v_wq[h], r.q)
    counts = jnp.zeros((SLOT, 128), F32)
    ones = jnp.ones((T, 128), BF16)
    for p in range(pairs):
        hot = r.oht[h, pair_rows(p), :]
        r.sums[:, pair(p)] = fold(mm(hot, r.q[:, pair(p)]))[:SENT].astype(BF16)
        counts = counts + place(mm(hot, ones)[:, :1], p)
    r.counts[...] = counts[:SENT]

    pl.semaphore_wait(barrier, 2 * S - 1)
    scatter(r.sums, r.rs, s, h)
    scatter(r.counts, r.rss, s, h)
    send("ids", r.v_ids.at[h], r.v_ids.at[h], x_dev)
    loads["wo"].wait()
    send("wo", r.v_wo.at[h], r.v_wo.at[h], x_dev)
    send("wq", r.v_wq.at[h], r.v_wq.at[h], x_dev)
    sib_half = pl.ds(pl.multiple_of((1 - core) * W, 128), W)
    own_half = pl.ds(pl.multiple_of(core * W, 128), W)
    loads["cot"].wait()
    send("cot", r.v_cot.at[0], r.v_cot.at[1], sib_dev)
    send("nrm", r.nrm.at[:, sib_half], r.nrm_sib, sib_dev)

    loads["wk"].wait()
    project(r.v_wk[...], r.k)
    loads["wv"].wait()
    project(r.v_wv[...], r.v)
    loads["wout"].wait()

    def d_act(j):
        cols = aligned(j * 256, 256)
        r.dact[:, cols] = mm_nt(r.v_cot[0], r.v_wout[cols, :])

    loop(F // 256, d_act)
    onehot(h)

    @pl.when(is_owner)
    def _():
        gathered_at_owner(r.rs, S, 0)
        gathered_at_owner(r.rss, S, 1)
        divisor = jnp.maximum(expand(total_of(r.rss, S)), 1.0)
        r.divisor[...] = divisor
        r.ag1[aligned(group * GROUP, GROUP), :] = (total_of(r.rs, S) / divisor).astype(BF16)
        spread(r.ag1, 0, 1, r.rs)

    arrive("ids")
    onehot_t(oh)
    onehot(oh)
    loads["keep"].wait()
    spread_arrive(r.ag1, 0)

    keep = r.v_keep[...]
    stats = jnp.zeros((SLOT, 128), F32)
    for p in range(pairs):
        scores = mm_nt(unfold(r.ag1[:, pair(p)]), r.k[:, pair(p)]) * scale
        scores = jnp.where(keep > 0, scores, -1e30)
        top = jnp.max(scores, axis=1, keepdims=True)
        weights = jnp.exp(scores - top) * keep
        r.e[pair_rows(p), :] = weights
        total = jnp.sum(weights, axis=1, keepdims=True)
        r.numer[:, pair(p)] = fold(mm(weights.astype(BF16), r.v[:, pair(p)]))[:SENT].astype(BF16)
        stats = stats + place(top, p) + place(total, p, 8)
    r.stats[...] = stats
    scatter(r.numer, r.rs, s, h)
    scatter(r.stats.at[pl.ds(0, SENT)], r.rss, s, h)

    @pl.when(is_owner)
    def _():
        gathered_at_owner(r.rs, S, 2)
        gathered_at_owner(r.rss, S, 3)

        def highest(i, acc):
            return jnp.maximum(acc, r.rss[i])

        top = lax.fori_loop(1, S, highest, r.rss[0])

        def add(i, carry):
            numer, total = carry
            theirs = r.rss[i]
            weight = jnp.exp(theirs - top)
            return (
                numer + expand(weight) * r.rs[i].astype(F32),
                total + weight * pltpu.roll(theirs, 120, 1),
            )

        numer, total = lax.fori_loop(0, S, add, (jnp.zeros((GROUP, W), F32), jnp.zeros((GROUP, 128), F32)))
        used = lanes < LH
        total = jnp.where(used, total, 1.0)
        out = numer / expand(total)
        r.own_out[...] = out
        rows = aligned(group * GROUP, GROUP)
        r.ag2[h, rows, :] = out.astype(BF16)
        r.aglse[rows, :] = jnp.where(used, top + jnp.log(total), 0.0)
        spread(r.ag2.at[h], 1, 2, r.rs)
        spread(r.aglse, 2, 1, r.rss)

    for name in ["win", "g2", "b2"]:
        loads[name].wait()
    arrive("wo")
    for x in range(2):
        spread_arrive(r.ag2.at[x], 1, x)

    for x in range(2):
        for p in range(pairs):
            r.gat[x, :, pair(p)] = mm(r.oh[x, :, pair_rows(p)], unfold(r.ag2[x, :, pair(p)])).astype(BF16)

    def second_norm(i):
        rows = aligned(i * 128, 128)
        attn = mm(r.gat[0, rows, :], r.v_wo[0]) + mm(r.gat[1, rows, :], r.v_wo[1])
        resid = r.v_tok[rows, :].astype(F32) + attn
        r.resid[rows, :] = resid
        scaled, _ = normalize(resid)
        r.n2[0, rows, :] = (scaled * r.v_g2[...] + r.v_b2[...]).astype(BF16)

    loop(T // 128, second_norm)
    send("n2", r.n2.at[0], r.n2.at[1], sib_dev)
    send("gat", r.gat.at[h], r.gat_sib, sib_dev)

    def feed_forward(base):
        rows = aligned(base, half)

        def tile(j):
            cols = aligned(j * 256, 256)
            up = mm(r.n2[0, rows, :], r.v_win[:, cols])
            share = 0.5 + 0.5 * lax.erf(up * (0.5**0.5))
            density = jnp.exp(up * up * -0.5) * 0.3989422804014327
            r.act[rows, cols] = (up * share).astype(BF16)
            r.dup[rows, cols] = (r.dact[rows, cols] * (share + up * density)).astype(BF16)

        loop(F // 256, tile)

    def d_normed2(base, out):
        rows = aligned(base, half)

        def tile(j):
            cols = aligned(j * 256, 256)
            out[:, cols] = mm_nt(r.dup[rows, :], r.v_win[cols, :]).astype(out.dtype)

        loop(D // 256, tile)

    feed_forward(oh * half)
    d_normed2(oh * half, r.dn_send)
    send("dn", r.dn_send, r.dn_recv, x_dev)
    feed_forward(h * half)
    sib_units = pl.ds(pl.multiple_of((1 - core) * (F // 2), 128), F // 2)
    own_units = pl.ds(pl.multiple_of(core * (F // 2), 128), F // 2)
    send("act", r.act.at[:, sib_units], r.act_sib, sib_dev)
    send("dup", r.dup.at[:, sib_units], r.dup_sib, sib_dev)
    d_normed2(h * half, r.dn_own)

    z_count = n // 2
    z, y = lax.div(chip, 2), lax.rem(chip, 2)
    position = jnp.where(y == 0, z, n - 1 - z)

    def device_at(p):
        p = lax.rem(p + n, n)
        return (2 * jnp.where(p < z_count, 2 * p, 2 * (n - 1 - p) + 1) + core, h)

    streams = []
    chunk = (D // 2) // n

    def add_stream(part, row_base, fin_block):
        i = len(streams)
        forward = i % 2 == 0
        streams.append(
            SimpleNamespace(
                i=i,
                part=part,
                base=row_base,
                fin=fin_block,
                recv=(r.ring_wide.at[i] if i < 4 else r.ring_slim.at[i - 4]) if ring else None,
                p=position if forward else n - 1 - position,
                to=device_at(position + 1) if forward else device_at(position - 1),
                step=0,
                sent=[],
            )
        )
        return streams[-1]

    def part_chunk(st, k):
        k = lax.rem(k + 2 * n, n)
        return st.part.at[pl.ds(pl.multiple_of(st.base + k * chunk, 16), chunk)]

    def fin_chunk(st, k):
        k = lax.rem(k + 2 * n, n)
        return st.fin(k * chunk, chunk)

    def ring_copy(st, t):
        if t == 0:
            src, dst = part_chunk(st, st.p), st.recv.at[0]
        elif t < n - 1:
            src, dst = st.recv.at[t - 1], st.recv.at[t]
        else:
            src = dst = fin_chunk(st, st.p + 1 - (t - (n - 1)))
        return remote(src, dst, r.ring_send.at[st.i, t], r.ring_recv.at[st.i, t], st.to)

    def advance(st):
        if not ring or st.step > 2 * (n - 1):
            return
        t = st.step
        st.step += 1
        if t > 0:
            came = t - 1
            if came < n - 1:
                copy = ring_copy(st, came)
                copy.wait_recv()
                mine = part_chunk(st, st.p - 1 - came)
                summed = (st.recv[came].astype(F32) + mine[...].astype(F32)).astype(BF16)
                if came < n - 2:
                    st.recv[came] = summed
                else:
                    fin_chunk(st, st.p + 1)[...] = summed
            else:
                block = fin_chunk(st, st.p - (came - (n - 1)))
                remote(block, block, r.ring_send.at[st.i, came], r.ring_recv.at[st.i, came], st.to).wait_recv()
        if t < 2 * (n - 1):
            copy = ring_copy(st, t)
            copy.start()
            st.sent.append(copy)
            at_end.append(copy.wait_send)
        else:
            whole = st.fin(0, D // 2)
            send(f"ring{st.i}", whole, whole, sib_dev)

    def turn(count=1):
        for _ in range(count):
            for st in list(streams):
                advance(st)

    def keep_part(st):
        if not ring:
            st.fin(0, D // 2)[...] = st.part[pl.ds(st.base, D // 2), :]

    if not ring:
        for name in ["fin_out", "fin_in", "fin_k", "fin_v", "fin_q", "fin_o"]:
            ref = getattr(r, name)
            ref[...] = jnp.zeros_like(ref)

    arrive("act")
    arrive("cot")

    def grad_out(j):
        cols = pl.ds(pl.multiple_of(core * (F // 2) + j * 256, 128), 256)
        tile = mm_tn(r.act[:, cols], r.v_cot[0]) + mm_tn(r.act_sib[:, aligned(j * 256, 256)], r.v_cot[1])
        r.part_out[aligned(j * 256, 256), :] = tile.astype(BF16)

    loop(F // 2 // 256, grad_out)

    def rows_of(ref, base, cols=None):
        def block(at, size):
            rows = pl.ds(pl.multiple_of(base + at, 16), size)
            return ref.at[rows] if cols is None else ref.at[rows, cols]

        return block

    for k in range(2):
        st = add_stream(r.part_out, k * (D // 2), rows_of(r.fin_out, core * (F // 2) + k * (D // 2)))
        keep_part(st)
        advance(st)
    arrive("dup")
    arrive("n2")

    def grad_in(j):
        cols = aligned(j * 256, 256)
        tile = mm_tn(r.n2[0, :, cols], r.dup[:, own_units]) + mm_tn(r.n2[1, :, cols], r.dup_sib[...])
        r.part_in[cols, :] = tile.astype(BF16)

    loop(D // 256, grad_in)
    for k in range(2):
        st = add_stream(r.part_in, k * (D // 2), rows_of(r.fin_in, k * (D // 2), own_units))
        keep_part(st)
        advance(st)

    arrive("dn")

    def second_norm_back(i, carry):
        gain_sum, shift_sum = carry
        rows = pl.ds(pl.multiple_of(h * half + i * 64, 64), 64)
        at = aligned(i * 64, 64)
        scaled, inverse = normalize(r.resid[rows, :])
        grad = r.dn_own[at, :] + r.dn_recv[at, :].astype(F32)
        d_resid = r.v_cot[0, rows, :].astype(F32) + normalize_back(grad, r.v_g2[...], scaled, inverse)
        r.dres[at, :] = d_resid
        r.dat[rows, :] = d_resid.astype(BF16)
        return gain_sum + fold_rows(grad * scaled), shift_sum + fold_rows(grad)

    zero = jnp.zeros((8, D), F32)
    gain_sum, shift_sum = lax.fori_loop(0, half // 64, second_norm_back, (zero, zero))
    r.norm_grads[2:3, :] = jnp.sum(gain_sum, axis=0, keepdims=True)
    r.norm_grads[3:4, :] = jnp.sum(shift_sum, axis=0, keepdims=True)
    own_rows = aligned(h * half, half)
    other_rows = aligned(oh * half, half)
    send("dat", r.dat.at[own_rows], r.dat.at[own_rows], x_dev)
    for x in range(2):
        d_gathered = mm_nt(r.dat[own_rows, :], r.v_wo[x]).astype(BF16)
        for p in range(pairs):
            hot = r.oht[x, pair_rows(p), own_rows]
            r.dc[x, :, pair(p)] = fold(mm(hot, d_gathered[:, pair(p)]))[:SENT].astype(BF16)
    for x in range(2):
        scatter(r.dc.at[x], r.rs, me, x)

    turn(1)

    def ffn_part(j):
        cols = aligned(j * 256, 256)
        r.fp[h, :, cols] = mm(r.act[...], r.v_wout[:, cols]).astype(BF16)

    loop(D // 256, ffn_part)
    send("fp", r.fp.at[h], r.fp.at[h], x_dev)
    turn(1)

    @pl.when(is_owner)
    def _():
        gathered_at_owner(r.rs, 2 * S, 4)
        rows = aligned(group * GROUP, GROUP)
        d_cluster = total_of(r.rs, 2 * S).astype(BF16)
        r.ag3[rows, :] = d_cluster
        spread(r.ag3, 3, 1, r.rs)
        product = d_cluster.astype(F32) * r.own_out[...]
        delta = jnp.zeros((GROUP, 128), F32)
        for p in range(pairs):
            block = product[:, pair(p)]
            delta = delta + jnp.where(
                lanes == 2 * p, jnp.sum(jnp.where(left, block, 0.0), axis=1, keepdims=True), 0.0
            )
            delta = delta + jnp.where(
                lanes == 2 * p + 1, jnp.sum(jnp.where(left, 0.0, block), axis=1, keepdims=True), 0.0
            )
        r.agdelta[rows, :] = delta
        spread(r.agdelta, 4, 1, r.rss)

    turn(1)
    arrive("dat")
    send("dat_sib", r.dat.at[:, sib_half], r.dat_sib, sib_dev)
    arrive("gat")
    spread_arrive(r.aglse, 2)
    spread_arrive(r.ag3, 3)
    spread_arrive(r.agdelta, 4)

    for p in range(pairs):
        d_probs = mm_nt(unfold(r.ag3[:, pair(p)]), r.v[:, pair(p)])
        factor = jnp.exp(column(r.stats[...], p) - column(r.aglse[...], p))
        probs = r.e[pair_rows(p), :] * factor
        r.pb[pair_rows(p), :] = probs.astype(BF16)
        d_scores = (probs * (d_probs - column(r.agdelta[...], p))).astype(BF16)
        r.dsb[pair_rows(p), :] = d_scores
        r.dcen[:, pair(p)] = fold(mm(d_scores, r.k[:, pair(p)]))[:SENT].astype(BF16)
    scatter(r.dcen, r.rs, s, h)

    turn(1)
    for p in range(pairs):
        r.dkv[0, :, pair(p)] = (mm_tn(r.dsb[pair_rows(p), :], unfold(r.ag1[:, pair(p)])) * scale).astype(BF16)
        r.dkv[1, :, pair(p)] = mm_tn(r.pb[pair_rows(p), :], unfold(r.ag3[:, pair(p)])).astype(BF16)
    send("dkv", r.dkv, r.dkv_sib, sib_dev)
    turn(1)

    @pl.when(is_owner)
    def _():
        gathered_at_owner(r.rs, S, 5)
        rows = aligned(group * GROUP, GROUP)
        r.ag4[h, rows, :] = (total_of(r.rs, S) * scale / r.divisor[...]).astype(BF16)
        spread(r.ag4.at[h], 5, 2, r.rs)

    def kv_part(rows):
        return mm_nt(r.dkv[0, rows, :], r.v_wk[...]) + mm_nt(r.dkv[1, rows, :], r.v_wv[...])

    r.kv_send[...] = kv_part(other_rows).astype(BF16)
    send("kv", r.kv_send, r.kv_recv, x_dev)
    turn(1)
    arrive("dkv")
    arrive("nrm")
    for i in range(2):
        tile = mm_tn(r.nrm[:, own_half], r.dkv[i]) + mm_tn(r.nrm_sib[...], r.dkv_sib[i])
        r.part_small[i] = tile.astype(BF16)
    for i, name in enumerate(["fin_k", "fin_v"]):
        st = add_stream(r.part_small.at[i], 0, rows_of(getattr(r, name), core * W))
        keep_part(st)
        advance(st)
    r.kv_own[...] = kv_part(own_rows)
    turn(1)
    arrive("dat_sib")
    tile = mm_tn(r.gat[h], r.dat[:, own_half]) + mm_tn(r.gat_sib[...], r.dat_sib[...])
    r.part_small[2] = tile.astype(BF16)
    st = add_stream(r.part_small.at[2], 0, rows_of(r.fin_o, 0, own_half))
    keep_part(st)
    advance(st)
    turn(1)

    for x in range(2):
        spread_arrive(r.ag4.at[x], 5, x)
    for p in range(pairs):
        r.dq[:, pair(p)] = mm(r.oh[h, :, pair_rows(p)], unfold(r.ag4[h, :, pair(p)])).astype(BF16)
    send("dq", r.dq, r.dq_sib, sib_dev)
    for p in range(pairs):
        r.dq_other[:, pair(p)] = mm(r.oh[oh, own_rows, pair_rows(p)], unfold(r.ag4[oh, :, pair(p)])).astype(BF16)
    turn(1)
    arrive("dq")
    r.part_small[3] = (mm_tn(r.nrm[:, own_half], r.dq[...]) + mm_tn(r.nrm_sib[...], r.dq_sib[...])).astype(BF16)
    st = add_stream(r.part_small.at[3], 0, rows_of(r.fin_q, core * W))
    keep_part(st)
    advance(st)
    turn(1)

    arrive("kv")
    arrive("wq")

    def first_norm_back(i, carry):
        gain_sum, shift_sum = carry
        rows = pl.ds(pl.multiple_of(h * half + i * 64, 64), 64)
        at = aligned(i * 64, 64)
        scaled, inverse = normalize(r.v_tok[rows, :].astype(F32))
        grad = r.kv_own[at, :] + r.kv_recv[at, :].astype(F32)
        grad = grad + mm_nt(r.dq[rows, :], r.v_wq[h]) + mm_nt(r.dq_other[at, :], r.v_wq[oh])
        grad_tokens = r.dres[at, :] + normalize_back(grad, r.v_g1[...], scaled, inverse)
        r.gtok[rows, :] = grad_tokens.astype(BF16)
        return gain_sum + fold_rows(grad * scaled), shift_sum + fold_rows(grad)

    gain_sum, shift_sum = lax.fori_loop(0, half // 64, first_norm_back, (zero, zero))
    r.norm_grads[0:1, :] = jnp.sum(gain_sum, axis=0, keepdims=True)
    r.norm_grads[1:2, :] = jnp.sum(shift_sum, axis=0, keepdims=True)
    send("norm", r.norm_grads, r.norm_recv, x_dev)
    send("gtok", r.gtok.at[own_rows], r.gtok.at[own_rows], x_dev)
    turn(1)
    arrive("norm")
    r.norm_pair[...] = r.norm_grads[...] + r.norm_recv[...]

    blocks = D // 128

    def norm_to(g):
        cols = pl.ds(g * 128, 128)
        mine = s == first + g
        copy = remote(r.norm_pair.at[:, cols], r.norm_rs.at[s], r.norm_send.at[g], r.norm_sem.at[0], (first + g, h))
        return cols, mine, copy

    for g in range(blocks):
        cols, mine, copy = norm_to(g)

        @pl.when(jnp.logical_not(mine))
        def _():
            copy.start()

        @pl.when(mine)
        def _():
            r.norm_rs[s] = r.norm_pair[:, cols]

    turn(1)
    arrive("fp")

    def block_out(i):
        rows = aligned(i * 64, 64)
        r.bout[rows, :] = (r.resid[rows, :] + r.fp[0, rows, :].astype(F32) + r.fp[1, rows, :].astype(F32)).astype(BF16)

    loop(T // 64, block_out)
    turn(1)
    norm_owner = jnp.logical_and(s >= first, s < first + blocks)

    @pl.when(norm_owner)
    def _():
        block = r.norm_rs.at[pl.ds(0, S - 1)]
        remote(block, block, r.norm_send.at[0], r.norm_sem.at[0], x_dev).wait_recv()

        def add(i, acc):
            return acc + r.norm_rs[i]

        cols = aligned(group * 128, 128)
        r.norm_fin[:, cols] = lax.fori_loop(0, S, add, jnp.zeros((8, 128), F32))
        block = r.norm_fin.at[:, cols]

        def to(k):
            remote(block, block, r.norm_send.at[blocks], r.norm_sem.at[1 + group], (lax.rem(s + k + 1, S), h)).start()

        loop(S - 1, to)

    turn(1)
    for g in range(blocks):
        block = r.norm_fin.at[:, pl.ds(g * 128, 128)]

        @pl.when(s != first + g)
        def _():
            remote(block, block, r.norm_send.at[0], r.norm_sem.at[1 + g], x_dev).wait_recv()

    arrive("gtok")
    if ring:
        while any(st.step <= 2 * (n - 1) for st in streams):
            turn(1)
        for st in streams:
            arrive(f"ring{st.i}")

    outs = [
        ("bout", "o_block"),
        ("gtok", "o_tokens"),
        ("norm_fin", "o_norm"),
        ("fin_q", "o_q"),
        ("fin_k", "o_k"),
        ("fin_v", "o_v"),
        ("fin_o", "o_o"),
        ("fin_in", "o_in"),
        ("fin_out", "o_out"),
    ]
    stores = [
        pltpu.make_async_copy(getattr(r, a), getattr(r, b), r.store_sem.at[i]) for i, (a, b) in enumerate(outs)
    ]
    for store in stores:
        store.start()
    for finish in at_end:
        finish()
    for g in range(blocks):
        cols, mine, copy = norm_to(g)

        @pl.when(jnp.logical_not(mine))
        def _():
            copy.wait_send()

    @pl.when(norm_owner)
    def _():
        block = r.norm_rs.at[pl.ds(0, S - 1)]
        remote(block, block, r.norm_send.at[blocks], r.norm_sem.at[0], x_dev).wait_send()

    for store in stores:
        store.wait()


def per_device(
    S,
    tokens,
    norm1_gain,
    norm1_shift,
    w_query,
    w_key,
    w_value,
    w_output,
    norm2_gain,
    norm2_shift,
    w_in,
    w_out,
    cluster_ids,
    masked_keys,
    cotangent,
):
    T, D = tokens.shape
    LH = cluster_ids.shape[1]
    W = w_query.shape[1]
    F = w_in.shape[1]
    n = S // 2
    ring = n <= 8
    cfg = SimpleNamespace(S=S, T=T, D=D, W=W, LH=LH, F=F, ring=ring, scatter_of=[0, 1, 2, 3, 4, 4, 5])

    positions = lax.axis_index("seq") * T + lax.iota(jnp.int32, T)
    hits = jnp.any(positions[:, None] == masked_keys[None, :], axis=1)
    keep = jnp.where(hits, 0.0, 1.0).astype(F32)[None, :]
    ids = jnp.pad(cluster_ids.T, ((0, 8 - LH), (0, 0)), constant_values=-1)

    inputs = dict(
        tok=tokens,
        g1=norm1_gain[None],
        b1=norm1_shift[None],
        wq=w_query,
        wk=w_key,
        wv=w_value,
        wo=w_output,
        g2=norm2_gain[None],
        b2=norm2_shift[None],
        win=w_in,
        wout=w_out,
        ids=ids,
        keep=keep,
        cot=cotangent,
    )
    outputs = dict(
        o_block=((T, D), BF16),
        o_tokens=((T, D), BF16),
        o_norm=((8, D), F32),
        o_q=((D, W), BF16),
        o_k=((D, W), BF16),
        o_v=((D, W), BF16),
        o_o=((W, D), BF16),
        o_in=((D, F), BF16),
        o_out=((F, D), BF16),
    )
    half = T // 2
    vmem = dict(
        v_tok=((T, D), BF16),
        v_g1=((1, D), F32),
        v_b1=((1, D), F32),
        v_wq=((2, D, W), BF16),
        v_wk=((D, W), BF16),
        v_wv=((D, W), BF16),
        v_wo=((2, W, D), BF16),
        v_g2=((1, D), F32),
        v_b2=((1, D), F32),
        v_win=((D, F), BF16),
        v_wout=((F, D), BF16),
        v_ids=((2, 8, T), jnp.int32),
        v_keep=((1, T), F32),
        v_cot=((2, T, D), BF16),
        nrm=((T, D), BF16),
        nrm_sib=((T, W), BF16),
        q=((T, W), BF16),
        k=((T, W), BF16),
        v=((T, W), BF16),
        oht=((2, LH * SLOT, T), BF16),
        oh=((2, T, LH * SLOT), BF16),
        sums=((SENT, W), BF16),
        counts=((SENT, 128), F32),
        rs=((2 * S, GROUP, W), BF16),
        rss=((S, GROUP, 128), F32),
        divisor=((GROUP, W), F32),
        ag1=((SLOT, W), BF16),
        dact=((T, F), F32),
        e=((LH * SLOT, T), F32),
        numer=((SENT, W), BF16),
        stats=((SLOT, 128), F32),
        own_out=((GROUP, W), F32),
        ag2=((2, SLOT, W), BF16),
        aglse=((SLOT, 128), F32),
        gat=((2, T, W), BF16),
        gat_sib=((T, W), BF16),
        resid=((T, D), F32),
        n2=((2, T, D), BF16),
        act=((T, F), BF16),
        dup=((T, F), BF16),
        act_sib=((T, F // 2), BF16),
        dup_sib=((T, F // 2), BF16),
        dn_send=((half, D), BF16),
        dn_recv=((half, D), BF16),
        dn_own=((half, D), F32),
        dres=((half, D), F32),
        dat=((T, D), BF16),
        dat_sib=((T, W), BF16),
        dc=((2, SENT, W), BF16),
        ag3=((SLOT, W), BF16),
        agdelta=((SLOT, 128), F32),
        pb=((LH * SLOT, T), BF16),
        dsb=((LH * SLOT, T), BF16),
        dcen=((SENT, W), BF16),
        ag4=((2, SLOT, W), BF16),
        dkv=((2, T, W), BF16),
        dkv_sib=((2, T, W), BF16),
        kv_send=((half, D), BF16),
        kv_recv=((half, D), BF16),
        kv_own=((half, D), F32),
        dq=((T, W), BF16),
        dq_sib=((T, W), BF16),
        dq_other=((half, W), BF16),
        gtok=((T, D), BF16),
        norm_grads=((8, D), F32),
        norm_recv=((8, D), F32),
        norm_pair=((8, D), F32),
        norm_rs=((S, 8, 128), F32),
        norm_fin=((8, D), F32),
        fp=((2, T, D), BF16),
        bout=((T, D), BF16),
        part_out=((F // 2, D), BF16),
        part_in=((D, F // 2), BF16),
        part_small=((4, W, W), BF16),
        fin_out=((F, D), BF16),
        fin_in=((D, F), BF16),
        fin_k=((D, W), BF16),
        fin_v=((D, W), BF16),
        fin_q=((D, W), BF16),
        fin_o=((W, D), BF16),
    )
    steps = 2 * (n - 1) if ring else 1
    if ring:
        chunk = (D // 2) // n
        vmem["ring_wide"] = ((4, n - 1, chunk, D), BF16)
        vmem["ring_slim"] = ((4, n - 1, chunk, W), BF16)
    sems = dict(
        load_sem=(14,),
        store_sem=(9,),
        ex_send=(32,),
        ex_recv=(32,),
        sc_send=(7, GROUPS),
        sc_recv=(6,),
        sp_send=(6,),
        sp_recv=(6, 2, GROUPS),
        ring_send=(STREAMS, steps),
        ring_recv=(STREAMS, steps),
        norm_send=(D // 128 + 1,),
        norm_sem=(D // 128 + 1,),
    )
    names = list(inputs) + list(outputs) + list(vmem) + list(sems)
    results = pl.pallas_call(
        functools.partial(kernel, cfg, names),
        out_shape=[jax.ShapeDtypeStruct(*o) for o in outputs.values()],
        in_specs=[pl.BlockSpec(memory_space=pl.ANY)] * len(inputs),
        out_specs=[pl.BlockSpec(memory_space=pl.ANY)] * len(outputs),
        scratch_shapes=[pltpu.VMEM(*b) for b in vmem.values()] + [pltpu.SemaphoreType.DMA(b) for b in sems.values()],
        compiler_params=pltpu.CompilerParams(collective_id=0, has_side_effects=True, vmem_limit_bytes=cfg_vmem()),
        name="block",
    )(*inputs.values())
    block, grad_tokens, norms, *grads = results
    grads = [g.astype(F32) for g in grads]
    if not ring:
        grads = lax.psum(grads, "seq")
    grad_q, grad_k, grad_v, grad_o, grad_in, grad_out = grads
    return (
        block,
        grad_tokens.astype(F32),
        norms[0],
        norms[1],
        grad_q,
        grad_k,
        grad_v,
        grad_o,
        norms[2],
        norms[3],
        grad_in,
        grad_out,
    )


def cfg_vmem():
    return 62 * 2**20


def solution(mesh):
    columns, rows = P(None, "head"), P("head", None)
    by_token = P("seq", None)
    return jax.shard_map(
        functools.partial(per_device, mesh.shape["seq"]),
        mesh=mesh,
        in_specs=(by_token, P(), P(), columns, columns, columns, rows, P(), P(), columns, rows, P("seq", "head"), P(), by_token),
        out_specs=(by_token, by_token, P(), P(), columns, columns, columns, rows, P(), P(), columns, rows),
        check_vma=False,
    )
```

```python
import functools
from types import SimpleNamespace

import jax
import jax.numpy as jnp
from jax import lax
from jax.experimental import pallas as pl
from jax.experimental.pallas import tpu as pltpu
from jax.sharding import PartitionSpec as P

CLUSTERS = 100
EPSILON = 1e-05
MESH = pl.DeviceIdType.MESH
F32 = jnp.float32
BF16 = jnp.bfloat16
SLOT = 128
GROUP = 16
GROUPS = -(-CLUSTERS // GROUP)
SENT = GROUPS * GROUP
STREAMS = 6


def mm(a, b):
    return lax.dot_general(a, b, (((1,), (0,)), ((), ())), preferred_element_type=F32)


def mm_nt(a, b):
    return lax.dot_general(a, b, (((1,), (1,)), ((), ())), preferred_element_type=F32)


def mm_tn(a, b):
    return lax.dot_general(a, b, (((0,), (0,)), ((), ())), preferred_element_type=F32)


def aligned(index, size):
    return pl.ds(pl.multiple_of(index, size), size)


def remote(src, dst, send_sem, recv_sem, device):
    return pltpu.make_async_remote_copy(
        src_ref=src, dst_ref=dst, send_sem=send_sem, recv_sem=recv_sem, device_id=device, device_id_type=MESH
    )


def loop(count, body):
    def step(i, carry):
        body(i)
        return carry

    lax.fori_loop(0, count, step, 0)


def normalize(values):
    centred = values - jnp.mean(values, axis=-1, keepdims=True)
    inverse = lax.rsqrt(jnp.mean(centred * centred, axis=-1, keepdims=True) + EPSILON)
    return centred * inverse, inverse


def normalize_back(grad, gain, scaled, inverse):
    inner = grad * gain
    return inverse * (
        inner - jnp.mean(inner, axis=-1, keepdims=True) - scaled * jnp.mean(inner * scaled, axis=-1, keepdims=True)
    )


def fold_rows(values):
    return jnp.sum(values.reshape(values.shape[0] // 8, 8, values.shape[1]), axis=0)


def kernel(cfg, names, *all_refs):
    r = SimpleNamespace(**dict(zip(names, all_refs)))
    S, T, D, W, LH, F = cfg.S, cfg.T, cfg.D, cfg.W, cfg.LH, cfg.F
    pairs = LH // 2
    half = T // 2
    scale = (W // LH) ** (-0.5)
    ring = cfg.ring
    n = S // 2
    s = lax.axis_index("seq")
    h = lax.axis_index("head")
    oh = 1 - h
    core = lax.rem(s, 2)
    chip = lax.div(s, 2)
    me = s * 2 + h
    x_dev = (s, oh)
    sib_dev = (s + 1 - 2 * core, h)
    first = S // 4
    is_owner = jnp.logical_and(s >= first, s < first + GROUPS)
    group = s - first
    lanes = lax.broadcasted_iota(jnp.int32, (1, 128), 1)
    left = lanes < 64

    def fold(block):
        return jnp.where(left, block[:SLOT], block[SLOT:])

    def unfold(block):
        zero = jnp.zeros_like(block)
        return jnp.concatenate([jnp.where(left, block, zero), jnp.where(left, zero, block)], axis=0)

    def expand(stats):
        return jnp.concatenate(
            [jnp.where(left, stats[:, 2 * p : 2 * p + 1], stats[:, 2 * p + 1 : 2 * p + 2]) for p in range(pairs)], axis=1
        )

    def column(stats, p, at=0):
        return jnp.concatenate(
            [stats[:, at + 2 * p : at + 2 * p + 1], stats[:, at + 2 * p + 1 : at + 2 * p + 2]], axis=0
        )

    def place(columns, p, at=0):
        rows = columns.shape[0] // 2
        return jnp.where(lanes == at + 2 * p, columns[:rows], 0.0) + jnp.where(
            lanes == at + 2 * p + 1, columns[rows:], 0.0
        )

    def pair(p):
        return slice(p * 128, (p + 1) * 128)

    def pair_rows(p):
        return slice(p * 2 * SLOT, (p + 1) * 2 * SLOT)

    at_end = []

    loads = {}
    for i, name in enumerate(
        ["ids", "tok", "g1", "b1", "wq", "wo", "wk", "wv", "cot", "wout", "masked", "win", "g2", "b2"]
    ):
        dst = getattr(r, "v_" + name)
        dst = {"cot": lambda d: d.at[0], "wq": lambda d: d.at[h], "wo": lambda d: d.at[h], "ids": lambda d: d.at[h]}.get(
            name, lambda d: d
        )(dst)
        loads[name] = pltpu.make_async_copy(getattr(r, name), dst, r.load_sem.at[i])

    barrier = pltpu.get_barrier_semaphore()

    def greet(k):
        other = lax.rem(me + k + 1, 2 * S)
        pl.semaphore_signal(
            barrier, inc=1, device_id=(lax.div(other, 2), lax.rem(other, 2)), device_id_type=MESH
        )

    loop(2 * S - 1, greet)
    for load in loads.values():
        load.start()

    exchanges = {}

    def send(name, src, dst, device):
        i = len(exchanges)
        copy = remote(src, dst, r.ex_send.at[i], r.ex_recv.at[i], device)
        copy.start()
        exchanges[name] = copy
        at_end.append(copy.wait_send)

    def arrive(name):
        exchanges[name].wait_recv()

    counters = {"scatter": 0, "spread": 0}

    def scatter(src, dst, slot, plane):
        i = counters["scatter"]
        counters["scatter"] += 1

        def at(g):
            rows = pl.ds(g * GROUP, GROUP)
            mine = jnp.logical_and(s == first + g, h == plane)
            copy = remote(src.at[rows], dst.at[slot], r.sc_send.at[i, g], r.sc_recv.at[cfg.scatter_of[i]], (first + g, plane))
            return rows, mine, copy

        for g in range(GROUPS):
            rows, mine, copy = at(g)

            @pl.when(jnp.logical_not(mine))
            def _():
                copy.start()

            @pl.when(mine)
            def _():
                dst[slot] = src[rows, :]

        def finish():
            for g in range(GROUPS):
                rows, mine, copy = at(g)

                @pl.when(jnp.logical_not(mine))
                def _():
                    copy.wait_send()

        at_end.append(finish)

    def gathered_at_owner(buf, count, i):
        block = buf.at[pl.ds(0, count - 1)]
        remote(block, block, r.sc_send.at[0, 0], r.sc_recv.at[i], x_dev).wait_recv()

    def spread(buf, i, planes, like):
        rows = aligned(group * GROUP, GROUP)
        block = buf.at[rows]

        def to(k):
            copy = remote(block, block, r.sp_send.at[i], r.sp_recv.at[i, h, group], (lax.rem(s + k + 1, S), h))
            copy.start()

        def across(k):
            copy = remote(block, block, r.sp_send.at[i], r.sp_recv.at[i, h, group], (lax.rem(s + k, S), oh))
            copy.start()

        loop(S - 1, to)
        if planes == 2:
            loop(S, across)

        def finish():
            @pl.when(is_owner)
            def _():
                block = like.at[pl.ds(0, S * planes - 1)]
                remote(block, block, r.sp_send.at[i], r.sp_recv.at[i, 0, 0], x_dev).wait_send()

        at_end.append(finish)

    def spread_arrive(buf, i, from_plane=None):
        for g in range(GROUPS):
            mine = s == first + g
            plane = h
            if from_plane is not None:
                mine = jnp.logical_and(mine, h == from_plane)
                plane = from_plane

            @pl.when(jnp.logical_not(mine))
            def _():
                block = buf.at[pl.ds(g * GROUP, GROUP)]
                remote(block, block, r.sp_send.at[i], r.sp_recv.at[i, plane, g], x_dev).wait_recv()

    def total_of(buf, count):
        def add(i, acc):
            return acc + buf[i].astype(F32)

        return lax.fori_loop(0, count, add, jnp.zeros((GROUP, buf.shape[-1]), F32))

    r.ag1[...] = jnp.zeros_like(r.ag1)
    r.ag3[...] = jnp.zeros_like(r.ag3)
    r.ag2[...] = jnp.zeros_like(r.ag2)
    r.ag4[...] = jnp.zeros_like(r.ag4)
    r.aglse[...] = jnp.zeros_like(r.aglse)
    r.agdelta[...] = jnp.zeros_like(r.agdelta)
    r.norm_grads[...] = jnp.zeros_like(r.norm_grads)

    def onehot(x):
        ids = r.v_ids[x]
        rows = lax.broadcasted_iota(jnp.int32, (SLOT, T), 0)
        for j in range(LH):
            r.oht[x, j * SLOT : (j + 1) * SLOT, :] = jnp.where(rows == ids[j : j + 1, :], 1.0, 0.0).astype(BF16)
        for p in range(pairs):
            r.oh[x, :, pair_rows(p)] = r.oht[x, pair_rows(p), :].T

    def gain(ref):
        return ref[...].reshape(1, D)

    loads["ids"].wait()
    onehot(h)
    for name in ["g1", "b1", "tok"]:
        loads[name].wait()

    def first_norm(i):
        rows = aligned(i * 64, 64)
        scaled, _ = normalize(r.v_tok[rows, :].astype(F32))
        r.nrm[rows, :] = (scaled * gain(r.v_g1) + gain(r.v_b1)).astype(BF16)

    loop(T // 64, first_norm)
    loads["wq"].wait()

    def project(weight, out):
        def tile(i):
            rows = aligned(i * 256, 256)
            out[rows, :] = mm(r.nrm[rows, :], weight).astype(BF16)

        loop(T // 256, tile)

    project(r.v_wq[h], r.q)
    counts = jnp.zeros((SLOT, 128), F32)
    ones = jnp.ones((T, 128), BF16)
    for p in range(pairs):
        hot = r.oht[h, pair_rows(p), :]
        r.sums[:, pair(p)] = fold(mm(hot, r.q[:, pair(p)]))[:SENT].astype(BF16)
        counts = counts + place(mm(hot, ones)[:, :1], p)
    r.counts[...] = counts[:SENT]

    pl.semaphore_wait(barrier, 2 * S - 1)
    scatter(r.sums, r.rs, s, h)
    scatter(r.counts, r.rss, s, h)
    send("ids", r.v_ids.at[h], r.v_ids.at[h], x_dev)
    loads["wo"].wait()
    wo_mine, wo_sib = pl.ds(pl.multiple_of(core * (W // 2), 16), W // 2), pl.ds(pl.multiple_of((1 - core) * (W // 2), 16), W // 2)
    send("wo", r.v_wo.at[h, wo_mine], r.v_wo.at[h, wo_mine], x_dev)
    sib_half = pl.ds(pl.multiple_of((1 - core) * W, 128), W)
    own_half = pl.ds(pl.multiple_of(core * W, 128), W)
    loads["cot"].wait()
    send("cot", r.v_cot.at[0], r.v_cot.at[1], sib_dev)
    send("nrm", r.nrm.at[:, sib_half], r.nrm_sib, sib_dev)

    loads["wk"].wait()
    project(r.v_wk[...], r.k)
    loads["wv"].wait()
    project(r.v_wv[...], r.v)
    loads["wout"].wait()

    def d_act(j):
        cols = aligned(j * 256, 256)
        r.dact[:, cols] = mm_nt(r.v_cot[0], r.v_wout[cols, :])

    loop(F // 256, d_act)

    @pl.when(is_owner)
    def _():
        gathered_at_owner(r.rs, S, 0)
        gathered_at_owner(r.rss, S, 1)
        divisor = jnp.maximum(expand(total_of(r.rss, S)), 1.0)
        r.divisor[...] = divisor
        r.ag1[aligned(group * GROUP, GROUP), :] = (total_of(r.rs, S) / divisor).astype(BF16)
        spread(r.ag1, 0, 1, r.rs)

    arrive("ids")
    onehot(oh)
    arrive("wo")
    send("wo_sib", r.v_wo.at[oh, wo_mine], r.v_wo.at[oh, wo_mine], sib_dev)
    loads["masked"].wait()
    positions = s * T + lax.broadcasted_iota(jnp.int32, (1, T), 1)

    def mark(i, hits):
        keys = r.v_masked[aligned(i * 8, 8), :].T
        for j in range(8):
            found = jnp.where(keys[:, j : j + 1] == positions, 1.0, 0.0)
            hits = jnp.maximum(hits, jnp.max(found.reshape(16, 8, T), axis=0))
        return hits

    hits = lax.fori_loop(0, cfg.M // 1024, mark, jnp.zeros((8, T), F32))
    keep = 1.0 - jnp.max(hits, axis=0, keepdims=True)
    spread_arrive(r.ag1, 0)

    stats = jnp.zeros((SLOT, 128), F32)
    for p in range(pairs):
        scores = mm_nt(unfold(r.ag1[:, pair(p)]), r.k[:, pair(p)]) * scale
        scores = jnp.where(keep > 0, scores, -1e30)
        top = jnp.max(scores, axis=1, keepdims=True)
        weights = jnp.exp(scores - top) * keep
        r.e[pair_rows(p), :] = weights
        total = jnp.sum(weights, axis=1, keepdims=True)
        r.numer[:, pair(p)] = fold(mm(weights.astype(BF16), r.v[:, pair(p)]))[:SENT].astype(BF16)
        stats = stats + place(top, p) + place(total, p, 8)
    r.stats[...] = stats
    scatter(r.numer, r.rs, s, h)
    scatter(r.stats.at[pl.ds(0, SENT)], r.rss, s, h)

    @pl.when(is_owner)
    def _():
        gathered_at_owner(r.rs, S, 2)
        gathered_at_owner(r.rss, S, 3)

        def highest(i, acc):
            return jnp.maximum(acc, r.rss[i])

        top = lax.fori_loop(1, S, highest, r.rss[0])

        def add(i, carry):
            numer, total = carry
            theirs = r.rss[i]
            weight = jnp.exp(theirs - top)
            return (
                numer + expand(weight) * r.rs[i].astype(F32),
                total + weight * pltpu.roll(theirs, 120, 1),
            )

        numer, total = lax.fori_loop(0, S, add, (jnp.zeros((GROUP, W), F32), jnp.zeros((GROUP, 128), F32)))
        used = lanes < LH
        total = jnp.where(used, total, 1.0)
        out = numer / expand(total)
        r.own_out[...] = out
        rows = aligned(group * GROUP, GROUP)
        r.ag2[h, rows, :] = out.astype(BF16)
        r.aglse[rows, :] = jnp.where(used, top + jnp.log(total), 0.0)
        spread(r.ag2.at[h], 1, 2, r.rs)
        spread(r.aglse, 2, 1, r.rss)

    for name in ["win", "g2", "b2"]:
        loads[name].wait()
    arrive("wo_sib")
    for x in range(2):
        spread_arrive(r.ag2.at[x], 1, x)

    for x in range(2):
        for p in range(pairs):
            r.gat[x, :, pair(p)] = mm(r.oh[x, :, pair_rows(p)], unfold(r.ag2[x, :, pair(p)])).astype(BF16)

    def second_norm(i):
        rows = aligned(i * 128, 128)
        attn = mm(r.gat[0, rows, :], r.v_wo[0]) + mm(r.gat[1, rows, :], r.v_wo[1])
        resid = r.v_tok[rows, :].astype(F32) + attn
        r.resid[rows, :] = resid
        scaled, _ = normalize(resid)
        r.n2[0, rows, :] = (scaled * gain(r.v_g2) + gain(r.v_b2)).astype(BF16)

    loop(T // 128, second_norm)
    send("n2", r.n2.at[0], r.n2.at[1], sib_dev)
    send("gat", r.gat.at[h], r.gat_sib, sib_dev)

    def feed_forward(base):
        rows = aligned(base, half)

        def tile(j):
            cols = aligned(j * 256, 256)
            up = mm(r.n2[0, rows, :], r.v_win[:, cols])
            share = 0.5 + 0.5 * lax.erf(up * (0.5**0.5))
            density = jnp.exp(up * up * -0.5) * 0.3989422804014327
            r.act[rows, cols] = (up * share).astype(BF16)
            r.dup[rows, cols] = (r.dact[rows, cols] * (share + up * density)).astype(BF16)

        loop(F // 256, tile)

    def d_normed2(base, out):
        rows = aligned(base, half)

        def tile(j):
            cols = aligned(j * 256, 256)
            out[:, cols] = mm_nt(r.dup[rows, :], r.v_win[cols, :]).astype(out.dtype)

        loop(D // 256, tile)

    feed_forward(oh * half)
    d_normed2(oh * half, r.dn_send)
    send("dn", r.dn_send, r.dn_recv, x_dev)
    feed_forward(h * half)
    sib_units = pl.ds(pl.multiple_of((1 - core) * (F // 2), 128), F // 2)
    own_units = pl.ds(pl.multiple_of(core * (F // 2), 128), F // 2)
    send("act", r.act.at[:, sib_units], r.act_sib, sib_dev)
    send("dup", r.dup.at[:, sib_units], r.dup_sib, sib_dev)
    d_normed2(h * half, r.dn_own)

    z_count = n // 2
    z, y = lax.div(chip, 2), lax.rem(chip, 2)
    position = jnp.where(y == 0, z, n - 1 - z)

    def device_at(p):
        p = lax.rem(p + n, n)
        return (2 * jnp.where(p < z_count, 2 * p, 2 * (n - 1 - p) + 1) + core, h)

    streams = []
    ahead, behind = n // 2, n - 1 - n // 2

    def add_stream(part, fin_block):
        i = len(streams)
        st = SimpleNamespace(i=i, part=part, fin=fin_block, turn=0)
        st.chunk = part.shape[0] // n
        st.recv = (r.ring_wide.at[i] if i < 2 else r.ring_slim.at[i - 2]) if ring else None
        st.ways = [(1, ahead, 0), (-1, behind, ahead)] if i % 2 == 0 else [(-1, ahead, 0), (1, behind, ahead)]
        if ring:
            streams.append(st)
        else:
            st.fin(0, part.shape[0])[...] = part[...]
        return st

    def part_chunk(st, k):
        return st.part.at[pl.ds(pl.multiple_of(lax.rem(k + 2 * n, n) * st.chunk, 16), st.chunk)]

    def fin_chunk(st, k):
        return st.fin(lax.rem(k + 2 * n, n) * st.chunk, st.chunk)

    def sum_copy(st, way, t):
        sign, hops, slot = way
        src = part_chunk(st, position + sign * hops) if t == 0 else st.recv.at[slot + t - 1]
        return remote(
            src,
            st.recv.at[slot + t],
            r.ring_send.at[st.i, slot + t],
            r.ring_recv.at[st.i, slot + t],
            device_at(position + sign),
        )

    def pass_copy(st, way, t):
        sign, hops, slot = way
        block = fin_chunk(st, position - sign * t)
        return remote(
            block,
            block,
            r.ring_send.at[st.i, n - 1 + slot + t],
            r.ring_recv.at[st.i, n - 1 + slot + t],
            device_at(position + sign),
        )

    def start(copy):
        copy.start()
        at_end.append(copy.wait_send)

    def advance(st):
        t = st.turn
        st.turn += 1
        if t <= ahead:
            for way in st.ways:
                sign, hops, slot = way
                if 0 < t <= hops:
                    sum_copy(st, way, t - 1).wait_recv()
                    if t < hops:
                        came = st.recv[slot + t - 1].astype(F32) + part_chunk(st, position + sign * (hops - t))[...].astype(F32)
                        st.recv[slot + t - 1] = came.astype(BF16)
                if t < hops:
                    start(sum_copy(st, way, t))
            if t == ahead:
                total = part_chunk(st, position)[...].astype(F32)
                for sign, hops, slot in st.ways:
                    total = total + st.recv[slot + hops - 1].astype(F32)
                fin_chunk(st, position)[...] = total.astype(BF16)
                for way in st.ways:
                    start(pass_copy(st, way, 0))
        elif t <= 2 * ahead:
            u = t - ahead
            for way in st.ways:
                sign, hops, slot = way
                if u <= hops:
                    block = fin_chunk(st, position - sign * u)
                    remote(
                        block, block, r.ring_send.at[st.i, 0], r.ring_recv.at[st.i, n - 1 + slot + u - 1], x_dev
                    ).wait_recv()
                if u < hops:
                    start(pass_copy(st, way, u))
            if u == ahead:
                whole = st.fin(0, st.part.shape[0])
                send(f"ring{st.i}", whole, whole, sib_dev)

    def turn(count=1):
        for _ in range(count):
            for st in streams:
                if st.turn <= 2 * ahead:
                    advance(st)

    if not ring:
        for name in ["fin_out", "fin_in", "fin_k", "fin_v", "fin_q", "fin_o"]:
            ref = getattr(r, name)
            ref[...] = jnp.zeros_like(ref)

    arrive("act")
    arrive("cot")

    def grad_out(j):
        cols = pl.ds(pl.multiple_of(core * (F // 2) + j * 256, 128), 256)
        tile = mm_tn(r.act[:, cols], r.v_cot[0]) + mm_tn(r.act_sib[:, aligned(j * 256, 256)], r.v_cot[1])
        r.part_out[aligned(j * 256, 256), :] = tile.astype(BF16)

    loop(F // 2 // 256, grad_out)

    def rows_of(ref, base, cols=None):
        def block(at, size):
            rows = pl.ds(pl.multiple_of(base + at, 16), size)
            return ref.at[rows] if cols is None else ref.at[rows, cols]

        return block

    add_stream(r.part_out, rows_of(r.fin_out, core * (F // 2)))
    turn()
    arrive("dup")
    arrive("n2")

    def grad_in(j):
        cols = aligned(j * 256, 256)
        tile = mm_tn(r.n2[0, :, cols], r.dup[:, own_units]) + mm_tn(r.n2[1, :, cols], r.dup_sib[...])
        r.part_in[cols, :] = tile.astype(BF16)

    loop(D // 256, grad_in)
    add_stream(r.part_in, rows_of(r.fin_in, 0, own_units))
    if ring:
        advance(streams[-1])

    arrive("dn")

    def second_norm_back(i, carry):
        gain_sum, shift_sum = carry
        rows = pl.ds(pl.multiple_of(h * half + i * 64, 64), 64)
        at = aligned(i * 64, 64)
        scaled, inverse = normalize(r.resid[rows, :])
        grad = r.dn_own[at, :] + r.dn_recv[at, :].astype(F32)
        d_resid = r.v_cot[0, rows, :].astype(F32) + normalize_back(grad, gain(r.v_g2), scaled, inverse)
        r.dres[at, :] = d_resid
        r.dat[rows, :] = d_resid.astype(BF16)
        return gain_sum + fold_rows(grad * scaled), shift_sum + fold_rows(grad)

    zero = jnp.zeros((8, D), F32)
    gain_sum, shift_sum = lax.fori_loop(0, half // 64, second_norm_back, (zero, zero))
    r.norm_grads[2:3, :] = jnp.sum(gain_sum, axis=0, keepdims=True)
    r.norm_grads[3:4, :] = jnp.sum(shift_sum, axis=0, keepdims=True)
    own_rows = aligned(h * half, half)
    other_rows = aligned(oh * half, half)
    for x in range(2):
        d_gathered = mm_nt(r.dat[own_rows, :], r.v_wo[x]).astype(BF16)
        for p in range(pairs):
            hot = r.oht[x, pair_rows(p), own_rows]
            r.dc[x, :, pair(p)] = fold(mm(hot, d_gathered[:, pair(p)]))[:SENT].astype(BF16)
    for x in range(2):
        scatter(r.dc.at[x], r.rs, me, x)
    send("dat", r.dat.at[own_rows], r.dat.at[own_rows], x_dev)

    turn(1)

    def ffn_part(j):
        cols = aligned(j * 256, 256)
        r.fp[h, :, cols] = mm(r.act[...], r.v_wout[:, cols]).astype(BF16)

    loop(D // 256, ffn_part)
    send("fp", r.fp.at[h], r.fp.at[h], x_dev)
    wq_mine = pl.ds(pl.multiple_of(core * W, 16), W)
    send("wq", r.v_wq.at[h, wq_mine], r.v_wq.at[h, wq_mine], x_dev)
    turn(1)

    @pl.when(is_owner)
    def _():
        gathered_at_owner(r.rs, 2 * S, 4)
        rows = aligned(group * GROUP, GROUP)
        d_cluster = total_of(r.rs, 2 * S).astype(BF16)
        r.ag3[rows, :] = d_cluster
        spread(r.ag3, 3, 1, r.rs)
        product = d_cluster.astype(F32) * r.own_out[...]
        delta = jnp.zeros((GROUP, 128), F32)
        for p in range(pairs):
            block = product[:, pair(p)]
            delta = delta + jnp.where(
                lanes == 2 * p, jnp.sum(jnp.where(left, block, 0.0), axis=1, keepdims=True), 0.0
            )
            delta = delta + jnp.where(
                lanes == 2 * p + 1, jnp.sum(jnp.where(left, 0.0, block), axis=1, keepdims=True), 0.0
            )
        r.agdelta[rows, :] = delta
        spread(r.agdelta, 4, 1, r.rss)

    turn(1)
    arrive("dat")
    send("dat_sib", r.dat.at[:, sib_half], r.dat_sib, sib_dev)
    arrive("gat")
    spread_arrive(r.aglse, 2)
    spread_arrive(r.ag3, 3)
    spread_arrive(r.agdelta, 4)

    for p in range(pairs):
        d_probs = mm_nt(unfold(r.ag3[:, pair(p)]), r.v[:, pair(p)])
        factor = jnp.exp(column(r.stats[...], p) - column(r.aglse[...], p))
        probs = r.e[pair_rows(p), :] * factor
        r.pb[pair_rows(p), :] = probs.astype(BF16)
        d_scores = (probs * (d_probs - column(r.agdelta[...], p))).astype(BF16)
        r.dsb[pair_rows(p), :] = d_scores
        r.dcen[:, pair(p)] = fold(mm(d_scores, r.k[:, pair(p)]))[:SENT].astype(BF16)
    scatter(r.dcen, r.rs, s, h)

    turn(1)
    for p in range(pairs):
        r.dkv[0, :, pair(p)] = (mm_tn(r.dsb[pair_rows(p), :], unfold(r.ag1[:, pair(p)])) * scale).astype(BF16)
        r.dkv[1, :, pair(p)] = mm_tn(r.pb[pair_rows(p), :], unfold(r.ag3[:, pair(p)])).astype(BF16)
    send("dkv", r.dkv, r.dkv_sib, sib_dev)
    turn(1)

    @pl.when(is_owner)
    def _():
        gathered_at_owner(r.rs, S, 5)
        rows = aligned(group * GROUP, GROUP)
        r.ag4[h, rows, :] = (total_of(r.rs, S) * scale / r.divisor[...]).astype(BF16)
        spread(r.ag4.at[h], 5, 2, r.rs)

    def kv_part(rows):
        return mm_nt(r.dkv[0, rows, :], r.v_wk[...]) + mm_nt(r.dkv[1, rows, :], r.v_wv[...])

    r.kv_send[...] = kv_part(other_rows).astype(BF16)
    send("kv", r.kv_send, r.kv_recv, x_dev)
    turn(1)
    arrive("dkv")
    arrive("nrm")
    for i in range(2):
        tile = mm_tn(r.nrm[:, own_half], r.dkv[i]) + mm_tn(r.nrm_sib[...], r.dkv_sib[i])
        r.part_small[i] = tile.astype(BF16)
    for i, name in enumerate(["fin_k", "fin_v"]):
        add_stream(r.part_small.at[i], rows_of(getattr(r, name), core * W))
        if ring:
            advance(streams[-1])
    r.kv_own[...] = kv_part(own_rows)
    arrive("wq")
    send("wq_sib", r.v_wq.at[oh, wq_mine], r.v_wq.at[oh, wq_mine], sib_dev)
    turn(1)
    arrive("dat_sib")
    tile = mm_tn(r.gat[h], r.dat[:, own_half]) + mm_tn(r.gat_sib[...], r.dat_sib[...])
    r.part_small[2] = tile.astype(BF16)
    add_stream(r.part_small.at[2], rows_of(r.fin_o, 0, own_half))
    if ring:
        advance(streams[-1])
    turn(1)

    for x in range(2):
        spread_arrive(r.ag4.at[x], 5, x)
    for p in range(pairs):
        r.dq[:, pair(p)] = mm(r.oh[h, :, pair_rows(p)], unfold(r.ag4[h, :, pair(p)])).astype(BF16)
    send("dq", r.dq, r.dq_sib, sib_dev)
    for p in range(pairs):
        r.dq_other[:, pair(p)] = mm(r.oh[oh, own_rows, pair_rows(p)], unfold(r.ag4[oh, :, pair(p)])).astype(BF16)
    turn(1)
    arrive("dq")
    r.part_small[3] = (mm_tn(r.nrm[:, own_half], r.dq[...]) + mm_tn(r.nrm_sib[...], r.dq_sib[...])).astype(BF16)
    add_stream(r.part_small.at[3], rows_of(r.fin_q, core * W))
    if ring:
        advance(streams[-1])
    turn(1)

    arrive("kv")
    arrive("wq_sib")

    def first_norm_back(i, carry):
        gain_sum, shift_sum = carry
        rows = pl.ds(pl.multiple_of(h * half + i * 64, 64), 64)
        at = aligned(i * 64, 64)
        scaled, inverse = normalize(r.v_tok[rows, :].astype(F32))
        grad = r.kv_own[at, :] + r.kv_recv[at, :].astype(F32)
        grad = grad + mm_nt(r.dq[rows, :], r.v_wq[h]) + mm_nt(r.dq_other[at, :], r.v_wq[oh])
        grad_tokens = r.dres[at, :] + normalize_back(grad, gain(r.v_g1), scaled, inverse)
        r.gtok[rows, :] = grad_tokens.astype(BF16)
        return gain_sum + fold_rows(grad * scaled), shift_sum + fold_rows(grad)

    gain_sum, shift_sum = lax.fori_loop(0, half // 64, first_norm_back, (zero, zero))
    r.norm_grads[0:1, :] = jnp.sum(gain_sum, axis=0, keepdims=True)
    r.norm_grads[1:2, :] = jnp.sum(shift_sum, axis=0, keepdims=True)
    send("norm", r.norm_grads, r.norm_recv, x_dev)
    send("gtok", r.gtok.at[own_rows], r.gtok.at[own_rows], x_dev)
    turn(1)
    arrive("norm")
    r.norm_pair[...] = r.norm_grads[...] + r.norm_recv[...]

    blocks = D // 128

    def norm_to(g):
        cols = pl.ds(g * 128, 128)
        mine = s == first + g
        copy = remote(r.norm_pair.at[:, cols], r.norm_rs.at[s], r.norm_send.at[g], r.norm_sem.at[0], (first + g, h))
        return cols, mine, copy

    for g in range(blocks):
        cols, mine, copy = norm_to(g)

        @pl.when(jnp.logical_not(mine))
        def _():
            copy.start()

        @pl.when(mine)
        def _():
            r.norm_rs[s] = r.norm_pair[:, cols]

    turn(1)
    arrive("fp")

    def block_out(i):
        rows = aligned(i * 64, 64)
        r.bout[rows, :] = (r.resid[rows, :] + r.fp[0, rows, :].astype(F32) + r.fp[1, rows, :].astype(F32)).astype(BF16)

    loop(T // 64, block_out)
    turn(1)
    norm_owner = jnp.logical_and(s >= first, s < first + blocks)

    @pl.when(norm_owner)
    def _():
        block = r.norm_rs.at[pl.ds(0, S - 1)]
        remote(block, block, r.norm_send.at[0], r.norm_sem.at[0], x_dev).wait_recv()

        def add(i, acc):
            return acc + r.norm_rs[i]

        cols = aligned(group * 128, 128)
        r.norm_fin[:, cols] = lax.fori_loop(0, S, add, jnp.zeros((8, 128), F32))
        block = r.norm_fin.at[:, cols]

        def to(k):
            remote(block, block, r.norm_send.at[blocks], r.norm_sem.at[1 + group], (lax.rem(s + k + 1, S), h)).start()

        loop(S - 1, to)

    turn(1)
    for g in range(blocks):
        block = r.norm_fin.at[:, pl.ds(g * 128, 128)]

        @pl.when(s != first + g)
        def _():
            remote(block, block, r.norm_send.at[0], r.norm_sem.at[1 + g], x_dev).wait_recv()

    arrive("gtok")
    while any(st.turn <= 2 * ahead for st in streams):
        turn()
    for st in streams:
        arrive(f"ring{st.i}")

    outs = [
        ("bout", "o_block"),
        ("gtok", "o_tokens"),
        ("norm_fin", "o_norm"),
        ("fin_q", "o_q"),
        ("fin_k", "o_k"),
        ("fin_v", "o_v"),
        ("fin_o", "o_o"),
        ("fin_in", "o_in"),
        ("fin_out", "o_out"),
    ]
    stores = [
        pltpu.make_async_copy(getattr(r, a), getattr(r, b), r.store_sem.at[i]) for i, (a, b) in enumerate(outs)
    ]
    for store in stores:
        store.start()
    for finish in at_end:
        finish()
    for g in range(blocks):
        cols, mine, copy = norm_to(g)

        @pl.when(jnp.logical_not(mine))
        def _():
            copy.wait_send()

    @pl.when(norm_owner)
    def _():
        block = r.norm_rs.at[pl.ds(0, S - 1)]
        remote(block, block, r.norm_send.at[blocks], r.norm_sem.at[0], x_dev).wait_send()

    for store in stores:
        store.wait()


def per_device(
    S,
    tokens,
    norm1_gain,
    norm1_shift,
    w_query,
    w_key,
    w_value,
    w_output,
    norm2_gain,
    norm2_shift,
    w_in,
    w_out,
    cluster_ids,
    masked_keys,
    cotangent,
):
    T, D = tokens.shape
    LH = cluster_ids.shape[1]
    W = w_query.shape[1]
    F = w_in.shape[1]
    n = S // 2
    ring = n <= 8
    cfg = SimpleNamespace(S=S, T=T, D=D, W=W, LH=LH, F=F, ring=ring, scatter_of=[0, 1, 2, 3, 4, 4, 5])

    M = -(-masked_keys.shape[0] // 1024) * 1024
    if M != masked_keys.shape[0]:
        masked_keys = jnp.pad(masked_keys, (0, M - masked_keys.shape[0]), constant_values=-1)
    cfg.M = M
    inputs = dict(
        tok=tokens,
        g1=norm1_gain,
        b1=norm1_shift,
        wq=w_query,
        wk=w_key,
        wv=w_value,
        wo=w_output,
        g2=norm2_gain,
        b2=norm2_shift,
        win=w_in,
        wout=w_out,
        ids=cluster_ids.T,
        masked=masked_keys.reshape(M // 128, 128),
        cot=cotangent,
    )
    outputs = dict(
        o_block=((T, D), BF16),
        o_tokens=((T, D), BF16),
        o_norm=((8, D), F32),
        o_q=((D, W), BF16),
        o_k=((D, W), BF16),
        o_v=((D, W), BF16),
        o_o=((W, D), BF16),
        o_in=((D, F), BF16),
        o_out=((F, D), BF16),
    )
    half = T // 2
    vmem = dict(
        v_tok=((T, D), BF16),
        v_g1=((D,), F32),
        v_b1=((D,), F32),
        v_wq=((2, D, W), BF16),
        v_wk=((D, W), BF16),
        v_wv=((D, W), BF16),
        v_wo=((2, W, D), BF16),
        v_g2=((D,), F32),
        v_b2=((D,), F32),
        v_win=((D, F), BF16),
        v_wout=((F, D), BF16),
        v_ids=((2, LH, T), jnp.int32),
        v_masked=((M // 128, 128), jnp.int32),
        v_cot=((2, T, D), BF16),
        nrm=((T, D), BF16),
        nrm_sib=((T, W), BF16),
        q=((T, W), BF16),
        k=((T, W), BF16),
        v=((T, W), BF16),
        oht=((2, LH * SLOT, T), BF16),
        oh=((2, T, LH * SLOT), BF16),
        sums=((SENT, W), BF16),
        counts=((SENT, 128), F32),
        rs=((2 * S, GROUP, W), BF16),
        rss=((S, GROUP, 128), F32),
        divisor=((GROUP, W), F32),
        ag1=((SLOT, W), BF16),
        dact=((T, F), F32),
        e=((LH * SLOT, T), F32),
        numer=((SENT, W), BF16),
        stats=((SLOT, 128), F32),
        own_out=((GROUP, W), F32),
        ag2=((2, SLOT, W), BF16),
        aglse=((SLOT, 128), F32),
        gat=((2, T, W), BF16),
        gat_sib=((T, W), BF16),
        resid=((T, D), F32),
        n2=((2, T, D), BF16),
        act=((T, F), BF16),
        dup=((T, F), BF16),
        act_sib=((T, F // 2), BF16),
        dup_sib=((T, F // 2), BF16),
        dn_send=((half, D), BF16),
        dn_recv=((half, D), BF16),
        dn_own=((half, D), F32),
        dres=((half, D), F32),
        dat=((T, D), BF16),
        dat_sib=((T, W), BF16),
        dc=((2, SENT, W), BF16),
        ag3=((SLOT, W), BF16),
        agdelta=((SLOT, 128), F32),
        pb=((LH * SLOT, T), BF16),
        dsb=((LH * SLOT, T), BF16),
        dcen=((SENT, W), BF16),
        ag4=((2, SLOT, W), BF16),
        dkv=((2, T, W), BF16),
        dkv_sib=((2, T, W), BF16),
        kv_send=((half, D), BF16),
        kv_recv=((half, D), BF16),
        kv_own=((half, D), F32),
        dq=((T, W), BF16),
        dq_sib=((T, W), BF16),
        dq_other=((half, W), BF16),
        gtok=((T, D), BF16),
        norm_grads=((8, D), F32),
        norm_recv=((8, D), F32),
        norm_pair=((8, D), F32),
        norm_rs=((S, 8, 128), F32),
        norm_fin=((8, D), F32),
        fp=((2, T, D), BF16),
        bout=((T, D), BF16),
        part_out=((F // 2, D), BF16),
        part_in=((D, F // 2), BF16),
        part_small=((4, W, W), BF16),
        fin_out=((F, D), BF16),
        fin_in=((D, F), BF16),
        fin_k=((D, W), BF16),
        fin_v=((D, W), BF16),
        fin_q=((D, W), BF16),
        fin_o=((W, D), BF16),
    )
    steps = 2 * (n - 1) if ring else 1
    if ring:
        vmem["ring_wide"] = ((2, n - 1, D // n, D), BF16)
        vmem["ring_slim"] = ((4, n - 1, W // n, W), BF16)
    sems = dict(
        load_sem=(14,),
        store_sem=(9,),
        ex_send=(32,),
        ex_recv=(32,),
        sc_send=(7, GROUPS),
        sc_recv=(6,),
        sp_send=(6,),
        sp_recv=(6, 2, GROUPS),
        ring_send=(STREAMS, steps),
        ring_recv=(STREAMS, steps),
        norm_send=(D // 128 + 1,),
        norm_sem=(D // 128 + 1,),
    )
    names = list(inputs) + list(outputs) + list(vmem) + list(sems)
    results = pl.pallas_call(
        functools.partial(kernel, cfg, names),
        out_shape=[jax.ShapeDtypeStruct(*o) for o in outputs.values()],
        in_specs=[pl.BlockSpec(memory_space=pl.ANY)] * len(inputs),
        out_specs=[pl.BlockSpec(memory_space=pl.ANY)] * len(outputs),
        scratch_shapes=[pltpu.VMEM(*b) for b in vmem.values()] + [pltpu.SemaphoreType.DMA(b) for b in sems.values()],
        compiler_params=pltpu.CompilerParams(collective_id=0, has_side_effects=True, vmem_limit_bytes=cfg_vmem()),
        name="block",
    )(*inputs.values())
    block, grad_tokens, norms, *grads = results
    if not ring:
        grads = lax.psum(grads, "seq")
    block, gain1, shift1, gain2, shift2, grad_tokens, *grads = widen(block, norms, [grad_tokens] + grads)
    grad_q, grad_k, grad_v, grad_o, grad_in, grad_out = grads
    return (
        block,
        grad_tokens,
        gain1,
        shift1,
        grad_q,
        grad_k,
        grad_v,
        grad_o,
        gain2,
        shift2,
        grad_in,
        grad_out,
    )


def widen(block, norms, arrays):
    D = norms.shape[1]
    tiles = [
        (i, k * size, size)
        for i, a in enumerate(arrays)
        for size in [a.shape[0] // max(2, a.shape[0] // 256)]
        for k in range(a.shape[0] // size)
    ]
    count = len(arrays)

    def kernel(*refs):
        block_in, norms_in, *rest = refs
        ins, rest = rest[:count], rest[count:]
        block_out, *rest = rest
        norm_outs, rest = rest[:4], rest[4:]
        outs, rest = rest[:count], rest[count:]
        block_tmp, norms_tmp, *rest = rest
        flat, rest = rest[:4], rest[4:]
        narrow, rest = rest[:count], rest[count:]
        wide, rest = rest[:count], rest[count:]
        sem_in, sem_out, sem = rest
        first = pltpu.make_async_copy(block_in, block_tmp, sem.at[0])
        first_norms = pltpu.make_async_copy(norms_in, norms_tmp, sem.at[1])
        loads = [
            pltpu.make_async_copy(ins[i].at[pl.ds(at, size)], narrow[i].at[pl.ds(at, size)], sem_in.at[k])
            for k, (i, at, size) in enumerate(tiles)
        ]
        for load in loads:
            load.start()
        first_norms.start()
        first.start()
        stores = []
        for k, (i, at, size) in enumerate(tiles):
            loads[k].wait()

            def cast(j, i=i, at=at):
                rows = pl.ds(pl.multiple_of(at + j * 32, 32), 32)
                wide[i][rows, :] = narrow[i][rows, :].astype(F32)

            loop(size // 32, cast)
            rows = pl.ds(at, size)
            stores.append(pltpu.make_async_copy(wide[i].at[rows], outs[i].at[rows], sem_out.at[k]))
            stores[-1].start()
        first_norms.wait()
        for k in range(4):
            flat[k][...] = norms_tmp[k, :]
            stores.append(pltpu.make_async_copy(flat[k], norm_outs[k], sem.at[2 + k]))
            stores[-1].start()
        first.wait()
        stores.append(pltpu.make_async_copy(block_tmp, block_out, sem.at[6]))
        stores[-1].start()
        for store in stores:
            store.wait()

    out_shape = [jax.ShapeDtypeStruct(block.shape, block.dtype)]
    out_shape += [jax.ShapeDtypeStruct((D,), F32)] * 4
    out_shape += [jax.ShapeDtypeStruct(a.shape, F32) for a in arrays]
    anywhere = pl.BlockSpec(memory_space=pl.ANY)
    return pl.pallas_call(
        kernel,
        out_shape=out_shape,
        in_specs=[anywhere] * (count + 2),
        out_specs=[anywhere] * len(out_shape),
        scratch_shapes=[pltpu.VMEM(block.shape, block.dtype), pltpu.VMEM(norms.shape, F32)]
        + [pltpu.VMEM((D,), F32)] * 4
        + [pltpu.VMEM(a.shape, a.dtype) for a in arrays]
        + [pltpu.VMEM(a.shape, F32) for a in arrays]
        + [pltpu.SemaphoreType.DMA((len(tiles),)), pltpu.SemaphoreType.DMA((len(tiles),)), pltpu.SemaphoreType.DMA((7,))],
        compiler_params=pltpu.CompilerParams(vmem_limit_bytes=cfg_vmem()),
        name="widen",
    )(block, norms, *arrays)


def cfg_vmem():
    return 62 * 2**20


def solution(mesh):
    columns, rows = P(None, "head"), P("head", None)
    by_token = P("seq", None)
    return jax.shard_map(
        functools.partial(per_device, mesh.shape["seq"]),
        mesh=mesh,
        in_specs=(by_token, P(), P(), columns, columns, columns, rows, P(), P(), columns, rows, P("seq", "head"), P(), by_token),
        out_specs=(by_token, by_token, P(), P(), columns, columns, columns, rows, P(), P(), columns, rows),
        check_vma=False,
    )
```

```python
import functools
from types import SimpleNamespace

import jax
import jax.numpy as jnp
from jax import lax
from jax.experimental import pallas as pl
from jax.experimental.pallas import tpu as pltpu
from jax.sharding import PartitionSpec as P

CLUSTERS = 100
EPSILON = 1e-05
MESH = pl.DeviceIdType.MESH
F32 = jnp.float32
BF16 = jnp.bfloat16
SLOT = 128
GROUP = 16
GROUPS = -(-CLUSTERS // GROUP)
SENT = GROUPS * GROUP
STREAMS = 9


def mm(a, b):
    return lax.dot_general(a, b, (((1,), (0,)), ((), ())), preferred_element_type=F32)


def mm_nt(a, b):
    return lax.dot_general(a, b, (((1,), (1,)), ((), ())), preferred_element_type=F32)


def mm_tn(a, b):
    return lax.dot_general(a, b, (((0,), (0,)), ((), ())), preferred_element_type=F32)


def aligned(index, size):
    return pl.ds(pl.multiple_of(index, size), size)


def remote(src, dst, send_sem, recv_sem, device):
    return pltpu.make_async_remote_copy(
        src_ref=src, dst_ref=dst, send_sem=send_sem, recv_sem=recv_sem, device_id=device, device_id_type=MESH
    )


def loop(count, body):
    def step(i, carry):
        body(i)
        return carry

    lax.fori_loop(0, count, step, 0)


def normalize(values):
    centred = values - jnp.mean(values, axis=-1, keepdims=True)
    inverse = lax.rsqrt(jnp.mean(centred * centred, axis=-1, keepdims=True) + EPSILON)
    return centred * inverse, inverse


def normalize_back(grad, gain, scaled, inverse):
    inner = grad * gain
    return inverse * (
        inner - jnp.mean(inner, axis=-1, keepdims=True) - scaled * jnp.mean(inner * scaled, axis=-1, keepdims=True)
    )


ERFC = (
    0.27643095583919713,
    0.2770312983463117,
    0.2368366418089808,
    0.21634403047784398,
    -0.05751923336137985,
    0.34364725799951945,
    -0.5200124379554546,
    0.2829391760305868,
    -0.05569765451595309,
)


def normal_share(x, bell):
    t = 1.0 / (1.0 + (0.49 * 0.5**0.5) * jnp.abs(x))
    series = 0.5 * ERFC[-1]
    for factor in ERFC[-2::-1]:
        series = series * t + 0.5 * factor
    tail = series * t * bell
    return jnp.where(x < 0, tail, 1.0 - tail)


def fold_rows(values):
    return jnp.sum(values.reshape(values.shape[0] // 8, 8, values.shape[1]), axis=0)


def kernel(cfg, names, *all_refs):
    r = SimpleNamespace(**dict(zip(names, all_refs)))
    S, T, D, W, LH, F = cfg.S, cfg.T, cfg.D, cfg.W, cfg.LH, cfg.F
    pairs = LH // 2
    half = T // 2
    scale = (W // LH) ** (-0.5)
    ring = cfg.ring
    n = S // 2
    s = lax.axis_index("seq")
    h = lax.axis_index("head")
    oh = 1 - h
    core = lax.rem(s, 2)
    chip = lax.div(s, 2)
    me = s * 2 + h
    x_dev = (s, oh)
    sib_dev = (s + 1 - 2 * core, h)
    first = S // 4
    is_owner = jnp.logical_and(s >= first, s < first + GROUPS)
    group = s - first
    lanes = lax.broadcasted_iota(jnp.int32, (1, 128), 1)
    left = lanes < 64

    def fold(block):
        return jnp.where(left, block[:SLOT], block[SLOT:])

    def unfold(block):
        zero = jnp.zeros_like(block)
        return jnp.concatenate([jnp.where(left, block, zero), jnp.where(left, zero, block)], axis=0)

    def expand(stats):
        return jnp.concatenate(
            [jnp.where(left, stats[:, 2 * p : 2 * p + 1], stats[:, 2 * p + 1 : 2 * p + 2]) for p in range(pairs)], axis=1
        )

    def column(stats, p, at=0):
        return jnp.concatenate(
            [stats[:, at + 2 * p : at + 2 * p + 1], stats[:, at + 2 * p + 1 : at + 2 * p + 2]], axis=0
        )

    def place(columns, p, at=0):
        rows = columns.shape[0] // 2
        return jnp.where(lanes == at + 2 * p, columns[:rows], 0.0) + jnp.where(
            lanes == at + 2 * p + 1, columns[rows:], 0.0
        )

    def pair(p):
        return slice(p * 128, (p + 1) * 128)

    def pair_rows(p):
        return slice(p * 2 * SLOT, (p + 1) * 2 * SLOT)

    at_end = []

    loads = {}
    for i, name in enumerate(
        ["ids", "tok", "g1", "b1", "wq", "wo", "wk", "wv", "cot", "wout", "masked", "win", "g2", "b2"]
    ):
        dst = getattr(r, "v_" + name)
        dst = {"cot": lambda d: d.at[0], "wq": lambda d: d.at[h], "wo": lambda d: d.at[h], "ids": lambda d: d.at[h]}.get(
            name, lambda d: d
        )(dst)
        loads[name] = pltpu.make_async_copy(getattr(r, name), dst, r.load_sem.at[i])

    barrier = pltpu.get_barrier_semaphore()

    def greet(k):
        other = lax.rem(me + k + 1, 2 * S)
        pl.semaphore_signal(
            barrier, inc=1, device_id=(lax.div(other, 2), lax.rem(other, 2)), device_id_type=MESH
        )

    loop(2 * S - 1, greet)
    for load in loads.values():
        load.start()

    exchanges = {}

    def send(name, src, dst, device):
        i = len(exchanges)
        copy = remote(src, dst, r.ex_send.at[i], r.ex_recv.at[i], device)
        copy.start()
        exchanges[name] = copy
        at_end.append(copy.wait_send)

    def arrive(name):
        exchanges[name].wait_recv()

    counters = {"scatter": 0, "spread": 0}

    def scatter(src, dst, slot, plane):
        i = counters["scatter"]
        counters["scatter"] += 1

        def at(g):
            rows = pl.ds(g * GROUP, GROUP)
            mine = jnp.logical_and(s == first + g, h == plane)
            copy = remote(
                src.at[rows], dst.at[slot, :, cols], r.sc_send.at[i, g], r.sc_recv.at[cfg.scatter_of[i]], (first + g, plane)
            )
            return rows, mine, copy

        cols = pl.ds(0, src.shape[1])

        for g in range(GROUPS):
            rows, mine, copy = at(g)

            @pl.when(jnp.logical_not(mine))
            def _():
                copy.start()

            @pl.when(mine)
            def _():
                dst[slot, :, cols] = src[rows, :]

        def finish():
            for g in range(GROUPS):
                rows, mine, copy = at(g)

                @pl.when(jnp.logical_not(mine))
                def _():
                    copy.wait_send()

        at_end.append(finish)

    def gathered_at_owner(buf, count, width, i):
        block = buf.at[pl.ds(0, count - 1), :, pl.ds(0, width)]
        remote(block, block, r.sc_send.at[0, 0], r.sc_recv.at[i], x_dev).wait_recv()

    def spread(buf, i, like):
        rows = aligned(group * GROUP, GROUP)
        block = buf.at[rows]

        def to(k):
            copy = remote(block, block, r.sp_send.at[i], r.sp_recv.at[i, group], (lax.rem(s + k + 1, S), h))
            copy.start()

        loop(S - 1, to)

        def finish():
            @pl.when(is_owner)
            def _():
                block = like.at[pl.ds(0, S - 1), :, pl.ds(0, buf.shape[1])]
                remote(block, block, r.sp_send.at[i], r.sp_recv.at[i, 0], x_dev).wait_send()

        at_end.append(finish)

    def spread_arrive(buf, i):
        for g in range(GROUPS):

            @pl.when(s != first + g)
            def _():
                block = buf.at[pl.ds(g * GROUP, GROUP)]
                remote(block, block, r.sp_send.at[i], r.sp_recv.at[i, g], x_dev).wait_recv()

    def spread_pass(buf, i, j):
        for g in range(GROUPS):
            block = buf.at[h, pl.ds(g * GROUP, GROUP)]

            @pl.when(s != first + g)
            def _():
                remote(block, block, r.sp_send.at[i], r.sp_recv.at[i, g], x_dev).wait_recv()

            copy = remote(block, block, r.pass_send.at[j, g], r.pass_recv.at[j, g], x_dev)
            copy.start()
            at_end.append(copy.wait_send)

    def pass_arrive(buf, j):
        for g in range(GROUPS):
            block = buf.at[oh, pl.ds(g * GROUP, GROUP)]
            remote(block, block, r.pass_send.at[j, g], r.pass_recv.at[j, g], x_dev).wait_recv()

    def total_of(buf, count, width):
        def add(i, acc):
            return acc + jnp.sum(buf[aligned(i * 16, 16), :, :width].astype(F32), axis=0)

        return lax.fori_loop(0, count // 16, add, jnp.zeros((GROUP, width), F32))

    def split(values):
        high = values.astype(BF16).astype(F32)
        return high, values - high

    z_count = n // 2
    z, y = lax.div(chip, 2), lax.rem(chip, 2)
    position = jnp.where(y == 0, z, n - 1 - z)

    def device_at(p):
        p = lax.rem(p + n, n)
        return (2 * jnp.where(p < z_count, 2 * p, 2 * (n - 1 - p) + 1) + core, h)

    streams = []
    ahead, behind = n // 2, n - 1 - n // 2

    def add_stream(name, part, fin_block, recv, shared=True, at=0, last=2 * ahead):
        i = len(streams)
        st = SimpleNamespace(name=name, i=i, part=part, fin=fin_block, turn=at, last=last)
        st.chunk = part.shape[0] // n
        st.recv = recv
        st.shared = shared
        st.ways = [(1, ahead, 0), (-1, behind, ahead)] if i % 2 == 0 else [(-1, ahead, 0), (1, behind, ahead)]
        if ring:
            streams.append(st)
            advance(st)
        else:
            st.fin(0, part.shape[0])[...] = part[...]
        return st

    def part_chunk(st, k):
        return st.part.at[pl.ds(pl.multiple_of(lax.rem(k + 2 * n, n) * st.chunk, 16), st.chunk)]

    def fin_chunk(st, k):
        return st.fin(lax.rem(k + 2 * n, n) * st.chunk, st.chunk)

    def sum_copy(st, way, t):
        sign, hops, slot = way
        src = part_chunk(st, position + sign * hops) if t == 0 else st.recv.at[slot + t - 1]
        return remote(
            src,
            st.recv.at[slot + t],
            r.ring_send.at[st.i, slot + t],
            r.ring_recv.at[st.i, slot + t],
            device_at(position + sign),
        )

    def pass_copy(st, way, t):
        sign, hops, slot = way
        block = fin_chunk(st, position - sign * t)
        return remote(
            block,
            block,
            r.ring_send.at[st.i, n - 1 + slot + t],
            r.ring_recv.at[st.i, n - 1 + slot + t],
            device_at(position + sign),
        )

    def start(copy):
        copy.start()
        at_end.append(copy.wait_send)

    def advance(st):
        t = st.turn
        st.turn += 1
        if t <= ahead:
            for way in st.ways:
                sign, hops, slot = way
                if 0 < t <= hops and st.recv is not None:
                    sum_copy(st, way, t - 1).wait_recv()
                    if t < hops:
                        came = st.recv[slot + t - 1].astype(F32) + part_chunk(st, position + sign * (hops - t))[...].astype(F32)
                        st.recv[slot + t - 1] = came.astype(BF16)
                if t < hops:
                    start(sum_copy(st, way, t))
            if t == ahead:
                if st.recv is not None:
                    total = part_chunk(st, position)[...].astype(F32)
                    for sign, hops, slot in st.ways:
                        total = total + st.recv[slot + hops - 1].astype(F32)
                    fin_chunk(st, position)[...] = total.astype(BF16)
                for way in st.ways if st.last > ahead else []:
                    start(pass_copy(st, way, 0))
        elif t <= 2 * ahead:
            u = t - ahead
            for way in st.ways:
                sign, hops, slot = way
                if u <= hops:
                    block = fin_chunk(st, position - sign * u)
                    remote(
                        block, block, r.ring_send.at[st.i, 0], r.ring_recv.at[st.i, n - 1 + slot + u - 1], x_dev
                    ).wait_recv()
                if u < hops:
                    start(pass_copy(st, way, u))
            if u == ahead and st.shared:
                whole = st.fin(0, st.part.shape[0])
                send(f"ring{st.i}", whole, whole, sib_dev)

    def tick(*wanted):
        for name in wanted:
            for st in streams:
                if st.name == name and st.turn <= st.last:
                    advance(st)

    def pending():
        return [st.name for st in streams if st.turn <= st.last]

    if not ring:
        for name in ["fin_out", "fin_in", "fin_k", "fin_v", "fin_q", "fin_o"]:
            ref = getattr(r, name)
            ref[...] = jnp.zeros_like(ref)

    def rows_of(ref, base, cols=None):
        def block(at, size):
            rows = pl.ds(pl.multiple_of(base + at, 16), size)
            return ref.at[rows] if cols is None else ref.at[rows, cols]

        return block

    stores = []
    targets = dict(
        bout=r.o_block,
        gtok=r.o_tokens,
        norm_fin=r.o_norm,
        fin_q=r.o_q,
        fin_k=r.o_k,
        fin_v=r.o_v,
        fin_o=r.o_o,
        fin_in=r.o_in,
        fin_out=r.o_out,
    )

    def store(name):
        copy = pltpu.make_async_copy(getattr(r, name), targets[name], r.store_sem.at[len(stores)])
        copy.start()
        stores.append(copy)

    r.ag1[...] = jnp.zeros_like(r.ag1)
    r.ag3[...] = jnp.zeros_like(r.ag3)
    r.ag2[...] = jnp.zeros_like(r.ag2)
    r.ag4[...] = jnp.zeros_like(r.ag4)
    r.agdelta[...] = jnp.zeros_like(r.agdelta)
    r.norm_grads[...] = jnp.zeros_like(r.norm_grads)

    def onehot_t(ids, out):
        rows = lax.broadcasted_iota(jnp.int32, (SLOT, T), 0)
        for j in range(LH):
            out[j * SLOT : (j + 1) * SLOT, :] = jnp.where(rows == ids[j : j + 1, :], 1.0, 0.0).astype(BF16)

    def onehot(x):
        onehot_t(r.v_ids[x], r.oht.at[x])
        for p in range(pairs):
            r.oh[x, :, pair_rows(p)] = r.oht[x, pair_rows(p), :].T

    def gain(ref):
        return ref[...].reshape(1, D)

    loads["ids"].wait()
    onehot(h)
    for name in ["g1", "b1", "tok"]:
        loads[name].wait()

    def first_norm(i):
        rows = aligned(i * 64, 64)
        scaled, _ = normalize(r.v_tok[rows, :].astype(F32))
        r.nrm[rows, :] = (scaled * gain(r.v_g1) + gain(r.v_b1)).astype(BF16)

    loop(T // 64, first_norm)
    loads["wq"].wait()

    def project(weight, out):
        def tile(i):
            rows = aligned(i * 256, 256)
            out[rows, :] = mm(r.nrm[rows, :], weight).astype(BF16)

        loop(T // 256, tile)

    project(r.v_wq[h], r.q)
    counts = jnp.zeros((SLOT, 128), F32)
    ones = jnp.ones((T, 128), BF16)
    for p in range(pairs):
        hot = r.oht[h, pair_rows(p), :]
        r.sums[:, pair(p)] = fold(mm(hot, r.q[:, pair(p)]))[:SENT].astype(BF16)
        counts = counts + place(mm(hot, ones)[:, :1], p)
    high = jnp.where(counts >= 256.0, 256.0, 0.0) + jnp.where(counts >= 512.0, 256.0, 0.0)
    r.sums[:, W:] = (high + pltpu.roll(counts - high, 8, 1))[:SENT].astype(BF16)

    pl.semaphore_wait(barrier, 2 * S - 1)
    scatter(r.sums, r.rs, s, h)
    send("ids", r.v_ids.at[h], r.v_ids.at[h], x_dev)
    loads["wo"].wait()
    wo_mine = pl.ds(pl.multiple_of(core * (W // 2), 16), W // 2)
    send("wo", r.v_wo.at[h, wo_mine], r.v_wo.at[h, wo_mine], x_dev)
    wq_mine = pl.ds(pl.multiple_of(core * W, 16), W)
    send("wq", r.v_wq.at[h, wq_mine], r.v_wq.at[h, wq_mine], x_dev)
    sib_half = pl.ds(pl.multiple_of((1 - core) * W, 128), W)
    own_half = pl.ds(pl.multiple_of(core * W, 128), W)
    loads["cot"].wait()
    send("cot", r.v_cot.at[0], r.v_cot.at[1], sib_dev)
    send("nrm", r.nrm.at[:, sib_half], r.nrm_sib, sib_dev)
    send("ids_sib", r.v_ids.at[h], r.ids_sib, sib_dev)

    loads["wk"].wait()
    project(r.v_wk[...], r.k)
    loads["wv"].wait()
    project(r.v_wv[...], r.v)
    loads["wout"].wait()

    def d_act(j):
        cols = aligned(j * 256, 256)
        r.dact[:, cols] = mm_nt(r.v_cot[0], r.v_wout[cols, :])

    loop(F // 256, d_act)
    if ring:
        arrive("nrm")
        arrive("ids_sib")
        onehot_t(r.ids_sib[...], r.oht_sib)
        nrm_t, nrm_sib_t = r.nrm[:, own_half].T, r.nrm_sib[...].T
        for p in range(pairs):
            tile = mm_nt(nrm_t, r.oht[h, pair_rows(p), :]) + mm_nt(nrm_sib_t, r.oht_sib[pair_rows(p), :])
            r.part_n[:, pair_rows(p)] = tile.astype(BF16)

    @pl.when(is_owner)
    def _():
        gathered_at_owner(r.rs, S, W + 128, 0)
        total = total_of(r.rs, S, W + 128)
        counts = total[:, W:]
        divisor = jnp.maximum(expand(counts + pltpu.roll(counts, 120, 1)), 1.0)
        r.divisor[...] = divisor
        r.ag1[aligned(group * GROUP, GROUP), :] = (total[:, :W] / divisor).astype(BF16)
        spread(r.ag1, 0, r.rs)

    if ring:
        add_stream("n", r.part_n, lambda at, size: r.fin_n, r.ring_n, shared=False, last=ahead)
    arrive("ids")
    onehot(oh)
    arrive("wo")
    send("wo_sib", r.v_wo.at[oh, wo_mine], r.v_wo.at[oh, wo_mine], sib_dev)
    loads["masked"].wait()
    positions = s * T + lax.broadcasted_iota(jnp.int32, (1, T), 1)

    def mark(i, hits):
        keys = r.v_masked[aligned(i * 8, 8), :].T
        for j in range(8):
            found = jnp.where(keys[:, j : j + 1] == positions, 1.0, 0.0)
            hits = jnp.maximum(hits, jnp.max(found.reshape(16, 8, T), axis=0))
        return hits

    hits = lax.fori_loop(0, cfg.M // 1024, mark, jnp.zeros((8, T), F32))
    keep = 1.0 - jnp.max(hits, axis=0, keepdims=True)
    spread_arrive(r.ag1, 0)

    stats = jnp.zeros((SLOT, 128), F32)
    sent_stats = jnp.zeros((SLOT, 128), F32)
    for p in range(pairs):
        scores = mm_nt(unfold(r.ag1[:, pair(p)]), r.k[:, pair(p)]) * scale
        scores = jnp.where(keep > 0, scores, -1e30)
        high, low = split(jnp.max(scores, axis=1, keepdims=True))
        low = low.astype(BF16).astype(F32)
        top = high + low
        weights = jnp.where(keep > 0, jnp.exp(scores - top), 0.0)
        r.e[pair_rows(p), :] = weights
        total_high, total_low = split(jnp.sum(weights, axis=1, keepdims=True))
        r.numer[:, pair(p)] = fold(mm(weights.astype(BF16), r.v[:, pair(p)]))[:SENT].astype(BF16)
        stats = stats + place(top, p)
        sent_stats = sent_stats + place(high, p) + place(low, p, 8) + place(total_high, p, 16) + place(total_low, p, 24)
    r.stats[...] = stats
    r.numer[:, W:] = sent_stats[:SENT].astype(BF16)
    scatter(r.numer, r.rs, s, h)
    tick("n")

    @pl.when(is_owner)
    def _():
        gathered_at_owner(r.rs, S, W + 128, 1)

        used = lanes < LH

        def stats_of(i):
            theirs = r.rs[aligned(i * 16, 16), :, W:].astype(F32).reshape(16 * GROUP, 128)
            return theirs, (theirs + pltpu.roll(theirs, 120, 1)).reshape(16, GROUP, 128)

        def highest(i, acc):
            return jnp.maximum(acc, jnp.max(stats_of(i)[1], axis=0))

        top = lax.fori_loop(0, S // 16, highest, jnp.full((GROUP, 128), -3e38, F32))

        def add(i, carry):
            numer, total = carry
            theirs, tops = stats_of(i)
            weight = jnp.where(used, jnp.exp(tops - top), 0.0).reshape(16 * GROUP, 128)
            totals = weight * (pltpu.roll(theirs, 112, 1) + pltpu.roll(theirs, 104, 1))
            part = expand(weight) * r.rs[aligned(i * 16, 16), :, :W].astype(F32).reshape(16 * GROUP, W)
            return (
                numer + jnp.sum(part.reshape(16, GROUP, W), axis=0),
                total + jnp.sum(totals.reshape(16, GROUP, 128), axis=0),
            )

        numer, total = lax.fori_loop(
            0, S // 16, add, (jnp.zeros((GROUP, W), F32), jnp.zeros((GROUP, 128), F32))
        )
        total = jnp.where(used, total, 1.0)
        out = numer / expand(total)
        r.own_out[...] = out
        r.own_lse[...] = jnp.where(used, top + jnp.log(total), 0.0)
        r.ag2[h, aligned(group * GROUP, GROUP), :] = out.astype(BF16)
        spread(r.ag2.at[h], 1, r.rs)

    for name in ["win", "g2", "b2"]:
        loads[name].wait()
    arrive("wo_sib")
    arrive("wq")
    send("wq_sib", r.v_wq.at[oh, wq_mine], r.v_wq.at[oh, wq_mine], sib_dev)
    tick("n")
    spread_pass(r.ag2, 1, 0)
    pass_arrive(r.ag2, 0)

    for x in range(2):
        for p in range(pairs):
            r.gat[x, :, pair(p)] = mm(r.oh[x, :, pair_rows(p)], unfold(r.ag2[x, :, pair(p)])).astype(BF16)

    def second_norm(i):
        rows = aligned(i * 128, 128)
        attn = mm(r.gat[0, rows, :], r.v_wo[0]) + mm(r.gat[1, rows, :], r.v_wo[1])
        resid = r.v_tok[rows, :].astype(F32) + attn
        r.resid[rows, :] = resid
        scaled, _ = normalize(resid)
        r.n2[0, rows, :] = (scaled * gain(r.v_g2) + gain(r.v_b2)).astype(BF16)

    loop(T // 128, second_norm)
    tick("n")
    send("n2", r.n2.at[0], r.n2.at[1], sib_dev)
    send("gat", r.gat.at[h], r.gat_sib, sib_dev)

    def feed_forward(base):
        rows = aligned(base, half)

        def tile(j):
            cols = aligned(j * 256, 256)
            up = mm(r.n2[0, rows, :], r.v_win[:, cols])
            bell = jnp.exp(up * up * -0.5)
            share = normal_share(up, bell)
            density = bell * 0.3989422804014327
            r.act[rows, cols] = (up * share).astype(BF16)
            r.dup[rows, cols] = (r.dact[rows, cols] * (share + up * density)).astype(BF16)

        loop(F // 256, tile)

    def d_normed2(base, out):
        rows = aligned(base, half)

        def tile(j):
            cols = aligned(j * 256, 256)
            out[:, cols] = mm_nt(r.dup[rows, :], r.v_win[cols, :]).astype(out.dtype)

        loop(D // 256, tile)

    sib_units = pl.ds(pl.multiple_of((1 - core) * (F // 2), 128), F // 2)
    own_units = pl.ds(pl.multiple_of(core * (F // 2), 128), F // 2)
    feed_forward(oh * half)
    feed_forward(h * half)
    send("act", r.act.at[:, sib_units], r.act_sib, sib_dev)
    d_normed2(oh * half, r.dn_send)
    send("dn", r.dn_send, r.dn_recv, x_dev)
    send("dup", r.dup.at[:, sib_units], r.dup_sib, sib_dev)
    tick("n")

    arrive("act")
    arrive("cot")

    def grad_out(j):
        cols = pl.ds(pl.multiple_of(core * (F // 2) + j * 256, 128), 256)
        tile = mm_tn(r.act[:, cols], r.v_cot[0]) + mm_tn(r.act_sib[:, aligned(j * 256, 256)], r.v_cot[1])
        r.part_out[aligned(j * 256, 256), :] = tile.astype(BF16)

    loop(F // 2 // 256, grad_out)
    for k in range(2):
        base = k * (D // 2)
        add_stream(
            f"out{k}", r.part_out.at[pl.ds(base, D // 2)], rows_of(r.fin_out, core * (F // 2) + base), ring and r.ring_wide.at[k]
        )
    tick("n")
    arrive("dup")
    arrive("n2")

    def grad_in(j):
        cols = aligned(j * 256, 256)
        tile = mm_tn(r.n2[0, :, cols], r.dup[:, own_units]) + mm_tn(r.n2[1, :, cols], r.dup_sib[...])
        r.part_in[cols, :] = tile.astype(BF16)

    loop(D // 256, grad_in)

    for k in range(2):
        base = k * (D // 2)
        add_stream(
            f"in{k}", r.part_in.at[pl.ds(base, D // 2)], rows_of(r.fin_in, base, own_units), ring and r.ring_wide.at[2 + k]
        )

    def ffn_part(j):
        cols = aligned(j * 256, 256)
        r.fp[h, :, cols] = mm(r.act[...], r.v_wout[:, cols]).astype(BF16)

    d_normed2(h * half, r.dn_own)
    loop(D // 256, ffn_part)
    tick("n", "out0", "out1", "in0", "in1")

    arrive("dn")

    def second_norm_back(i, carry):
        gain_sum, shift_sum = carry
        rows = pl.ds(pl.multiple_of(h * half + i * 64, 64), 64)
        at = aligned(i * 64, 64)
        scaled, inverse = normalize(r.resid[rows, :])
        grad = r.dn_own[at, :] + r.dn_recv[at, :].astype(F32)
        d_resid = r.v_cot[0, rows, :].astype(F32) + normalize_back(grad, gain(r.v_g2), scaled, inverse)
        r.dres[at, :] = d_resid
        r.dat[rows, :] = d_resid.astype(BF16)
        return gain_sum + fold_rows(grad * scaled), shift_sum + fold_rows(grad)

    zero = jnp.zeros((8, D), F32)
    gain_sum, shift_sum = lax.fori_loop(0, half // 64, second_norm_back, (zero, zero))
    r.norm_grads[2:3, :] = jnp.sum(gain_sum, axis=0, keepdims=True)
    r.norm_grads[3:4, :] = jnp.sum(shift_sum, axis=0, keepdims=True)
    own_rows = aligned(h * half, half)
    other_rows = aligned(oh * half, half)
    for x in range(2):
        d_gathered = mm_nt(r.dat[own_rows, :], r.v_wo[x]).astype(BF16)
        for p in range(pairs):
            hot = r.oht[x, pair_rows(p), own_rows]
            r.dc[x, :, pair(p)] = fold(mm(hot, d_gathered[:, pair(p)]))[:SENT].astype(BF16)
    for x in range(2):
        scatter(r.dc.at[x], r.rs, me, x)
    send("dat", r.dat.at[own_rows], r.dat.at[own_rows], x_dev)

    send("fp_0", r.fp.at[h, own_rows], r.fp.at[h, own_rows], x_dev)
    tick("n", "out0", "out1")

    @pl.when(is_owner)
    def _():
        gathered_at_owner(r.rs, 2 * S, W, 2)
        rows = aligned(group * GROUP, GROUP)
        d_cluster = total_of(r.rs, 2 * S, W).astype(BF16)
        r.ag3[rows, :] = d_cluster
        spread(r.ag3, 2, r.rs)
        product = d_cluster.astype(F32) * r.own_out[...]
        delta = pltpu.roll(r.own_lse[...], 8, 1)
        for p in range(pairs):
            block = product[:, pair(p)]
            delta = delta + jnp.where(
                lanes == 2 * p, jnp.sum(jnp.where(left, block, 0.0), axis=1, keepdims=True), 0.0
            )
            delta = delta + jnp.where(
                lanes == 2 * p + 1, jnp.sum(jnp.where(left, 0.0, block), axis=1, keepdims=True), 0.0
            )
        r.agdelta[rows, :] = delta
        spread(r.agdelta, 3, r.like)

    tick("in0", "in1")
    spread_arrive(r.ag3, 2)
    spread_arrive(r.agdelta, 3)

    for p in range(pairs):
        d_probs = mm_nt(unfold(r.ag3[:, pair(p)]), r.v[:, pair(p)])
        factor = jnp.exp(column(r.stats[...], p) - column(r.agdelta[...], p, 8))
        probs = r.e[pair_rows(p), :] * factor
        r.pb[pair_rows(p), :] = probs.astype(BF16)
        d_scores = (probs * (d_probs - column(r.agdelta[...], p))).astype(BF16)
        r.dsb[pair_rows(p), :] = d_scores
        r.dcen[:, pair(p)] = fold(mm(d_scores, r.k[:, pair(p)]))[:SENT].astype(BF16)
    scatter(r.dcen, r.rs, s, h)

    for p in range(pairs):
        r.dkv[0, :, pair(p)] = (mm_tn(r.dsb[pair_rows(p), :], unfold(r.ag1[:, pair(p)])) * scale).astype(BF16)
        r.dkv[1, :, pair(p)] = mm_tn(r.pb[pair_rows(p), :], unfold(r.ag3[:, pair(p)])).astype(BF16)
    send("dkv", r.dkv, r.dkv_sib, sib_dev)

    def kv_part(rows):
        return mm_nt(r.dkv[0, rows, :], r.v_wk[...]) + mm_nt(r.dkv[1, rows, :], r.v_wv[...])

    r.kv_send[...] = kv_part(other_rows).astype(BF16)
    send("kv", r.kv_send, r.kv_recv, x_dev)
    arrive("dat")
    send("dat_sib", r.dat.at[:, sib_half], r.dat_sib, sib_dev)
    tick("n", "out0", "out1")

    @pl.when(is_owner)
    def _():
        gathered_at_owner(r.rs, S, W, 3)
        rows = aligned(group * GROUP, GROUP)
        r.ag4[h, rows, :] = (total_of(r.rs, S, W) * scale / r.divisor[...]).astype(BF16)
        spread(r.ag4.at[h], 4, r.rs)

    tick("in0", "in1")
    arrive("dkv")
    if not ring:
        arrive("nrm")
    for i, name in enumerate(["k", "v"]):
        tile = mm_tn(r.nrm[:, own_half], r.dkv[i]) + mm_tn(r.nrm_sib[...], r.dkv_sib[i])
        r.part_small[i] = tile.astype(BF16)
        add_stream(name, r.part_small.at[i], rows_of(getattr(r, "fin_" + name), core * W), ring and r.ring_slim.at[i])
    tick("out0", "out1")
    arrive("gat")
    arrive("dat_sib")
    r.part_small[2] = (mm_tn(r.gat[h], r.dat[:, own_half]) + mm_tn(r.gat_sib[...], r.dat_sib[...])).astype(BF16)
    add_stream("o", r.part_small.at[2], rows_of(r.fin_o, 0, own_half), ring and r.ring_slim.at[2])
    r.kv_own[...] = kv_part(own_rows)
    tick("out0", "out1", "in0", "in1", "k", "v")

    spread_pass(r.ag4, 4, 1)
    if ring:
        while "n" in pending():
            tick("n")
        size = W // n
        rows = pl.ds(pl.multiple_of(core * W + position * size, 16), size)
        for p in range(pairs):
            r.fin_q[rows, pair(p)] = mm(r.fin_n[:, pair_rows(p)], unfold(r.ag4[h, :, pair(p)])).astype(BF16)
        add_stream("q", r.fin_q.at[pl.ds(0, W)], rows_of(r.fin_q, core * W), None, at=ahead)
    else:
        for p in range(pairs):
            r.dq_all[:, pair(p)] = mm(r.oh[h, :, pair_rows(p)], unfold(r.ag4[h, :, pair(p)])).astype(BF16)
        send("dq", r.dq_all, r.dq_sib, sib_dev)
        arrive("dq")
        r.part_q[...] = (mm_tn(r.nrm[:, own_half], r.dq_all[...]) + mm_tn(r.nrm_sib[...], r.dq_sib[...])).astype(BF16)
        add_stream("q", r.part_q, rows_of(r.fin_q, core * W), None)
    pass_arrive(r.ag4, 1)
    for x in range(2):
        for p in range(pairs):
            r.dq[x, :, pair(p)] = mm(r.oh[x, own_rows, pair_rows(p)], unfold(r.ag4[x, :, pair(p)])).astype(BF16)

    arrive("kv")
    arrive("wq_sib")
    r.kv_own[...] += r.kv_recv[...].astype(F32) + mm_nt(r.dq[0], r.v_wq[0]) + mm_nt(r.dq[1], r.v_wq[1])

    def first_norm_back(i, carry):
        gain_sum, shift_sum = carry
        rows = pl.ds(pl.multiple_of(h * half + i * 64, 64), 64)
        at = aligned(i * 64, 64)
        scaled, inverse = normalize(r.v_tok[rows, :].astype(F32))
        grad = r.kv_own[at, :]
        grad_tokens = r.dres[at, :] + normalize_back(grad, gain(r.v_g1), scaled, inverse)
        r.gtok[rows, :] = grad_tokens.astype(BF16)
        return gain_sum + fold_rows(grad * scaled), shift_sum + fold_rows(grad)

    gain_sum, shift_sum = lax.fori_loop(0, half // 64, first_norm_back, (zero, zero))
    r.norm_grads[0:1, :] = jnp.sum(gain_sum, axis=0, keepdims=True)
    r.norm_grads[1:2, :] = jnp.sum(shift_sum, axis=0, keepdims=True)
    blocks = D // 128

    def norm_to(g, plane):
        cols = pl.ds(g * 128, 128)
        mine = jnp.logical_and(s == first + g, h == plane)
        copy = remote(
            r.norm_grads.at[:, cols], r.norm_rs.at[me], r.norm_send.at[g, plane], r.norm_sem.at[0], (first + g, plane)
        )
        return cols, mine, copy

    for plane in range(2):
        for g in range(blocks):
            cols, mine, copy = norm_to(g, plane)

            @pl.when(jnp.logical_not(mine))
            def _():
                copy.start()

            @pl.when(mine)
            def _():
                r.norm_rs[me] = r.norm_grads[:, cols]

    send("gtok", r.gtok.at[own_rows], r.gtok.at[own_rows], x_dev)
    send("fp_1", r.fp.at[h, other_rows], r.fp.at[h, other_rows], x_dev)
    tick(*pending())
    norm_owner = jnp.logical_and(s >= first, s < first + blocks)

    @pl.when(norm_owner)
    def _():
        block = r.norm_rs.at[pl.ds(0, 2 * S - 1)]
        remote(block, block, r.norm_send.at[0, 0], r.norm_sem.at[0], x_dev).wait_recv()

        def add(i, acc):
            return acc + r.norm_rs[i]

        cols = aligned(group * 128, 128)
        r.norm_fin[:, cols] = lax.fori_loop(0, 2 * S, add, jnp.zeros((8, 128), F32))
        block = r.norm_fin.at[:, cols]

        def to(k):
            remote(block, block, r.norm_send.at[blocks, 0], r.norm_sem.at[1 + group], (lax.rem(s + k + 1, S), h)).start()

        loop(S - 1, to)

    tick(*pending())
    for g in range(blocks):
        block = r.norm_fin.at[:, pl.ds(g * 128, 128)]

        @pl.when(s != first + g)
        def _():
            remote(block, block, r.norm_send.at[0, 0], r.norm_sem.at[1 + g], x_dev).wait_recv()

    store("norm_fin")
    while pending():
        tick(*pending())
    arrive("gtok")
    store("gtok")

    arrive("fp_0")
    arrive("fp_1")

    def block_out(i):
        rows = aligned(i * 64, 64)
        r.bout[rows, :] = (r.resid[rows, :] + r.fp[0, rows, :].astype(F32) + r.fp[1, rows, :].astype(F32)).astype(BF16)

    loop(T // 64, block_out)
    store("bout")
    for st in streams:
        if st.shared:
            arrive(f"ring{st.i}")

    for name in ["fin_in", "fin_out"]:
        store(name)
    for name in ["fin_q", "fin_k", "fin_v", "fin_o"]:
        store(name)
    for finish in at_end:
        finish()
    for plane in range(2):
        for g in range(blocks):
            cols, mine, copy = norm_to(g, plane)

            @pl.when(jnp.logical_not(mine))
            def _():
                copy.wait_send()

    @pl.when(norm_owner)
    def _():
        block = r.norm_rs.at[pl.ds(0, S - 1)]
        remote(block, block, r.norm_send.at[blocks, 0], r.norm_sem.at[0], x_dev).wait_send()

    for copy in stores:
        copy.wait()


def per_device(
    S,
    tokens,
    norm1_gain,
    norm1_shift,
    w_query,
    w_key,
    w_value,
    w_output,
    norm2_gain,
    norm2_shift,
    w_in,
    w_out,
    cluster_ids,
    masked_keys,
    cotangent,
):
    T, D = tokens.shape
    LH = cluster_ids.shape[1]
    W = w_query.shape[1]
    F = w_in.shape[1]
    n = S // 2
    ring = n <= 8
    cfg = SimpleNamespace(S=S, T=T, D=D, W=W, LH=LH, F=F, ring=ring, scatter_of=[0, 1, 2, 2, 3])

    M = -(-masked_keys.shape[0] // 1024) * 1024
    if M != masked_keys.shape[0]:
        masked_keys = jnp.pad(masked_keys, (0, M - masked_keys.shape[0]), constant_values=-1)
    cfg.M = M
    inputs = dict(
        tok=tokens,
        g1=norm1_gain,
        b1=norm1_shift,
        wq=w_query,
        wk=w_key,
        wv=w_value,
        wo=w_output,
        g2=norm2_gain,
        b2=norm2_shift,
        win=w_in,
        wout=w_out,
        ids=cluster_ids.T,
        masked=masked_keys.reshape(M // 128, 128),
        cot=cotangent,
    )
    outputs = dict(
        o_block=((T, D), BF16),
        o_tokens=((T, D), BF16),
        o_norm=((8, D), F32),
        o_q=((D, W), BF16),
        o_k=((D, W), BF16),
        o_v=((D, W), BF16),
        o_o=((W, D), BF16),
        o_in=((D, F), BF16),
        o_out=((F, D), BF16),
    )
    half = T // 2
    vmem = dict(
        v_tok=((T, D), BF16),
        v_g1=((D,), F32),
        v_b1=((D,), F32),
        v_wq=((2, D, W), BF16),
        v_wk=((D, W), BF16),
        v_wv=((D, W), BF16),
        v_wo=((2, W, D), BF16),
        v_g2=((D,), F32),
        v_b2=((D,), F32),
        v_win=((D, F), BF16),
        v_wout=((F, D), BF16),
        v_ids=((2, LH, T), jnp.int32),
        v_masked=((M // 128, 128), jnp.int32),
        v_cot=((2, T, D), BF16),
        nrm=((T, D), BF16),
        nrm_sib=((T, W), BF16),
        q=((T, W), BF16),
        k=((T, W), BF16),
        v=((T, W), BF16),
        oht=((2, LH * SLOT, T), BF16),
        oh=((2, T, LH * SLOT), BF16),
        sums=((SENT, W + 128), BF16),
        rs=((2 * S, GROUP, W + 128), BF16),
        like=((S, GROUP, 128), F32),
        divisor=((GROUP, W), F32),
        ag1=((SLOT, W), BF16),
        dact=((T, F), F32),
        e=((LH * SLOT, T), F32),
        numer=((SENT, W + 128), BF16),
        stats=((SLOT, 128), F32),
        own_out=((GROUP, W), F32),
        ag2=((2, SLOT, W), BF16),
        own_lse=((GROUP, 128), F32),
        gat=((2, T, W), BF16),
        gat_sib=((T, W), BF16),
        resid=((T, D), F32),
        n2=((2, T, D), BF16),
        act=((T, F), BF16),
        dup=((T, F), BF16),
        act_sib=((T, F // 2), BF16),
        dup_sib=((T, F // 2), BF16),
        dn_send=((half, D), BF16),
        dn_recv=((half, D), BF16),
        dn_own=((half, D), F32),
        dres=((half, D), F32),
        dat=((T, D), BF16),
        dat_sib=((T, W), BF16),
        dc=((2, SENT, W), BF16),
        ag3=((SLOT, W), BF16),
        agdelta=((SLOT, 128), F32),
        pb=((LH * SLOT, T), BF16),
        dsb=((LH * SLOT, T), BF16),
        dcen=((SENT, W), BF16),
        ag4=((2, SLOT, W), BF16),
        dkv=((2, T, W), BF16),
        dkv_sib=((2, T, W), BF16),
        kv_send=((half, D), BF16),
        kv_recv=((half, D), BF16),
        kv_own=((half, D), F32),
        dq=((2, half, W), BF16),
        gtok=((T, D), BF16),
        norm_grads=((8, D), F32),
        norm_rs=((2 * S, 8, 128), F32),
        norm_fin=((8, D), F32),
        fp=((2, T, D), BF16),
        bout=((T, D), BF16),
        part_out=((F // 2, D), BF16),
        part_in=((D, F // 2), BF16),
        part_small=((3, W, W), BF16),
        ids_sib=((LH, T), jnp.int32),
        fin_out=((F, D), BF16),
        fin_in=((D, F), BF16),
        fin_k=((D, W), BF16),
        fin_v=((D, W), BF16),
        fin_q=((D, W), BF16),
        fin_o=((W, D), BF16),
    )
    steps = 2 * (n - 1) if ring else 1
    if ring:
        vmem["ring_wide"] = ((4, n - 1, D // 2 // n, D), BF16)
        vmem["ring_slim"] = ((3, n - 1, W // n, W), BF16)
        vmem["ring_n"] = ((n - 1, W // n, LH * SLOT), BF16)
        vmem["oht_sib"] = ((LH * SLOT, T), BF16)
        vmem["part_n"] = ((W, LH * SLOT), BF16)
        vmem["fin_n"] = ((W // n, LH * SLOT), BF16)
    else:
        vmem["dq_all"] = ((T, W), BF16)
        vmem["dq_sib"] = ((T, W), BF16)
        vmem["part_q"] = ((W, W), BF16)
    sems = dict(
        load_sem=(14,),
        store_sem=(9,),
        ex_send=(32,),
        ex_recv=(32,),
        sc_send=(5, GROUPS),
        sc_recv=(4,),
        sp_send=(5,),
        sp_recv=(5, GROUPS),
        pass_send=(2, GROUPS),
        pass_recv=(2, GROUPS),
        ring_send=(STREAMS, steps),
        ring_recv=(STREAMS, steps),
        norm_send=(D // 128 + 1, 2),
        norm_sem=(D // 128 + 1,),
    )
    names = list(inputs) + list(outputs) + list(vmem) + list(sems)
    results = pl.pallas_call(
        functools.partial(kernel, cfg, names),
        out_shape=[jax.ShapeDtypeStruct(*o) for o in outputs.values()],
        in_specs=[pl.BlockSpec(memory_space=pl.ANY)] * len(inputs),
        out_specs=[pl.BlockSpec(memory_space=pl.ANY)] * len(outputs),
        scratch_shapes=[pltpu.VMEM(*b) for b in vmem.values()] + [pltpu.SemaphoreType.DMA(b) for b in sems.values()],
        compiler_params=pltpu.CompilerParams(collective_id=0, has_side_effects=True, vmem_limit_bytes=cfg_vmem()),
        name="block",
    )(*inputs.values())
    block, grad_tokens, norms, *grads = results
    if not ring:
        grads = lax.psum(grads, "seq")
    block, gain1, shift1, gain2, shift2, grad_tokens, *grads = widen(block, norms, [grad_tokens] + grads)
    grad_q, grad_k, grad_v, grad_o, grad_in, grad_out = grads
    return (
        block,
        grad_tokens,
        gain1,
        shift1,
        grad_q,
        grad_k,
        grad_v,
        grad_o,
        gain2,
        shift2,
        grad_in,
        grad_out,
    )


def widen(block, norms, arrays):
    D = norms.shape[1]
    tiles = [
        (i, k * size, size)
        for i, a in enumerate(arrays)
        for size in [a.shape[0] // max(2, a.shape[0] // 256)]
        for k in range(a.shape[0] // size)
    ]
    count = len(arrays)

    def kernel(*refs):
        block_in, norms_in, *rest = refs
        ins, rest = rest[:count], rest[count:]
        block_out, *rest = rest
        norm_outs, rest = rest[:4], rest[4:]
        outs, rest = rest[:count], rest[count:]
        block_tmp, norms_tmp, *rest = rest
        flat, rest = rest[:4], rest[4:]
        narrow, rest = rest[:count], rest[count:]
        wide, rest = rest[:count], rest[count:]
        sem_in, sem_out, sem = rest
        first = pltpu.make_async_copy(block_in, block_tmp, sem.at[0])
        first_norms = pltpu.make_async_copy(norms_in, norms_tmp, sem.at[1])
        loads = [
            pltpu.make_async_copy(ins[i].at[pl.ds(at, size)], narrow[i].at[pl.ds(at, size)], sem_in.at[k])
            for k, (i, at, size) in enumerate(tiles)
        ]
        for load in loads:
            load.start()
        first_norms.start()
        first.start()
        stores = []
        for k, (i, at, size) in enumerate(tiles):
            loads[k].wait()

            def cast(j, i=i, at=at):
                rows = pl.ds(pl.multiple_of(at + j * 32, 32), 32)
                wide[i][rows, :] = narrow[i][rows, :].astype(F32)

            loop(size // 32, cast)
            rows = pl.ds(at, size)
            stores.append(pltpu.make_async_copy(wide[i].at[rows], outs[i].at[rows], sem_out.at[k]))
            stores[-1].start()
        first_norms.wait()
        for k in range(4):
            flat[k][...] = norms_tmp[k, :]
            stores.append(pltpu.make_async_copy(flat[k], norm_outs[k], sem.at[2 + k]))
            stores[-1].start()
        first.wait()
        stores.append(pltpu.make_async_copy(block_tmp, block_out, sem.at[6]))
        stores[-1].start()
        for store in stores:
            store.wait()

    out_shape = [jax.ShapeDtypeStruct(block.shape, block.dtype)]
    out_shape += [jax.ShapeDtypeStruct((D,), F32)] * 4
    out_shape += [jax.ShapeDtypeStruct(a.shape, F32) for a in arrays]
    anywhere = pl.BlockSpec(memory_space=pl.ANY)
    return pl.pallas_call(
        kernel,
        out_shape=out_shape,
        in_specs=[anywhere] * (count + 2),
        out_specs=[anywhere] * len(out_shape),
        scratch_shapes=[pltpu.VMEM(block.shape, block.dtype), pltpu.VMEM(norms.shape, F32)]
        + [pltpu.VMEM((D,), F32)] * 4
        + [pltpu.VMEM(a.shape, a.dtype) for a in arrays]
        + [pltpu.VMEM(a.shape, F32) for a in arrays]
        + [pltpu.SemaphoreType.DMA((len(tiles),)), pltpu.SemaphoreType.DMA((len(tiles),)), pltpu.SemaphoreType.DMA((7,))],
        compiler_params=pltpu.CompilerParams(vmem_limit_bytes=cfg_vmem()),
        name="widen",
    )(block, norms, *arrays)


def cfg_vmem():
    return 62 * 2**20


def solution(mesh):
    columns, rows = P(None, "head"), P("head", None)
    by_token = P("seq", None)
    return jax.shard_map(
        functools.partial(per_device, mesh.shape["seq"]),
        mesh=mesh,
        in_specs=(by_token, P(), P(), columns, columns, columns, rows, P(), P(), columns, rows, P("seq", "head"), P(), by_token),
        out_specs=(by_token, by_token, P(), P(), columns, columns, columns, rows, P(), P(), columns, rows),
        check_vma=False,
    )
```

```python
import functools
from types import SimpleNamespace

import jax
import jax.numpy as jnp
from jax import lax
from jax.experimental import pallas as pl
from jax.experimental.pallas import tpu as pltpu
from jax.sharding import PartitionSpec as P

CLUSTERS = 100
EPSILON = 1e-05
MESH = pl.DeviceIdType.MESH
F32 = jnp.float32
BF16 = jnp.bfloat16
SLOT = 128
GROUP = 16
GROUPS = -(-CLUSTERS // GROUP)
SENT = GROUPS * GROUP
STREAMS = 9


def mm(a, b):
    return lax.dot_general(a, b, (((1,), (0,)), ((), ())), preferred_element_type=F32)


def mm_nt(a, b):
    return lax.dot_general(a, b, (((1,), (1,)), ((), ())), preferred_element_type=F32)


def mm_tn(a, b):
    return lax.dot_general(a, b, (((0,), (0,)), ((), ())), preferred_element_type=F32)


def aligned(index, size):
    return pl.ds(pl.multiple_of(index, size), size)


def remote(src, dst, send_sem, recv_sem, device):
    return pltpu.make_async_remote_copy(
        src_ref=src, dst_ref=dst, send_sem=send_sem, recv_sem=recv_sem, device_id=device, device_id_type=MESH
    )


def loop(count, body):
    def step(i, carry):
        body(i)
        return carry

    lax.fori_loop(0, count, step, 0)


def normalize(values):
    centred = values - jnp.mean(values, axis=-1, keepdims=True)
    inverse = lax.rsqrt(jnp.mean(centred * centred, axis=-1, keepdims=True) + EPSILON)
    return centred * inverse, inverse


def normalize_back(grad, gain, scaled, inverse):
    inner = grad * gain
    return inverse * (
        inner - jnp.mean(inner, axis=-1, keepdims=True) - scaled * jnp.mean(inner * scaled, axis=-1, keepdims=True)
    )


ERFC = (
    0.27643095583919713,
    0.2770312983463117,
    0.2368366418089808,
    0.21634403047784398,
    -0.05751923336137985,
    0.34364725799951945,
    -0.5200124379554546,
    0.2829391760305868,
    -0.05569765451595309,
)


def normal_share(x, bell):
    t = 1.0 / (1.0 + (0.49 * 0.5**0.5) * jnp.abs(x))
    series = 0.5 * ERFC[-1]
    for factor in ERFC[-2::-1]:
        series = series * t + 0.5 * factor
    tail = series * t * bell
    return jnp.where(x < 0, tail, 1.0 - tail)


def fold_rows(values):
    return jnp.sum(values.reshape(values.shape[0] // 8, 8, values.shape[1]), axis=0)


def kernel(cfg, names, *all_refs):
    r = SimpleNamespace(**dict(zip(names, all_refs)))
    r.bout, r.gtok, r.norm_fin = r.o_block, r.o_tokens, r.o_norm
    r.fin_q, r.fin_k, r.fin_v, r.fin_o, r.fin_in, r.fin_out = r.o_q, r.o_k, r.o_v, r.o_o, r.o_in, r.o_out
    S, T, D, W, LH, F = cfg.S, cfg.T, cfg.D, cfg.W, cfg.LH, cfg.F
    pairs = LH // 2
    half = T // 2
    scale = (W // LH) ** (-0.5)
    ring = cfg.ring
    n = S // 2
    s = lax.axis_index("seq")
    h = lax.axis_index("head")
    oh = 1 - h
    core = lax.rem(s, 2)
    chip = lax.div(s, 2)
    me = s * 2 + h
    x_dev = (s, oh)
    sib_dev = (s + 1 - 2 * core, h)
    first = S // 4
    is_owner = jnp.logical_and(s >= first, s < first + GROUPS)
    group = s - first
    lanes = lax.broadcasted_iota(jnp.int32, (1, 128), 1)
    left = lanes < 64

    def fold(block):
        return jnp.where(left, block[:SLOT], block[SLOT:])

    def unfold(block):
        zero = jnp.zeros_like(block)
        return jnp.concatenate([jnp.where(left, block, zero), jnp.where(left, zero, block)], axis=0)

    def expand(stats):
        return jnp.concatenate(
            [jnp.where(left, stats[:, 2 * p : 2 * p + 1], stats[:, 2 * p + 1 : 2 * p + 2]) for p in range(pairs)], axis=1
        )

    def column(stats, p, at=0):
        return jnp.concatenate(
            [stats[:, at + 2 * p : at + 2 * p + 1], stats[:, at + 2 * p + 1 : at + 2 * p + 2]], axis=0
        )

    def place(columns, p, at=0):
        rows = columns.shape[0] // 2
        return jnp.where(lanes == at + 2 * p, columns[:rows], 0.0) + jnp.where(
            lanes == at + 2 * p + 1, columns[rows:], 0.0
        )

    def pair(p):
        return slice(p * 128, (p + 1) * 128)

    def pair_rows(p):
        return slice(p * 2 * SLOT, (p + 1) * 2 * SLOT)

    at_end = []

    loads = {}
    for i, name in enumerate(
        ["ids", "tok", "g1", "b1", "wq", "wo", "wk", "wv", "cot", "wout", "masked", "win", "g2", "b2"]
    ):
        dst = getattr(r, "v_" + name)
        dst = {"cot": lambda d: d.at[0], "wq": lambda d: d.at[h], "wo": lambda d: d.at[h], "ids": lambda d: d.at[h]}.get(
            name, lambda d: d
        )(dst)
        loads[name] = pltpu.make_async_copy(getattr(r, name), dst, r.load_sem.at[i])

    barrier = pltpu.get_barrier_semaphore()

    def greet(k):
        other = lax.rem(me + k + 1, 2 * S)
        pl.semaphore_signal(
            barrier, inc=1, device_id=(lax.div(other, 2), lax.rem(other, 2)), device_id_type=MESH
        )

    loop(2 * S - 1, greet)
    for load in loads.values():
        load.start()

    exchanges = {}

    def send(name, src, dst, device):
        i = len(exchanges)
        copy = remote(src, dst, r.ex_send.at[i], r.ex_recv.at[i], device)
        copy.start()
        exchanges[name] = copy
        at_end.append(copy.wait_send)

    def arrive(name):
        exchanges[name].wait_recv()

    counters = {"scatter": 0, "spread": 0}

    def scatter(src, dst, slot, plane):
        i = counters["scatter"]
        counters["scatter"] += 1

        def at(g):
            rows = pl.ds(g * GROUP, GROUP)
            mine = jnp.logical_and(s == first + g, h == plane)
            copy = remote(
                src.at[rows], dst.at[slot, :, cols], r.sc_send.at[i, g], r.sc_recv.at[cfg.scatter_of[i]], (first + g, plane)
            )
            return rows, mine, copy

        cols = pl.ds(0, src.shape[1])

        for g in range(GROUPS):
            rows, mine, copy = at(g)

            @pl.when(jnp.logical_not(mine))
            def _():
                copy.start()

            @pl.when(mine)
            def _():
                dst[slot, :, cols] = src[rows, :]

        def finish():
            for g in range(GROUPS):
                rows, mine, copy = at(g)

                @pl.when(jnp.logical_not(mine))
                def _():
                    copy.wait_send()

        at_end.append(finish)

    def gathered_at_owner(buf, count, width, i):
        block = buf.at[pl.ds(0, count - 1), :, pl.ds(0, width)]
        remote(block, block, r.sc_send.at[0, 0], r.sc_recv.at[i], x_dev).wait_recv()

    def spread(buf, i, width):
        rows = aligned(group * GROUP, GROUP)
        block = buf.at[rows]

        def to(k):
            copy = remote(block, block, r.sp_send.at[i], r.sp_recv.at[i, group], (lax.rem(s + k + 1, S), h))
            copy.start()

        loop(S - 1, to)

        def finish():
            @pl.when(is_owner)
            def _():
                block = r.rs.at[pl.ds(0, S - 1), :, pl.ds(0, width)]
                remote(block, block, r.sp_send.at[i], r.sp_recv.at[i, 0], x_dev).wait_send()

        at_end.append(finish)

    def spread_arrive(buf, i):
        for g in range(GROUPS):

            @pl.when(s != first + g)
            def _():
                block = buf.at[pl.ds(g * GROUP, GROUP)]
                remote(block, block, r.sp_send.at[i], r.sp_recv.at[i, g], x_dev).wait_recv()

    def spread_pass(buf, i, j):
        for g in range(GROUPS):
            block = buf.at[h, pl.ds(g * GROUP, GROUP)]

            @pl.when(s != first + g)
            def _():
                remote(block, block, r.sp_send.at[i], r.sp_recv.at[i, g], x_dev).wait_recv()

            copy = remote(block, block, r.pass_send.at[j, g], r.pass_recv.at[j, g], x_dev)
            copy.start()
            at_end.append(copy.wait_send)

    def pass_arrive(buf, j):
        for g in range(GROUPS):
            block = buf.at[oh, pl.ds(g * GROUP, GROUP)]
            remote(block, block, r.pass_send.at[j, g], r.pass_recv.at[j, g], x_dev).wait_recv()

    def total_of(buf, count, width):
        def add(i, acc):
            return acc + jnp.sum(buf[aligned(i * 16, 16), :, :width].astype(F32), axis=0)

        return lax.fori_loop(0, count // 16, add, jnp.zeros((GROUP, width), F32))

    def split(values):
        high = values.astype(BF16).astype(F32)
        return high, values - high

    z_count = n // 2
    z, y = lax.div(chip, 2), lax.rem(chip, 2)
    position = jnp.where(y == 0, z, n - 1 - z)

    def device_at(p):
        p = lax.rem(p + n, n)
        return (2 * jnp.where(p < z_count, 2 * p, 2 * (n - 1 - p) + 1) + core, h)

    streams = []
    ahead, behind = n // 2, n - 1 - n // 2

    def add_stream(name, part, fin_block, recv, shared=True, at=0, last=2 * ahead):
        i = len(streams)
        st = SimpleNamespace(name=name, i=i, part=part, fin=fin_block, turn=at, last=last)
        st.chunk = part.shape[0] // n
        st.recv = recv
        st.shared = shared
        st.ways = [(1, ahead, 0), (-1, behind, ahead)] if i % 2 == 0 else [(-1, ahead, 0), (1, behind, ahead)]
        if ring:
            streams.append(st)
            advance(st)
        else:
            st.fin(0, part.shape[0])[...] = part[...]
        return st

    def part_chunk(st, k):
        return st.part.at[pl.ds(pl.multiple_of(lax.rem(k + 2 * n, n) * st.chunk, 16), st.chunk)]

    def fin_chunk(st, k):
        return st.fin(lax.rem(k + 2 * n, n) * st.chunk, st.chunk)

    def sum_copy(st, way, t):
        sign, hops, slot = way
        src = part_chunk(st, position + sign * hops) if t == 0 else st.recv.at[slot + t - 1]
        return remote(
            src,
            st.recv.at[slot + t],
            r.ring_send.at[st.i, slot + t],
            r.ring_recv.at[st.i, slot + t],
            device_at(position + sign),
        )

    def pass_copy(st, way, t):
        sign, hops, slot = way
        block = fin_chunk(st, position - sign * t)
        return remote(
            block,
            block,
            r.ring_send.at[st.i, n - 1 + slot + t],
            r.ring_recv.at[st.i, n - 1 + slot + t],
            device_at(position + sign),
        )

    def start(copy):
        copy.start()
        at_end.append(copy.wait_send)

    def advance(st):
        t = st.turn
        st.turn += 1
        if t <= ahead:
            for way in st.ways:
                sign, hops, slot = way
                if 0 < t <= hops and st.recv is not None:
                    sum_copy(st, way, t - 1).wait_recv()
                    if t < hops:
                        came = st.recv[slot + t - 1].astype(F32) + part_chunk(st, position + sign * (hops - t))[...].astype(F32)
                        st.recv[slot + t - 1] = came.astype(BF16)
                if t < hops:
                    start(sum_copy(st, way, t))
            if t == ahead:
                if st.recv is not None:
                    total = part_chunk(st, position)[...].astype(F32)
                    for sign, hops, slot in st.ways:
                        total = total + st.recv[slot + hops - 1].astype(F32)
                    fin_chunk(st, position)[...] = total.astype(BF16)
                for way in st.ways if st.last > ahead else []:
                    start(pass_copy(st, way, 0))
        elif t <= 2 * ahead:
            u = t - ahead
            for way in st.ways:
                sign, hops, slot = way
                if u <= hops:
                    block = fin_chunk(st, position - sign * u)
                    remote(
                        block, block, r.ring_send.at[st.i, 0], r.ring_recv.at[st.i, n - 1 + slot + u - 1], x_dev
                    ).wait_recv()
                if u < hops:
                    start(pass_copy(st, way, u))
            if u == ahead and st.shared:
                whole = st.fin(0, st.part.shape[0])
                send(f"ring{st.i}", whole, whole, sib_dev)

    def tick(*wanted):
        for name in wanted:
            for st in streams:
                if st.name == name and st.turn <= st.last:
                    advance(st)

    def pending():
        return [st.name for st in streams if st.turn <= st.last]

    if not ring:
        for name in ["fin_out", "fin_in", "fin_k", "fin_v", "fin_q", "fin_o"]:
            ref = getattr(r, name)
            ref[...] = jnp.zeros_like(ref)

    def rows_of(ref, base, cols=None):
        def block(at, size):
            rows = pl.ds(pl.multiple_of(base + at, 16), size)
            return ref.at[rows] if cols is None else ref.at[rows, cols]

        return block

    r.ag1[...] = jnp.zeros_like(r.ag1)
    r.ag3[...] = jnp.zeros_like(r.ag3)
    r.ag2[...] = jnp.zeros_like(r.ag2)
    r.ag4[...] = jnp.zeros_like(r.ag4)
    r.agdelta[...] = jnp.zeros_like(r.agdelta)
    r.norm_grads[...] = jnp.zeros_like(r.norm_grads)

    def onehot_t(ids, out):
        rows = lax.broadcasted_iota(jnp.int32, (SLOT, T), 0)
        for j in range(LH):
            out[j * SLOT : (j + 1) * SLOT, :] = jnp.where(rows == ids[j : j + 1, :], 1.0, 0.0).astype(BF16)

    def onehot(x):
        onehot_t(r.v_ids[x], r.oht.at[x])
        for p in range(pairs):
            r.oh[x, :, pair_rows(p)] = r.oht[x, pair_rows(p), :].T

    def gain(ref):
        return ref[...].reshape(1, D)

    loads["ids"].wait()
    onehot(h)
    for name in ["g1", "b1", "tok"]:
        loads[name].wait()

    def first_norm(i):
        rows = aligned(i * 64, 64)
        scaled, _ = normalize(r.v_tok[rows, :].astype(F32))
        r.nrm[rows, :] = (scaled * gain(r.v_g1) + gain(r.v_b1)).astype(BF16)

    loop(T // 64, first_norm)
    loads["wq"].wait()

    def project(weight, out):
        def tile(i):
            rows = aligned(i * 256, 256)
            out[rows, :] = mm(r.nrm[rows, :], weight).astype(BF16)

        loop(T // 256, tile)

    project(r.v_wq[h], r.q)
    counts = jnp.zeros((SLOT, 128), F32)
    ones = jnp.ones((T, 128), BF16)
    for p in range(pairs):
        hot = r.oht[h, pair_rows(p), :]
        r.sums[:, pair(p)] = fold(mm(hot, r.q[:, pair(p)]))[:SENT].astype(BF16)
        counts = counts + place(mm(hot, ones)[:, :1], p)
    high = jnp.where(counts >= 256.0, 256.0, 0.0) + jnp.where(counts >= 512.0, 256.0, 0.0)
    r.sums[:, W:] = (high + pltpu.roll(counts - high, 8, 1))[:SENT].astype(BF16)

    pl.semaphore_wait(barrier, 2 * S - 1)
    scatter(r.sums, r.rs, s, h)
    send("ids", r.v_ids.at[h], r.v_ids.at[h], x_dev)
    loads["wo"].wait()
    wo_mine = pl.ds(pl.multiple_of(core * (W // 2), 16), W // 2)
    send("wo", r.v_wo.at[h, wo_mine], r.v_wo.at[h, wo_mine], x_dev)
    wq_mine = pl.ds(pl.multiple_of(core * W, 16), W)
    send("wq", r.v_wq.at[h, wq_mine], r.v_wq.at[h, wq_mine], x_dev)
    sib_half = pl.ds(pl.multiple_of((1 - core) * W, 128), W)
    own_half = pl.ds(pl.multiple_of(core * W, 128), W)
    loads["cot"].wait()
    send("cot", r.v_cot.at[0], r.v_cot.at[1], sib_dev)
    send("nrm", r.nrm.at[:, sib_half], r.nrm_sib, sib_dev)
    send("ids_sib", r.v_ids.at[h], r.ids_sib, sib_dev)

    loads["wk"].wait()
    project(r.v_wk[...], r.k)
    loads["wv"].wait()
    project(r.v_wv[...], r.v)
    loads["wout"].wait()

    def d_act(j):
        cols = aligned(j * 256, 256)
        r.dact[:, cols] = mm_nt(r.v_cot[0], r.v_wout[cols, :])

    loop(F // 256, d_act)
    if ring:
        arrive("nrm")
        arrive("ids_sib")
        onehot_t(r.ids_sib[...], r.oht_sib)
        nrm_t, nrm_sib_t = r.nrm[:, own_half].T, r.nrm_sib[...].T
        for p in range(pairs):
            tile = mm_nt(nrm_t, r.oht[h, pair_rows(p), :]) + mm_nt(nrm_sib_t, r.oht_sib[pair_rows(p), :])
            r.part_n[:, pair_rows(p)] = tile.astype(BF16)

    @pl.when(is_owner)
    def _():
        gathered_at_owner(r.rs, S, W + 128, 0)
        total = total_of(r.rs, S, W + 128)
        counts = total[:, W:]
        divisor = jnp.maximum(expand(counts + pltpu.roll(counts, 120, 1)), 1.0)
        r.divisor[...] = divisor
        r.ag1[aligned(group * GROUP, GROUP), :] = (total[:, :W] / divisor).astype(BF16)
        spread(r.ag1, 0, W)

    if ring:
        add_stream("n", r.part_n, lambda at, size: r.fin_n, r.ring_n, shared=False, last=ahead)
    arrive("ids")
    onehot(oh)
    arrive("wo")
    send("wo_sib", r.v_wo.at[oh, wo_mine], r.v_wo.at[oh, wo_mine], sib_dev)
    loads["masked"].wait()
    positions = s * T + lax.broadcasted_iota(jnp.int32, (1, T), 1)

    def mark(i, hits):
        keys = r.v_masked[aligned(i * 8, 8), :].T
        for j in range(8):
            found = jnp.where(keys[:, j : j + 1] == positions, 1.0, 0.0)
            hits = jnp.maximum(hits, jnp.max(found.reshape(16, 8, T), axis=0))
        return hits

    hits = lax.fori_loop(0, cfg.M // 1024, mark, jnp.zeros((8, T), F32))
    keep = 1.0 - jnp.max(hits, axis=0, keepdims=True)
    spread_arrive(r.ag1, 0)

    stats = jnp.zeros((SLOT, 128), F32)
    sent_stats = jnp.zeros((SLOT, 128), F32)
    for p in range(pairs):
        scores = mm_nt(unfold(r.ag1[:, pair(p)]), r.k[:, pair(p)]) * scale
        scores = jnp.where(keep > 0, scores, -1e30)
        high, low = split(jnp.max(scores, axis=1, keepdims=True))
        low = low.astype(BF16).astype(F32)
        top = high + low
        weights = jnp.where(keep > 0, jnp.exp(scores - top), 0.0)
        r.e[pair_rows(p), :] = weights
        total_high, total_low = split(jnp.sum(weights, axis=1, keepdims=True))
        r.numer[:, pair(p)] = fold(mm(weights.astype(BF16), r.v[:, pair(p)]))[:SENT].astype(BF16)
        stats = stats + place(top, p)
        sent_stats = sent_stats + place(high, p) + place(low, p, 8) + place(total_high, p, 16) + place(total_low, p, 24)
    r.stats[...] = stats
    r.numer[:, W:] = sent_stats[:SENT].astype(BF16)
    scatter(r.numer, r.rs, s, h)
    tick("n")

    @pl.when(is_owner)
    def _():
        gathered_at_owner(r.rs, S, W + 128, 1)

        used = lanes < LH

        def stats_of(i):
            theirs = r.rs[aligned(i * 16, 16), :, W:].astype(F32).reshape(16 * GROUP, 128)
            return theirs, (theirs + pltpu.roll(theirs, 120, 1)).reshape(16, GROUP, 128)

        def highest(i, acc):
            return jnp.maximum(acc, jnp.max(stats_of(i)[1], axis=0))

        top = lax.fori_loop(0, S // 16, highest, jnp.full((GROUP, 128), -3e38, F32))

        def add(i, carry):
            numer, total = carry
            theirs, tops = stats_of(i)
            weight = jnp.where(used, jnp.exp(tops - top), 0.0).reshape(16 * GROUP, 128)
            totals = weight * (pltpu.roll(theirs, 112, 1) + pltpu.roll(theirs, 104, 1))
            part = expand(weight) * r.rs[aligned(i * 16, 16), :, :W].astype(F32).reshape(16 * GROUP, W)
            return (
                numer + jnp.sum(part.reshape(16, GROUP, W), axis=0),
                total + jnp.sum(totals.reshape(16, GROUP, 128), axis=0),
            )

        numer, total = lax.fori_loop(
            0, S // 16, add, (jnp.zeros((GROUP, W), F32), jnp.zeros((GROUP, 128), F32))
        )
        total = jnp.where(used, total, 1.0)
        out = numer / expand(total)
        r.own_out[...] = out
        r.own_lse[...] = jnp.where(used, top + jnp.log(total), 0.0)
        r.ag2[h, aligned(group * GROUP, GROUP), :] = out.astype(BF16)
        spread(r.ag2.at[h], 1, W)

    for name in ["win", "g2", "b2"]:
        loads[name].wait()
    arrive("wo_sib")
    arrive("wq")
    send("wq_sib", r.v_wq.at[oh, wq_mine], r.v_wq.at[oh, wq_mine], sib_dev)
    tick("n")
    spread_pass(r.ag2, 1, 0)
    pass_arrive(r.ag2, 0)

    for x in range(2):
        for p in range(pairs):
            r.gat[x, :, pair(p)] = mm(r.oh[x, :, pair_rows(p)], unfold(r.ag2[x, :, pair(p)])).astype(BF16)

    def second_norm(i):
        rows = aligned(i * 128, 128)
        attn = mm(r.gat[0, rows, :], r.v_wo[0]) + mm(r.gat[1, rows, :], r.v_wo[1])
        resid = r.v_tok[rows, :].astype(F32) + attn
        r.resid[rows, :] = resid
        scaled, _ = normalize(resid)
        r.n2[0, rows, :] = (scaled * gain(r.v_g2) + gain(r.v_b2)).astype(BF16)

    loop(T // 128, second_norm)
    tick("n")
    send("n2", r.n2.at[0], r.n2.at[1], sib_dev)
    send("gat", r.gat.at[h], r.gat_sib, sib_dev)

    def feed_forward(base):
        rows = aligned(base, half)

        def tile(j):
            cols = aligned(j * 256, 256)
            up = mm(r.n2[0, rows, :], r.v_win[:, cols])
            bell = jnp.exp(up * up * -0.5)
            share = normal_share(up, bell)
            density = bell * 0.3989422804014327
            r.act[rows, cols] = (up * share).astype(BF16)
            r.dup[rows, cols] = (r.dact[rows, cols] * (share + up * density)).astype(BF16)

        loop(F // 256, tile)

    def d_normed2(base, out):
        rows = aligned(base, half)

        def tile(j):
            cols = aligned(j * 256, 256)
            out[:, cols] = mm_nt(r.dup[rows, :], r.v_win[cols, :]).astype(out.dtype)

        loop(D // 256, tile)

    sib_units = pl.ds(pl.multiple_of((1 - core) * (F // 2), 128), F // 2)
    own_units = pl.ds(pl.multiple_of(core * (F // 2), 128), F // 2)
    feed_forward(oh * half)
    feed_forward(h * half)
    send("act", r.act.at[:, sib_units], r.act_sib, sib_dev)
    d_normed2(oh * half, r.dn_send)
    send("dn", r.dn_send, r.dn_recv, x_dev)
    send("dup", r.dup.at[:, sib_units], r.dup_sib, sib_dev)
    tick("n")

    arrive("act")
    arrive("cot")

    def grad_out(j):
        cols = pl.ds(pl.multiple_of(core * (F // 2) + j * 256, 128), 256)
        tile = mm_tn(r.act[:, cols], r.v_cot[0]) + mm_tn(r.act_sib[:, aligned(j * 256, 256)], r.v_cot[1])
        r.part_out[aligned(j * 256, 256), :] = tile.astype(BF16)

    loop(F // 2 // 256, grad_out)
    for k in range(2):
        base = k * (D // 2)
        add_stream(
            f"out{k}", r.part_out.at[pl.ds(base, D // 2)], rows_of(r.fin_out, core * (F // 2) + base), ring and r.ring_wide.at[k]
        )
    tick("n")
    arrive("dup")
    arrive("n2")

    def grad_in(j):
        cols = aligned(j * 256, 256)
        tile = mm_tn(r.n2[0, :, cols], r.dup[:, own_units]) + mm_tn(r.n2[1, :, cols], r.dup_sib[...])
        r.part_in[cols, :] = tile.astype(BF16)

    loop(D // 256, grad_in)

    for k in range(2):
        base = k * (D // 2)
        add_stream(
            f"in{k}", r.part_in.at[pl.ds(base, D // 2)], rows_of(r.fin_in, base, own_units), ring and r.ring_wide.at[2 + k]
        )

    def ffn_part(j):
        cols = aligned(j * 256, 256)
        r.fp[h, :, cols] = mm(r.act[...], r.v_wout[:, cols]).astype(BF16)

    d_normed2(h * half, r.dn_own)
    loop(D // 256, ffn_part)
    tick("n", "out0", "out1", "in0", "in1")

    arrive("dn")

    def second_norm_back(i, carry):
        gain_sum, shift_sum = carry
        rows = pl.ds(pl.multiple_of(h * half + i * 64, 64), 64)
        at = aligned(i * 64, 64)
        scaled, inverse = normalize(r.resid[rows, :])
        grad = r.dn_own[at, :] + r.dn_recv[at, :].astype(F32)
        d_resid = r.v_cot[0, rows, :].astype(F32) + normalize_back(grad, gain(r.v_g2), scaled, inverse)
        r.dres[at, :] = d_resid
        r.dat[rows, :] = d_resid.astype(BF16)
        return gain_sum + fold_rows(grad * scaled), shift_sum + fold_rows(grad)

    zero = jnp.zeros((8, D), F32)
    gain_sum, shift_sum = lax.fori_loop(0, half // 64, second_norm_back, (zero, zero))
    r.norm_grads[2:3, :] = jnp.sum(gain_sum, axis=0, keepdims=True)
    r.norm_grads[3:4, :] = jnp.sum(shift_sum, axis=0, keepdims=True)
    own_rows = aligned(h * half, half)
    other_rows = aligned(oh * half, half)
    for x in range(2):
        d_gathered = mm_nt(r.dat[own_rows, :], r.v_wo[x]).astype(BF16)
        for p in range(pairs):
            hot = r.oht[x, pair_rows(p), own_rows]
            r.dc[x, :, pair(p)] = fold(mm(hot, d_gathered[:, pair(p)]))[:SENT].astype(BF16)
    for x in range(2):
        scatter(r.dc.at[x], r.rs, me, x)
    send("dat", r.dat.at[own_rows], r.dat.at[own_rows], x_dev)

    send("fp_0", r.fp.at[h, own_rows], r.fp.at[h, own_rows], x_dev)
    tick("n", "out0", "out1")

    @pl.when(is_owner)
    def _():
        gathered_at_owner(r.rs, 2 * S, W, 2)
        rows = aligned(group * GROUP, GROUP)
        d_cluster = total_of(r.rs, 2 * S, W).astype(BF16)
        r.ag3[rows, :] = d_cluster
        spread(r.ag3, 2, W)
        product = d_cluster.astype(F32) * r.own_out[...]
        delta = pltpu.roll(r.own_lse[...], 8, 1)
        for p in range(pairs):
            block = product[:, pair(p)]
            delta = delta + jnp.where(
                lanes == 2 * p, jnp.sum(jnp.where(left, block, 0.0), axis=1, keepdims=True), 0.0
            )
            delta = delta + jnp.where(
                lanes == 2 * p + 1, jnp.sum(jnp.where(left, 0.0, block), axis=1, keepdims=True), 0.0
            )
        r.agdelta[rows, :] = delta
        spread(r.agdelta, 3, 256)

    tick("in0", "in1")
    spread_arrive(r.ag3, 2)
    spread_arrive(r.agdelta, 3)

    for p in range(pairs):
        d_probs = mm_nt(unfold(r.ag3[:, pair(p)]), r.v[:, pair(p)])
        factor = jnp.exp(column(r.stats[...], p) - column(r.agdelta[...], p, 8))
        probs = r.e[pair_rows(p), :] * factor
        r.pb[pair_rows(p), :] = probs.astype(BF16)
        d_scores = (probs * (d_probs - column(r.agdelta[...], p))).astype(BF16)
        r.dsb[pair_rows(p), :] = d_scores
        r.dcen[:, pair(p)] = fold(mm(d_scores, r.k[:, pair(p)]))[:SENT].astype(BF16)
    scatter(r.dcen, r.rs, s, h)

    for p in range(pairs):
        r.dkv[0, :, pair(p)] = (mm_tn(r.dsb[pair_rows(p), :], unfold(r.ag1[:, pair(p)])) * scale).astype(BF16)
        r.dkv[1, :, pair(p)] = mm_tn(r.pb[pair_rows(p), :], unfold(r.ag3[:, pair(p)])).astype(BF16)
    send("dkv", r.dkv, r.dkv_sib, sib_dev)

    def kv_part(rows):
        return mm_nt(r.dkv[0, rows, :], r.v_wk[...]) + mm_nt(r.dkv[1, rows, :], r.v_wv[...])

    r.kv_send[...] = kv_part(other_rows).astype(BF16)
    send("kv", r.kv_send, r.kv_recv, x_dev)
    arrive("dat")
    send("dat_sib", r.dat.at[:, sib_half], r.dat_sib, sib_dev)
    tick("n", "out0", "out1")

    tick("in0", "in1")
    arrive("dkv")
    if not ring:
        arrive("nrm")
    for i, name in enumerate(["k", "v"]):
        tile = mm_tn(r.nrm[:, own_half], r.dkv[i]) + mm_tn(r.nrm_sib[...], r.dkv_sib[i])
        r.part_small[i] = tile.astype(BF16)
        add_stream(name, r.part_small.at[i], rows_of(getattr(r, "fin_" + name), core * W), ring and r.ring_slim.at[i])
    tick("out0", "out1")
    arrive("gat")
    arrive("dat_sib")
    r.part_small[2] = (mm_tn(r.gat[h], r.dat[:, own_half]) + mm_tn(r.gat_sib[...], r.dat_sib[...])).astype(BF16)
    add_stream("o", r.part_small.at[2], rows_of(r.fin_o, 0, own_half), ring and r.ring_slim.at[2])
    r.dn_own[...] = kv_part(own_rows)
    @pl.when(is_owner)
    def _():
        gathered_at_owner(r.rs, S, W, 3)
        rows = aligned(group * GROUP, GROUP)
        r.ag4[h, rows, :] = (total_of(r.rs, S, W) * scale / r.divisor[...]).astype(BF16)
        spread(r.ag4.at[h], 4, W)

    tick("in0", "in1", "k", "v")

    spread_pass(r.ag4, 4, 1)
    tick(*pending())
    if ring:
        while "n" in pending():
            tick("n")
        size = W // n
        rows = pl.ds(pl.multiple_of(core * W + position * size, 16), size)
        for p in range(pairs):
            r.fin_q[rows, pair(p)] = mm(r.fin_n[:, pair_rows(p)], unfold(r.ag4[h, :, pair(p)])).astype(BF16)
        add_stream("q", r.fin_q.at[pl.ds(0, W)], rows_of(r.fin_q, core * W), None, at=ahead)
    else:
        for p in range(pairs):
            r.q[:, pair(p)] = mm(r.oh[h, :, pair_rows(p)], unfold(r.ag4[h, :, pair(p)])).astype(BF16)
        send("dq", r.q, r.dq_sib, sib_dev)
        arrive("dq")
        r.part_q[...] = (mm_tn(r.nrm[:, own_half], r.q[...]) + mm_tn(r.nrm_sib[...], r.dq_sib[...])).astype(BF16)
        add_stream("q", r.part_q, rows_of(r.fin_q, core * W), None)
    pass_arrive(r.ag4, 1)
    for x in range(2):
        for p in range(pairs):
            r.dq[x, :, pair(p)] = mm(r.oh[x, own_rows, pair_rows(p)], unfold(r.ag4[x, :, pair(p)])).astype(BF16)

    tick(*pending())
    arrive("kv")
    arrive("wq_sib")
    r.dn_own[...] += r.kv_recv[...].astype(F32) + mm_nt(r.dq[0], r.v_wq[0]) + mm_nt(r.dq[1], r.v_wq[1])

    def first_norm_back(i, carry):
        gain_sum, shift_sum = carry
        rows = pl.ds(pl.multiple_of(h * half + i * 64, 64), 64)
        at = aligned(i * 64, 64)
        scaled, inverse = normalize(r.v_tok[rows, :].astype(F32))
        grad = r.dn_own[at, :]
        grad_tokens = r.dres[at, :] + normalize_back(grad, gain(r.v_g1), scaled, inverse)
        r.gtok[rows, :] = grad_tokens.astype(BF16)
        return gain_sum + fold_rows(grad * scaled), shift_sum + fold_rows(grad)

    gain_sum, shift_sum = lax.fori_loop(0, half // 64, first_norm_back, (zero, zero))
    r.norm_grads[0:1, :] = jnp.sum(gain_sum, axis=0, keepdims=True)
    r.norm_grads[1:2, :] = jnp.sum(shift_sum, axis=0, keepdims=True)
    blocks = D // 128

    def norm_to(g, plane):
        cols = pl.ds(g * 128, 128)
        mine = jnp.logical_and(s == first + g, h == plane)
        copy = remote(
            r.norm_grads.at[:, cols], r.norm_rs.at[me], r.norm_send.at[g, plane], r.norm_sem.at[0], (first + g, plane)
        )
        return cols, mine, copy

    for plane in range(2):
        for g in range(blocks):
            cols, mine, copy = norm_to(g, plane)

            @pl.when(jnp.logical_not(mine))
            def _():
                copy.start()

            @pl.when(mine)
            def _():
                r.norm_rs[me] = r.norm_grads[:, cols]

    send("gtok", r.gtok.at[own_rows], r.gtok.at[own_rows], x_dev)
    send("fp_1", r.fp.at[h, other_rows], r.fp.at[h, other_rows], x_dev)
    tick(*pending())
    norm_owner = jnp.logical_and(s >= first, s < first + blocks)

    @pl.when(norm_owner)
    def _():
        block = r.norm_rs.at[pl.ds(0, 2 * S - 1)]
        remote(block, block, r.norm_send.at[0, 0], r.norm_sem.at[0], x_dev).wait_recv()

        def add(i, acc):
            return acc + r.norm_rs[i]

        cols = aligned(group * 128, 128)
        r.norm_fin[:, cols] = lax.fori_loop(0, 2 * S, add, jnp.zeros((8, 128), F32))
        block = r.norm_fin.at[:, cols]

        def to(k):
            remote(block, block, r.norm_send.at[blocks, 0], r.norm_sem.at[1 + group], (lax.rem(s + k + 1, S), h)).start()

        loop(S - 1, to)

    tick(*pending())
    for g in range(blocks):
        block = r.norm_fin.at[:, pl.ds(g * 128, 128)]

        @pl.when(s != first + g)
        def _():
            remote(block, block, r.norm_send.at[0, 0], r.norm_sem.at[1 + g], x_dev).wait_recv()

    while pending():
        tick(*pending())
    arrive("gtok")

    arrive("fp_0")
    arrive("fp_1")

    def block_out(i):
        rows = aligned(i * 64, 64)
        r.bout[rows, :] = (r.resid[rows, :] + r.fp[0, rows, :].astype(F32) + r.fp[1, rows, :].astype(F32)).astype(BF16)

    loop(T // 64, block_out)
    for st in streams:
        if st.shared:
            arrive(f"ring{st.i}")

    for finish in at_end:
        finish()
    for plane in range(2):
        for g in range(blocks):
            cols, mine, copy = norm_to(g, plane)

            @pl.when(jnp.logical_not(mine))
            def _():
                copy.wait_send()

    @pl.when(norm_owner)
    def _():
        block = r.norm_rs.at[pl.ds(0, S - 1)]
        remote(block, block, r.norm_send.at[blocks, 0], r.norm_sem.at[0], x_dev).wait_send()


def per_device(
    S,
    tokens,
    norm1_gain,
    norm1_shift,
    w_query,
    w_key,
    w_value,
    w_output,
    norm2_gain,
    norm2_shift,
    w_in,
    w_out,
    cluster_ids,
    masked_keys,
    cotangent,
):
    T, D = tokens.shape
    LH = cluster_ids.shape[1]
    W = w_query.shape[1]
    F = w_in.shape[1]
    n = S // 2
    ring = n <= 8
    cfg = SimpleNamespace(S=S, T=T, D=D, W=W, LH=LH, F=F, ring=ring, scatter_of=[0, 1, 2, 2, 3])

    M = -(-masked_keys.shape[0] // 1024) * 1024
    if M != masked_keys.shape[0]:
        masked_keys = jnp.pad(masked_keys, (0, M - masked_keys.shape[0]), constant_values=-1)
    cfg.M = M
    inputs = dict(
        tok=tokens,
        g1=norm1_gain,
        b1=norm1_shift,
        wq=w_query,
        wk=w_key,
        wv=w_value,
        wo=w_output,
        g2=norm2_gain,
        b2=norm2_shift,
        win=w_in,
        wout=w_out,
        ids=cluster_ids.T,
        masked=masked_keys.reshape(M // 128, 128),
        cot=cotangent,
    )
    outputs = dict(
        o_block=((T, D), BF16),
        o_tokens=((T, D), BF16),
        o_norm=((8, D), F32),
        o_q=((D, W), BF16),
        o_k=((D, W), BF16),
        o_v=((D, W), BF16),
        o_o=((W, D), BF16),
        o_in=((D, F), BF16),
        o_out=((F, D), BF16),
    )
    half = T // 2
    vmem = dict(
        v_tok=((T, D), BF16),
        v_g1=((D,), F32),
        v_b1=((D,), F32),
        v_wq=((2, D, W), BF16),
        v_wk=((D, W), BF16),
        v_wv=((D, W), BF16),
        v_wo=((2, W, D), BF16),
        v_g2=((D,), F32),
        v_b2=((D,), F32),
        v_win=((D, F), BF16),
        v_wout=((F, D), BF16),
        v_ids=((2, LH, T), jnp.int32),
        v_masked=((M // 128, 128), jnp.int32),
        v_cot=((2, T, D), BF16),
        nrm=((T, D), BF16),
        nrm_sib=((T, W), BF16),
        q=((T, W), BF16),
        k=((T, W), BF16),
        v=((T, W), BF16),
        oht=((2, LH * SLOT, T), BF16),
        oh=((2, T, LH * SLOT), BF16),
        sums=((SENT, W + 128), BF16),
        rs=((2 * S, GROUP, W + 128), BF16),
        divisor=((GROUP, W), F32),
        ag1=((SLOT, W), BF16),
        dact=((T, F), F32),
        e=((LH * SLOT, T), F32),
        numer=((SENT, W + 128), BF16),
        stats=((SLOT, 128), F32),
        own_out=((GROUP, W), F32),
        ag2=((2, SLOT, W), BF16),
        own_lse=((GROUP, 128), F32),
        gat=((2, T, W), BF16),
        gat_sib=((T, W), BF16),
        resid=((T, D), F32),
        n2=((2, T, D), BF16),
        act=((T, F), BF16),
        dup=((T, F), BF16),
        act_sib=((T, F // 2), BF16),
        dup_sib=((T, F // 2), BF16),
        dn_send=((half, D), BF16),
        dn_recv=((half, D), BF16),
        dn_own=((half, D), F32),
        dres=((half, D), F32),
        dat=((T, D), BF16),
        dat_sib=((T, W), BF16),
        dc=((2, SENT, W), BF16),
        ag3=((SLOT, W), BF16),
        agdelta=((SLOT, 128), F32),
        pb=((LH * SLOT, T), BF16),
        dsb=((LH * SLOT, T), BF16),
        dcen=((SENT, W), BF16),
        ag4=((2, SLOT, W), BF16),
        dkv=((2, T, W), BF16),
        dkv_sib=((2, T, W), BF16),
        kv_send=((half, D), BF16),
        kv_recv=((half, D), BF16),
        dq=((2, half, W), BF16),
        norm_grads=((8, D), F32),
        norm_rs=((2 * S, 8, 128), F32),
        fp=((2, T, D), BF16),
        part_out=((F // 2, D), BF16),
        part_in=((D, F // 2), BF16),
        part_small=((3, W, W), BF16),
        ids_sib=((LH, T), jnp.int32),
    )
    steps = 2 * (n - 1) if ring else 1
    if ring:
        vmem["ring_wide"] = ((4, n - 1, D // 2 // n, D), BF16)
        vmem["ring_slim"] = ((3, n - 1, W // n, W), BF16)
        vmem["ring_n"] = ((n - 1, W // n, LH * SLOT), BF16)
        vmem["oht_sib"] = ((LH * SLOT, T), BF16)
        vmem["part_n"] = ((W, LH * SLOT), BF16)
        vmem["fin_n"] = ((W // n, LH * SLOT), BF16)
    else:
        vmem["dq_sib"] = ((T, W), BF16)
        vmem["part_q"] = ((W, W), BF16)
    sems = dict(
        load_sem=(14,),
        ex_send=(32,),
        ex_recv=(32,),
        sc_send=(5, GROUPS),
        sc_recv=(4,),
        sp_send=(5,),
        sp_recv=(5, GROUPS),
        pass_send=(2, GROUPS),
        pass_recv=(2, GROUPS),
        ring_send=(STREAMS, steps),
        ring_recv=(STREAMS, steps),
        norm_send=(D // 128 + 1, 2),
        norm_sem=(D // 128 + 1,),
    )
    names = list(inputs) + list(outputs) + list(vmem) + list(sems)
    results = pl.pallas_call(
        functools.partial(kernel, cfg, names),
        out_shape=[pltpu.VMEM(*o) for o in outputs.values()],
        in_specs=[pl.BlockSpec(memory_space=pl.ANY)] * len(inputs),
        out_specs=[pl.BlockSpec(memory_space=pltpu.VMEM)] * len(outputs),
        scratch_shapes=[pltpu.VMEM(*b) for b in vmem.values()] + [pltpu.SemaphoreType.DMA(b) for b in sems.values()],
        compiler_params=pltpu.CompilerParams(collective_id=0, has_side_effects=True, vmem_limit_bytes=(54 if ring else 55) * 2**20),
        name="block",
    )(*inputs.values())
    block, grad_tokens, norms, *grads = results
    if not ring:
        grads = lax.psum(grads, "seq")
    block, gain1, shift1, gain2, shift2, grad_tokens, *grads = widen(block, norms, [grad_tokens] + grads)
    grad_q, grad_k, grad_v, grad_o, grad_in, grad_out = grads
    return (
        block,
        grad_tokens,
        gain1,
        shift1,
        grad_q,
        grad_k,
        grad_v,
        grad_o,
        gain2,
        shift2,
        grad_in,
        grad_out,
    )


def widen(block, norms, arrays):
    D = norms.shape[1]
    tiles = [
        (i, k * size, size)
        for i, a in enumerate(arrays)
        for size in [a.shape[0] // max(2, a.shape[0] // 256)]
        for k in range(a.shape[0] // size)
    ]
    count = len(arrays)

    def kernel(*refs):
        block_in, norms_in, *rest = refs
        ins, rest = rest[:count], rest[count:]
        block_out, *rest = rest
        norm_outs, rest = rest[:4], rest[4:]
        outs, rest = rest[:count], rest[count:]
        flat, rest = rest[:4], rest[4:]
        wide, rest = rest[:count], rest[count:]
        sem_out, sem = rest
        stores = []
        for k, (i, at, size) in enumerate(tiles):

            def cast(j, i=i, at=at):
                rows = pl.ds(pl.multiple_of(at + j * 32, 32), 32)
                wide[i][rows, :] = ins[i][rows, :].astype(F32)

            loop(size // 32, cast)
            rows = pl.ds(at, size)
            stores.append(pltpu.make_async_copy(wide[i].at[rows], outs[i].at[rows], sem_out.at[k]))
            stores[-1].start()
        for k in range(4):
            flat[k][...] = norms_in[k, :]
            stores.append(pltpu.make_async_copy(flat[k], norm_outs[k], sem.at[k]))
            stores[-1].start()
        stores.append(pltpu.make_async_copy(block_in, block_out, sem.at[4]))
        stores[-1].start()
        for store in stores:
            store.wait()

    out_shape = [jax.ShapeDtypeStruct(block.shape, block.dtype)]
    out_shape += [jax.ShapeDtypeStruct((D,), F32)] * 4
    out_shape += [jax.ShapeDtypeStruct(a.shape, F32) for a in arrays]
    anywhere = pl.BlockSpec(memory_space=pl.ANY)
    return pl.pallas_call(
        kernel,
        out_shape=out_shape,
        in_specs=[pl.BlockSpec(memory_space=pltpu.VMEM)] * (count + 2),
        out_specs=[anywhere] * len(out_shape),
        scratch_shapes=[pltpu.VMEM((D,), F32)] * 4
        + [pltpu.VMEM(a.shape, F32) for a in arrays]
        + [pltpu.SemaphoreType.DMA((len(tiles),)), pltpu.SemaphoreType.DMA((5,))],
        compiler_params=pltpu.CompilerParams(vmem_limit_bytes=20 * 2**20),
        name="widen",
    )(block, norms, *arrays)


def solution(mesh):
    columns, rows = P(None, "head"), P("head", None)
    by_token = P("seq", None)
    return jax.shard_map(
        functools.partial(per_device, mesh.shape["seq"]),
        mesh=mesh,
        in_specs=(by_token, P(), P(), columns, columns, columns, rows, P(), P(), columns, rows, P("seq", "head"), P(), by_token),
        out_specs=(by_token, by_token, P(), P(), columns, columns, columns, rows, P(), P(), columns, rows),
        check_vma=False,
    )
```

```python
import functools
from types import SimpleNamespace

import jax
import jax.numpy as jnp
from jax import lax
from jax.experimental import pallas as pl
from jax.experimental.pallas import tpu as pltpu
from jax.sharding import PartitionSpec as P

CLUSTERS = 100
EPSILON = 1e-05
MESH = pl.DeviceIdType.MESH
F32 = jnp.float32
BF16 = jnp.bfloat16
SLOT = 128
GROUP = 16
GROUPS = -(-CLUSTERS // GROUP)
SENT = GROUPS * GROUP
STREAMS = 9


def mm(a, b):
    return lax.dot_general(a, b, (((1,), (0,)), ((), ())), preferred_element_type=F32)


def mm_nt(a, b):
    return lax.dot_general(a, b, (((1,), (1,)), ((), ())), preferred_element_type=F32)


def mm_tn(a, b):
    return lax.dot_general(a, b, (((0,), (0,)), ((), ())), preferred_element_type=F32)


def aligned(index, size):
    return pl.ds(pl.multiple_of(index, size), size)


def remote(src, dst, send_sem, recv_sem, device):
    return pltpu.make_async_remote_copy(
        src_ref=src, dst_ref=dst, send_sem=send_sem, recv_sem=recv_sem, device_id=device, device_id_type=MESH
    )


def loop(count, body):
    def step(i, carry):
        body(i)
        return carry

    lax.fori_loop(0, count, step, 0)


def normalize(values):
    centred = values - jnp.mean(values, axis=-1, keepdims=True)
    inverse = lax.rsqrt(jnp.mean(centred * centred, axis=-1, keepdims=True) + EPSILON)
    return centred * inverse, inverse


def normalize_back(grad, gain, scaled, inverse):
    inner = grad * gain
    return inverse * (
        inner - jnp.mean(inner, axis=-1, keepdims=True) - scaled * jnp.mean(inner * scaled, axis=-1, keepdims=True)
    )


ERFC = (
    0.27643095583919713,
    0.2770312983463117,
    0.2368366418089808,
    0.21634403047784398,
    -0.05751923336137985,
    0.34364725799951945,
    -0.5200124379554546,
    0.2829391760305868,
    -0.05569765451595309,
)


def normal_share(x, bell):
    t = 1.0 / (1.0 + (0.49 * 0.5**0.5) * jnp.abs(x))
    series = 0.5 * ERFC[-1]
    for factor in ERFC[-2::-1]:
        series = series * t + 0.5 * factor
    tail = series * t * bell
    return jnp.where(x < 0, tail, 1.0 - tail)


def fold_rows(values):
    return jnp.sum(values.reshape(values.shape[0] // 8, 8, values.shape[1]), axis=0)


def kernel(cfg, names, *all_refs):
    r = SimpleNamespace(**dict(zip(names, all_refs)))
    r.bout, r.gtok, r.norm_fin = r.o_block, r.o_tokens, r.o_norm
    r.fin_q, r.fin_k, r.fin_v, r.fin_o, r.fin_in, r.fin_out = r.o_q, r.o_k, r.o_v, r.o_o, r.o_in, r.o_out
    S, T, D, W, LH, F = cfg.S, cfg.T, cfg.D, cfg.W, cfg.LH, cfg.F
    pairs = LH // 2
    half = T // 2
    scale = (W // LH) ** (-0.5)
    ring = cfg.ring
    n = S // 2
    s = lax.axis_index("seq")
    h = lax.axis_index("head")
    oh = 1 - h
    core = lax.rem(s, 2)
    chip = lax.div(s, 2)
    me = s * 2 + h
    x_dev = (s, oh)
    sib_dev = (s + 1 - 2 * core, h)
    first = S // 4
    is_owner = jnp.logical_and(s >= first, s < first + GROUPS)
    group = s - first
    lanes = lax.broadcasted_iota(jnp.int32, (1, 128), 1)
    left = lanes < 64

    def fold(block):
        return jnp.where(left, block[:SLOT], block[SLOT:])

    def unfold(block):
        zero = jnp.zeros_like(block)
        return jnp.concatenate([jnp.where(left, block, zero), jnp.where(left, zero, block)], axis=0)

    def expand(stats):
        return jnp.concatenate(
            [jnp.where(left, stats[:, 2 * p : 2 * p + 1], stats[:, 2 * p + 1 : 2 * p + 2]) for p in range(pairs)], axis=1
        )

    def column(stats, p, at=0):
        return jnp.concatenate(
            [stats[:, at + 2 * p : at + 2 * p + 1], stats[:, at + 2 * p + 1 : at + 2 * p + 2]], axis=0
        )

    def place(columns, p, at=0):
        rows = columns.shape[0] // 2
        return jnp.where(lanes == at + 2 * p, columns[:rows], 0.0) + jnp.where(
            lanes == at + 2 * p + 1, columns[rows:], 0.0
        )

    def pair(p):
        return slice(p * 128, (p + 1) * 128)

    def pair_rows(p):
        return slice(p * 2 * SLOT, (p + 1) * 2 * SLOT)

    at_end = []

    loads = {}
    for i, name in enumerate(
        ["ids", "tok", "g1", "b1", "wq", "wo", "wk", "wv", "cot", "wout", "masked", "win", "g2", "b2"]
    ):
        dst = getattr(r, "v_" + name)
        dst = {"cot": lambda d: d.at[0], "wq": lambda d: d.at[h], "wo": lambda d: d.at[h], "ids": lambda d: d.at[h]}.get(
            name, lambda d: d
        )(dst)
        loads[name] = pltpu.make_async_copy(getattr(r, name), dst, r.load_sem.at[i])

    barrier = pltpu.get_barrier_semaphore()

    def greet(k):
        other = lax.rem(me + k + 1, 2 * S)
        pl.semaphore_signal(
            barrier, inc=1, device_id=(lax.div(other, 2), lax.rem(other, 2)), device_id_type=MESH
        )

    loop(2 * S - 1, greet)
    for load in loads.values():
        load.start()

    exchanges = {}

    def send(name, src, dst, device):
        i = len(exchanges)
        copy = remote(src, dst, r.ex_send.at[i], r.ex_recv.at[i], device)
        copy.start()
        exchanges[name] = copy
        at_end.append(copy.wait_send)

    def arrive(name):
        exchanges[name].wait_recv()

    counters = {"scatter": 0, "spread": 0}

    def scatter(src, dst, slot, plane):
        i = counters["scatter"]
        counters["scatter"] += 1

        def at(g):
            rows = pl.ds(g * GROUP, GROUP)
            mine = jnp.logical_and(s == first + g, h == plane)
            copy = remote(
                src.at[rows], dst.at[slot, :, cols], r.sc_send.at[i, g], r.sc_recv.at[cfg.scatter_of[i]], (first + g, plane)
            )
            return rows, mine, copy

        cols = pl.ds(0, src.shape[1])

        for g in range(GROUPS):
            rows, mine, copy = at(g)

            @pl.when(jnp.logical_not(mine))
            def _():
                copy.start()

            @pl.when(mine)
            def _():
                dst[slot, :, cols] = src[rows, :]

        def finish():
            for g in range(GROUPS):
                rows, mine, copy = at(g)

                @pl.when(jnp.logical_not(mine))
                def _():
                    copy.wait_send()

        at_end.append(finish)

    def gathered_at_owner(buf, count, width, i):
        block = buf.at[pl.ds(0, count - 1), :, pl.ds(0, width)]
        remote(block, block, r.sc_send.at[0, 0], r.sc_recv.at[i], x_dev).wait_recv()

    def spread(buf, i, width):
        rows = aligned(group * GROUP, GROUP)
        block = buf.at[rows]

        def to(k):
            copy = remote(block, block, r.sp_send.at[i], r.sp_recv.at[i, group], (lax.rem(s + k + 1, S), h))
            copy.start()

        loop(S - 1, to)

        def finish():
            @pl.when(is_owner)
            def _():
                block = r.rs.at[pl.ds(0, S - 1), :, pl.ds(0, width)]
                remote(block, block, r.sp_send.at[i], r.sp_recv.at[i, 0], x_dev).wait_send()

        at_end.append(finish)

    def spread_arrive(buf, i):
        for g in range(GROUPS):

            @pl.when(s != first + g)
            def _():
                block = buf.at[pl.ds(g * GROUP, GROUP)]
                remote(block, block, r.sp_send.at[i], r.sp_recv.at[i, g], x_dev).wait_recv()

    def spread_pass(buf, i, j):
        for g in range(GROUPS):
            block = buf.at[h, pl.ds(g * GROUP, GROUP)]

            @pl.when(s != first + g)
            def _():
                remote(block, block, r.sp_send.at[i], r.sp_recv.at[i, g], x_dev).wait_recv()

            copy = remote(block, block, r.pass_send.at[j, g], r.pass_recv.at[j, g], x_dev)
            copy.start()
            at_end.append(copy.wait_send)

    def pass_arrive(buf, j):
        for g in range(GROUPS):
            block = buf.at[oh, pl.ds(g * GROUP, GROUP)]
            remote(block, block, r.pass_send.at[j, g], r.pass_recv.at[j, g], x_dev).wait_recv()

    def total_of(buf, count, width):
        def add(i, acc):
            return acc + jnp.sum(buf[aligned(i * 16, 16), :, :width].astype(F32), axis=0)

        return lax.fori_loop(0, count // 16, add, jnp.zeros((GROUP, width), F32))

    def split(values):
        high = values.astype(BF16).astype(F32)
        return high, values - high

    z_count = n // 2
    z, y = lax.div(chip, 2), lax.rem(chip, 2)
    position = jnp.where(y == 0, z, n - 1 - z)

    def device_at(p):
        p = lax.rem(p + n, n)
        return (2 * jnp.where(p < z_count, 2 * p, 2 * (n - 1 - p) + 1) + core, h)

    streams = []
    ahead, behind = n // 2, n - 1 - n // 2

    def add_stream(name, part, fin_block, recv, shared=True, at=0, last=2 * ahead):
        i = len(streams)
        st = SimpleNamespace(name=name, i=i, part=part, fin=fin_block, turn=at, last=last)
        st.chunk = part.shape[0] // n
        st.recv = recv
        st.shared = shared
        st.ways = [(1, ahead, 0), (-1, behind, ahead)] if i % 2 == 0 else [(-1, ahead, 0), (1, behind, ahead)]
        if ring:
            streams.append(st)
            advance(st)
        else:
            st.fin(0, part.shape[0])[...] = part[...]
        return st

    def part_chunk(st, k):
        return st.part.at[pl.ds(pl.multiple_of(lax.rem(k + 2 * n, n) * st.chunk, 16), st.chunk)]

    def fin_chunk(st, k):
        return st.fin(lax.rem(k + 2 * n, n) * st.chunk, st.chunk)

    def sum_copy(st, way, t):
        sign, hops, slot = way
        src = part_chunk(st, position + sign * hops) if t == 0 else st.recv.at[slot + t - 1]
        return remote(
            src,
            st.recv.at[slot + t],
            r.ring_send.at[st.i, slot + t],
            r.ring_recv.at[st.i, slot + t],
            device_at(position + sign),
        )

    def pass_copy(st, way, t):
        sign, hops, slot = way
        block = fin_chunk(st, position - sign * t)
        return remote(
            block,
            block,
            r.ring_send.at[st.i, n - 1 + slot + t],
            r.ring_recv.at[st.i, n - 1 + slot + t],
            device_at(position + sign),
        )

    def start(copy):
        copy.start()
        at_end.append(copy.wait_send)

    def advance(st):
        t = st.turn
        st.turn += 1
        if t <= ahead:
            for way in st.ways:
                sign, hops, slot = way
                if 0 < t <= hops and st.recv is not None:
                    sum_copy(st, way, t - 1).wait_recv()
                    if t < hops:
                        came = st.recv[slot + t - 1].astype(F32) + part_chunk(st, position + sign * (hops - t))[...].astype(F32)
                        st.recv[slot + t - 1] = came.astype(BF16)
                if t < hops:
                    start(sum_copy(st, way, t))
            if t == ahead:
                if st.recv is not None:
                    total = part_chunk(st, position)[...].astype(F32)
                    for sign, hops, slot in st.ways:
                        total = total + st.recv[slot + hops - 1].astype(F32)
                    fin_chunk(st, position)[...] = total.astype(BF16)
                for way in st.ways if st.last > ahead else []:
                    start(pass_copy(st, way, 0))
        elif t <= 2 * ahead:
            u = t - ahead
            for way in st.ways:
                sign, hops, slot = way
                if u <= hops:
                    block = fin_chunk(st, position - sign * u)
                    remote(
                        block, block, r.ring_send.at[st.i, 0], r.ring_recv.at[st.i, n - 1 + slot + u - 1], x_dev
                    ).wait_recv()
                if u < hops:
                    start(pass_copy(st, way, u))
            if u == ahead and st.shared:
                whole = st.fin(0, st.part.shape[0])
                send(f"ring{st.i}", whole, whole, sib_dev)

    def tick(*wanted):
        for name in wanted:
            for st in streams:
                if st.name == name and st.turn <= st.last:
                    advance(st)

    def pending():
        return [st.name for st in streams if st.turn <= st.last]

    if not ring:
        for name in ["fin_out", "fin_in", "fin_k", "fin_v", "fin_q", "fin_o"]:
            ref = getattr(r, name)
            ref[...] = jnp.zeros_like(ref)

    def rows_of(ref, base, cols=None):
        def block(at, size):
            rows = pl.ds(pl.multiple_of(base + at, 16), size)
            return ref.at[rows] if cols is None else ref.at[rows, cols]

        return block

    r.ag1[...] = jnp.zeros_like(r.ag1)
    r.ag3[...] = jnp.zeros_like(r.ag3)
    r.ag2[...] = jnp.zeros_like(r.ag2)
    r.ag4[...] = jnp.zeros_like(r.ag4)
    r.agdelta[...] = jnp.zeros_like(r.agdelta)
    r.norm_grads[...] = jnp.zeros_like(r.norm_grads)

    def onehot_t(ids, out):
        rows = lax.broadcasted_iota(jnp.int32, (SLOT, T), 0)
        for j in range(LH):
            out[j * SLOT : (j + 1) * SLOT, :] = jnp.where(rows == ids[j : j + 1, :], 1.0, 0.0).astype(BF16)

    def onehot(x):
        onehot_t(r.v_ids[x], r.oht.at[x])
        for p in range(pairs):
            r.oh[x, :, pair_rows(p)] = r.oht[x, pair_rows(p), :].T

    def gain(ref):
        return ref[...].reshape(1, D)

    loads["ids"].wait()
    onehot(h)
    for name in ["g1", "b1", "tok"]:
        loads[name].wait()

    def first_norm(i):
        rows = aligned(i * 64, 64)
        scaled, _ = normalize(r.v_tok[rows, :].astype(F32))
        r.nrm[rows, :] = (scaled * gain(r.v_g1) + gain(r.v_b1)).astype(BF16)

    loop(T // 64, first_norm)
    loads["wq"].wait()

    def project(weight, out):
        def tile(i):
            rows = aligned(i * 256, 256)
            out[rows, :] = mm(r.nrm[rows, :], weight).astype(BF16)

        loop(T // 256, tile)

    project(r.v_wq[h], r.q)
    counts = jnp.zeros((SLOT, 128), F32)
    ones = jnp.ones((T, 128), BF16)
    for p in range(pairs):
        hot = r.oht[h, pair_rows(p), :]
        r.sums[:, pair(p)] = fold(mm(hot, r.q[:, pair(p)]))[:SENT].astype(BF16)
        counts = counts + place(mm(hot, ones)[:, :1], p)
    high = jnp.where(counts >= 256.0, 256.0, 0.0) + jnp.where(counts >= 512.0, 256.0, 0.0)
    r.sums[:, W:] = (high + pltpu.roll(counts - high, 8, 1))[:SENT].astype(BF16)

    pl.semaphore_wait(barrier, 2 * S - 1)
    scatter(r.sums, r.rs, s, h)
    send("ids", r.v_ids.at[h], r.v_ids.at[h], x_dev)
    loads["wo"].wait()
    wo_mine = pl.ds(pl.multiple_of(core * (W // 2), 16), W // 2)
    send("wo", r.v_wo.at[h, wo_mine], r.v_wo.at[h, wo_mine], x_dev)
    wq_mine = pl.ds(pl.multiple_of(core * W, 16), W)
    send("wq", r.v_wq.at[h, wq_mine], r.v_wq.at[h, wq_mine], x_dev)
    sib_half = pl.ds(pl.multiple_of((1 - core) * W, 128), W)
    own_half = pl.ds(pl.multiple_of(core * W, 128), W)
    loads["cot"].wait()
    send("cot", r.v_cot.at[0], r.v_cot.at[1], sib_dev)
    send("nrm", r.nrm.at[:, sib_half], r.nrm_sib, sib_dev)
    send("ids_sib", r.v_ids.at[h], r.ids_sib, sib_dev)

    loads["wk"].wait()
    project(r.v_wk[...], r.k)
    loads["wv"].wait()
    project(r.v_wv[...], r.v)
    loads["wout"].wait()

    def d_act(j):
        cols = aligned(j * 256, 256)
        r.dact[:, cols] = mm_nt(r.v_cot[0], r.v_wout[cols, :])

    loop(F // 256, d_act)
    if ring:
        arrive("nrm")
        arrive("ids_sib")
        onehot_t(r.ids_sib[...], r.oht_sib)
        nrm_t, nrm_sib_t = r.nrm[:, own_half].T, r.nrm_sib[...].T
        for p in range(pairs):
            tile = mm_nt(nrm_t, r.oht[h, pair_rows(p), :]) + mm_nt(nrm_sib_t, r.oht_sib[pair_rows(p), :])
            r.part_n[:, pair_rows(p)] = tile.astype(BF16)

    @pl.when(is_owner)
    def _():
        gathered_at_owner(r.rs, S, W + 128, 0)
        total = total_of(r.rs, S, W + 128)
        counts = total[:, W:]
        divisor = jnp.maximum(expand(counts + pltpu.roll(counts, 120, 1)), 1.0)
        r.divisor[...] = divisor
        r.ag1[aligned(group * GROUP, GROUP), :] = (total[:, :W] / divisor).astype(BF16)
        spread(r.ag1, 0, W)

    if ring:
        add_stream("n", r.part_n, lambda at, size: r.fin_n, r.ring_n, shared=False, last=ahead)
    arrive("ids")
    onehot(oh)
    arrive("wo")
    send("wo_sib", r.v_wo.at[oh, wo_mine], r.v_wo.at[oh, wo_mine], sib_dev)
    loads["masked"].wait()
    positions = s * T + lax.broadcasted_iota(jnp.int32, (1, T), 1)

    def mark(i, hits):
        keys = r.v_masked[aligned(i * 8, 8), :].T
        for j in range(8):
            found = jnp.where(keys[:, j : j + 1] == positions, 1.0, 0.0)
            hits = jnp.maximum(hits, jnp.max(found.reshape(16, 8, T), axis=0))
        return hits

    hits = lax.fori_loop(0, cfg.M // 1024, mark, jnp.zeros((8, T), F32))
    keep = 1.0 - jnp.max(hits, axis=0, keepdims=True)
    spread_arrive(r.ag1, 0)

    stats = jnp.zeros((SLOT, 128), F32)
    sent_stats = jnp.zeros((SLOT, 128), F32)
    for p in range(pairs):
        scores = mm_nt(unfold(r.ag1[:, pair(p)]), r.k[:, pair(p)]) * scale
        scores = jnp.where(keep > 0, scores, -1e30)
        high, low = split(jnp.max(scores, axis=1, keepdims=True))
        low = low.astype(BF16).astype(F32)
        top = high + low
        weights = jnp.where(keep > 0, jnp.exp(scores - top), 0.0)
        r.e[pair_rows(p), :] = weights
        total_high, total_low = split(jnp.sum(weights, axis=1, keepdims=True))
        r.numer[:, pair(p)] = fold(mm(weights.astype(BF16), r.v[:, pair(p)]))[:SENT].astype(BF16)
        stats = stats + place(top, p)
        sent_stats = sent_stats + place(high, p) + place(low, p, 8) + place(total_high, p, 16) + place(total_low, p, 24)
    r.stats[...] = stats
    r.numer[:, W:] = sent_stats[:SENT].astype(BF16)
    scatter(r.numer, r.rs, s, h)
    tick("n")

    @pl.when(is_owner)
    def _():
        gathered_at_owner(r.rs, S, W + 128, 1)

        used = lanes < LH

        def stats_of(i):
            theirs = r.rs[aligned(i * 16, 16), :, W:].astype(F32).reshape(16 * GROUP, 128)
            return theirs, (theirs + pltpu.roll(theirs, 120, 1)).reshape(16, GROUP, 128)

        def highest(i, acc):
            return jnp.maximum(acc, jnp.max(stats_of(i)[1], axis=0))

        top = lax.fori_loop(0, S // 16, highest, jnp.full((GROUP, 128), -3e38, F32))

        def add(i, carry):
            numer, total = carry
            theirs, tops = stats_of(i)
            weight = jnp.where(used, jnp.exp(tops - top), 0.0).reshape(16 * GROUP, 128)
            totals = weight * (pltpu.roll(theirs, 112, 1) + pltpu.roll(theirs, 104, 1))
            part = expand(weight) * r.rs[aligned(i * 16, 16), :, :W].astype(F32).reshape(16 * GROUP, W)
            return (
                numer + jnp.sum(part.reshape(16, GROUP, W), axis=0),
                total + jnp.sum(totals.reshape(16, GROUP, 128), axis=0),
            )

        numer, total = lax.fori_loop(
            0, S // 16, add, (jnp.zeros((GROUP, W), F32), jnp.zeros((GROUP, 128), F32))
        )
        total = jnp.where(used, total, 1.0)
        out = numer / expand(total)
        r.own_out[...] = out
        r.own_lse[...] = jnp.where(used, top + jnp.log(total), 0.0)
        r.ag2[h, aligned(group * GROUP, GROUP), :] = out.astype(BF16)
        spread(r.ag2.at[h], 1, W)
        block = r.ag2.at[h, aligned(group * GROUP, GROUP)]

        def across(k):
            remote(block, block, r.pass_send.at[0, 0], r.pass_recv.at[0, group], (lax.rem(s + k, S), oh)).start()

        loop(S, across)

    for name in ["win", "g2", "b2"]:
        loads[name].wait()
    arrive("wo_sib")
    arrive("wq")
    send("wq_sib", r.v_wq.at[oh, wq_mine], r.v_wq.at[oh, wq_mine], sib_dev)
    tick("n")
    spread_arrive(r.ag2.at[h], 1)

    def across_sent():
        @pl.when(is_owner)
        def _():
            block = r.rs.at[pl.ds(0, S), :, pl.ds(0, W)]
            remote(block, block, r.pass_send.at[0, 0], r.pass_recv.at[0, 0], x_dev).wait_send()

    at_end.append(across_sent)

    def gather(x):
        for p in range(pairs):
            r.gat[x, :, pair(p)] = mm(r.oh[x, :, pair_rows(p)], unfold(r.ag2[x, :, pair(p)])).astype(BF16)

    gather(h)
    pass_arrive(r.ag2, 0)
    gather(oh)

    def second_norm(i):
        rows = aligned(i * 128, 128)
        attn = mm(r.gat[0, rows, :], r.v_wo[0]) + mm(r.gat[1, rows, :], r.v_wo[1])
        resid = r.v_tok[rows, :].astype(F32) + attn
        r.resid[rows, :] = resid
        scaled, _ = normalize(resid)
        r.n2[0, rows, :] = (scaled * gain(r.v_g2) + gain(r.v_b2)).astype(BF16)

    loop(T // 128, second_norm)
    tick("n")
    send("n2", r.n2.at[0], r.n2.at[1], sib_dev)
    send("gat", r.gat.at[h], r.gat_sib, sib_dev)

    def feed_forward(base):
        rows = aligned(base, half)

        def tile(j):
            cols = aligned(j * 256, 256)
            up = mm(r.n2[0, rows, :], r.v_win[:, cols])
            bell = jnp.exp(up * up * -0.5)
            share = normal_share(up, bell)
            density = bell * 0.3989422804014327
            r.act[rows, cols] = (up * share).astype(BF16)
            r.dup[rows, cols] = (r.dact[rows, cols] * (share + up * density)).astype(BF16)

        loop(F // 256, tile)

    def d_normed2(base, out):
        rows = aligned(base, half)

        def tile(j):
            cols = aligned(j * 256, 256)
            out[:, cols] = mm_nt(r.dup[rows, :], r.v_win[cols, :]).astype(out.dtype)

        loop(D // 256, tile)

    sib_units = pl.ds(pl.multiple_of((1 - core) * (F // 2), 128), F // 2)
    own_units = pl.ds(pl.multiple_of(core * (F // 2), 128), F // 2)
    feed_forward(oh * half)
    feed_forward(h * half)
    send("act", r.act.at[:, sib_units], r.act_sib, sib_dev)
    d_normed2(oh * half, r.dn_send)
    send("dn", r.dn_send, r.dn_recv, x_dev)
    send("dup", r.dup.at[:, sib_units], r.dup_sib, sib_dev)
    tick("n")

    arrive("act")
    arrive("cot")

    def grad_out(j):
        cols = pl.ds(pl.multiple_of(core * (F // 2) + j * 256, 128), 256)
        tile = mm_tn(r.act[:, cols], r.v_cot[0]) + mm_tn(r.act_sib[:, aligned(j * 256, 256)], r.v_cot[1])
        r.part_out[aligned(j * 256, 256), :] = tile.astype(BF16)

    loop(F // 2 // 256, grad_out)
    for k in range(2):
        base = k * (D // 2)
        add_stream(
            f"out{k}", r.part_out.at[pl.ds(base, D // 2)], rows_of(r.fin_out, core * (F // 2) + base), ring and r.ring_wide.at[k]
        )
    tick("n")
    arrive("dup")
    arrive("n2")

    def grad_in(j):
        cols = aligned(j * 256, 256)
        tile = mm_tn(r.n2[0, :, cols], r.dup[:, own_units]) + mm_tn(r.n2[1, :, cols], r.dup_sib[...])
        r.part_in[cols, :] = tile.astype(BF16)

    loop(D // 256, grad_in)

    for k in range(2):
        base = k * (D // 2)
        add_stream(
            f"in{k}", r.part_in.at[pl.ds(base, D // 2)], rows_of(r.fin_in, base, own_units), ring and r.ring_wide.at[2 + k]
        )

    def ffn_part(j):
        cols = aligned(j * 256, 256)
        r.fp[h, :, cols] = mm(r.act[...], r.v_wout[:, cols]).astype(BF16)

    d_normed2(h * half, r.dn_own)
    loop(D // 256, ffn_part)
    tick("n", "out0", "out1", "in0", "in1")

    arrive("dn")

    def second_norm_back(i, carry):
        gain_sum, shift_sum = carry
        rows = pl.ds(pl.multiple_of(h * half + i * 64, 64), 64)
        at = aligned(i * 64, 64)
        scaled, inverse = normalize(r.resid[rows, :])
        grad = r.dn_own[at, :] + r.dn_recv[at, :].astype(F32)
        d_resid = r.v_cot[0, rows, :].astype(F32) + normalize_back(grad, gain(r.v_g2), scaled, inverse)
        r.dres[at, :] = d_resid
        r.dat[rows, :] = d_resid.astype(BF16)
        return gain_sum + fold_rows(grad * scaled), shift_sum + fold_rows(grad)

    zero = jnp.zeros((8, D), F32)
    gain_sum, shift_sum = lax.fori_loop(0, half // 64, second_norm_back, (zero, zero))
    r.norm_grads[2:3, :] = jnp.sum(gain_sum, axis=0, keepdims=True)
    r.norm_grads[3:4, :] = jnp.sum(shift_sum, axis=0, keepdims=True)
    own_rows = aligned(h * half, half)
    other_rows = aligned(oh * half, half)
    for x in range(2):
        d_gathered = mm_nt(r.dat[own_rows, :], r.v_wo[x]).astype(BF16)
        for p in range(pairs):
            hot = r.oht[x, pair_rows(p), own_rows]
            r.dc[x, :, pair(p)] = fold(mm(hot, d_gathered[:, pair(p)]))[:SENT].astype(BF16)
    for x in range(2):
        scatter(r.dc.at[x], r.rs, me, x)
    send("dat", r.dat.at[own_rows], r.dat.at[own_rows], x_dev)

    send("fp_0", r.fp.at[h, own_rows], r.fp.at[h, own_rows], x_dev)
    tick("n", "out0", "out1")

    @pl.when(is_owner)
    def _():
        gathered_at_owner(r.rs, 2 * S, W, 2)
        rows = aligned(group * GROUP, GROUP)
        d_cluster = total_of(r.rs, 2 * S, W).astype(BF16)
        r.ag3[rows, :] = d_cluster
        spread(r.ag3, 2, W)
        product = d_cluster.astype(F32) * r.own_out[...]
        delta = pltpu.roll(r.own_lse[...], 8, 1)
        for p in range(pairs):
            block = product[:, pair(p)]
            delta = delta + jnp.where(
                lanes == 2 * p, jnp.sum(jnp.where(left, block, 0.0), axis=1, keepdims=True), 0.0
            )
            delta = delta + jnp.where(
                lanes == 2 * p + 1, jnp.sum(jnp.where(left, 0.0, block), axis=1, keepdims=True), 0.0
            )
        r.agdelta[rows, :] = delta
        spread(r.agdelta, 3, 256)

    tick("in0", "in1")
    spread_arrive(r.ag3, 2)
    spread_arrive(r.agdelta, 3)

    for p in range(pairs):
        d_probs = mm_nt(unfold(r.ag3[:, pair(p)]), r.v[:, pair(p)])
        factor = jnp.exp(column(r.stats[...], p) - column(r.agdelta[...], p, 8))
        probs = r.e[pair_rows(p), :] * factor
        r.pb[pair_rows(p), :] = probs.astype(BF16)
        d_scores = (probs * (d_probs - column(r.agdelta[...], p))).astype(BF16)
        r.dsb[pair_rows(p), :] = d_scores
        r.dcen[:, pair(p)] = fold(mm(d_scores, r.k[:, pair(p)]))[:SENT].astype(BF16)
    scatter(r.dcen, r.rs, s, h)

    for p in range(pairs):
        r.dkv[0, :, pair(p)] = (mm_tn(r.dsb[pair_rows(p), :], unfold(r.ag1[:, pair(p)])) * scale).astype(BF16)
        r.dkv[1, :, pair(p)] = mm_tn(r.pb[pair_rows(p), :], unfold(r.ag3[:, pair(p)])).astype(BF16)
    send("dkv", r.dkv, r.dkv_sib, sib_dev)

    def kv_part(rows):
        return mm_nt(r.dkv[0, rows, :], r.v_wk[...]) + mm_nt(r.dkv[1, rows, :], r.v_wv[...])

    r.kv_send[...] = kv_part(other_rows).astype(BF16)
    send("kv", r.kv_send, r.kv_recv, x_dev)
    arrive("dat")
    send("dat_sib", r.dat.at[:, sib_half], r.dat_sib, sib_dev)
    tick("n", "out0", "out1")

    tick("in0", "in1")
    arrive("dkv")
    if not ring:
        arrive("nrm")
    for i, name in enumerate(["k", "v"]):
        tile = mm_tn(r.nrm[:, own_half], r.dkv[i]) + mm_tn(r.nrm_sib[...], r.dkv_sib[i])
        r.part_small[i] = tile.astype(BF16)
        add_stream(name, r.part_small.at[i], rows_of(getattr(r, "fin_" + name), core * W), ring and r.ring_slim.at[i])
    tick("out0", "out1")
    arrive("gat")
    arrive("dat_sib")
    r.part_small[2] = (mm_tn(r.gat[h], r.dat[:, own_half]) + mm_tn(r.gat_sib[...], r.dat_sib[...])).astype(BF16)
    add_stream("o", r.part_small.at[2], rows_of(r.fin_o, 0, own_half), ring and r.ring_slim.at[2])
    r.dn_own[...] = kv_part(own_rows)
    @pl.when(is_owner)
    def _():
        gathered_at_owner(r.rs, S, W, 3)
        rows = aligned(group * GROUP, GROUP)
        r.ag4[h, rows, :] = (total_of(r.rs, S, W) * scale / r.divisor[...]).astype(BF16)
        spread(r.ag4.at[h], 4, W)

    tick("in0", "in1", "k", "v")

    spread_pass(r.ag4, 4, 1)
    tick(*pending())
    if ring:
        while "n" in pending():
            tick("n")
        size = W // n
        rows = pl.ds(pl.multiple_of(core * W + position * size, 16), size)
        for p in range(pairs):
            r.fin_q[rows, pair(p)] = mm(r.fin_n[:, pair_rows(p)], unfold(r.ag4[h, :, pair(p)])).astype(BF16)
        add_stream("q", r.fin_q.at[pl.ds(0, W)], rows_of(r.fin_q, core * W), None, at=ahead)
    else:
        for p in range(pairs):
            r.q[:, pair(p)] = mm(r.oh[h, :, pair_rows(p)], unfold(r.ag4[h, :, pair(p)])).astype(BF16)
        send("dq", r.q, r.dq_sib, sib_dev)
        arrive("dq")
        r.part_q[...] = (mm_tn(r.nrm[:, own_half], r.q[...]) + mm_tn(r.nrm_sib[...], r.dq_sib[...])).astype(BF16)
        add_stream("q", r.part_q, rows_of(r.fin_q, core * W), None)
    pass_arrive(r.ag4, 1)
    for x in range(2):
        for p in range(pairs):
            r.dq[x, :, pair(p)] = mm(r.oh[x, own_rows, pair_rows(p)], unfold(r.ag4[x, :, pair(p)])).astype(BF16)

    tick(*pending())
    arrive("kv")
    arrive("wq_sib")
    r.dn_own[...] += r.kv_recv[...].astype(F32) + mm_nt(r.dq[0], r.v_wq[0]) + mm_nt(r.dq[1], r.v_wq[1])

    def first_norm_back(i, carry):
        gain_sum, shift_sum = carry
        rows = pl.ds(pl.multiple_of(h * half + i * 64, 64), 64)
        at = aligned(i * 64, 64)
        scaled, inverse = normalize(r.v_tok[rows, :].astype(F32))
        grad = r.dn_own[at, :]
        grad_tokens = r.dres[at, :] + normalize_back(grad, gain(r.v_g1), scaled, inverse)
        r.gtok[rows, :] = grad_tokens.astype(BF16)
        return gain_sum + fold_rows(grad * scaled), shift_sum + fold_rows(grad)

    gain_sum, shift_sum = lax.fori_loop(0, half // 64, first_norm_back, (zero, zero))
    r.norm_grads[0:1, :] = jnp.sum(gain_sum, axis=0, keepdims=True)
    r.norm_grads[1:2, :] = jnp.sum(shift_sum, axis=0, keepdims=True)
    blocks = D // 128

    def norm_to(g, plane):
        cols = pl.ds(g * 128, 128)
        mine = jnp.logical_and(s == first + g, h == plane)
        copy = remote(
            r.norm_grads.at[:, cols], r.norm_rs.at[me], r.norm_send.at[g, plane], r.norm_sem.at[0], (first + g, plane)
        )
        return cols, mine, copy

    for plane in range(2):
        for g in range(blocks):
            cols, mine, copy = norm_to(g, plane)

            @pl.when(jnp.logical_not(mine))
            def _():
                copy.start()

            @pl.when(mine)
            def _():
                r.norm_rs[me] = r.norm_grads[:, cols]

    send("gtok", r.gtok.at[own_rows], r.gtok.at[own_rows], x_dev)
    send("fp_1", r.fp.at[h, other_rows], r.fp.at[h, other_rows], x_dev)
    tick(*pending())
    norm_owner = jnp.logical_and(s >= first, s < first + blocks)

    @pl.when(norm_owner)
    def _():
        block = r.norm_rs.at[pl.ds(0, 2 * S - 1)]
        remote(block, block, r.norm_send.at[0, 0], r.norm_sem.at[0], x_dev).wait_recv()

        def add(i, acc):
            return acc + r.norm_rs[i]

        cols = aligned(group * 128, 128)
        r.norm_fin[:, cols] = lax.fori_loop(0, 2 * S, add, jnp.zeros((8, 128), F32))
        block = r.norm_fin.at[:, cols]

        def to(k):
            remote(block, block, r.norm_send.at[blocks, 0], r.norm_sem.at[1 + group], (lax.rem(s + k + 1, S), h)).start()

        loop(S - 1, to)

    tick(*pending())
    for g in range(blocks):
        block = r.norm_fin.at[:, pl.ds(g * 128, 128)]

        @pl.when(s != first + g)
        def _():
            remote(block, block, r.norm_send.at[0, 0], r.norm_sem.at[1 + g], x_dev).wait_recv()

    while pending():
        tick(*pending())
    arrive("gtok")

    arrive("fp_0")
    arrive("fp_1")

    def block_out(i):
        rows = aligned(i * 64, 64)
        r.bout[rows, :] = (r.resid[rows, :] + r.fp[0, rows, :].astype(F32) + r.fp[1, rows, :].astype(F32)).astype(BF16)

    loop(T // 64, block_out)
    for st in streams:
        if st.shared:
            arrive(f"ring{st.i}")

    for finish in at_end:
        finish()
    for plane in range(2):
        for g in range(blocks):
            cols, mine, copy = norm_to(g, plane)

            @pl.when(jnp.logical_not(mine))
            def _():
                copy.wait_send()

    @pl.when(norm_owner)
    def _():
        block = r.norm_rs.at[pl.ds(0, S - 1)]
        remote(block, block, r.norm_send.at[blocks, 0], r.norm_sem.at[0], x_dev).wait_send()


def per_device(
    S,
    tokens,
    norm1_gain,
    norm1_shift,
    w_query,
    w_key,
    w_value,
    w_output,
    norm2_gain,
    norm2_shift,
    w_in,
    w_out,
    cluster_ids,
    masked_keys,
    cotangent,
):
    T, D = tokens.shape
    LH = cluster_ids.shape[1]
    W = w_query.shape[1]
    F = w_in.shape[1]
    n = S // 2
    ring = n <= 8
    cfg = SimpleNamespace(S=S, T=T, D=D, W=W, LH=LH, F=F, ring=ring, scatter_of=[0, 1, 2, 2, 3])

    M = -(-masked_keys.shape[0] // 1024) * 1024
    if M != masked_keys.shape[0]:
        masked_keys = jnp.pad(masked_keys, (0, M - masked_keys.shape[0]), constant_values=-1)
    cfg.M = M
    inputs = dict(
        tok=tokens,
        g1=norm1_gain,
        b1=norm1_shift,
        wq=w_query,
        wk=w_key,
        wv=w_value,
        wo=w_output,
        g2=norm2_gain,
        b2=norm2_shift,
        win=w_in,
        wout=w_out,
        ids=cluster_ids.T,
        masked=masked_keys.reshape(M // 128, 128),
        cot=cotangent,
    )
    outputs = dict(
        o_block=((T, D), BF16),
        o_tokens=((T, D), BF16),
        o_norm=((8, D), F32),
        o_q=((D, W), BF16),
        o_k=((D, W), BF16),
        o_v=((D, W), BF16),
        o_o=((W, D), BF16),
        o_in=((D, F), BF16),
        o_out=((F, D), BF16),
    )
    half = T // 2
    vmem = dict(
        v_tok=((T, D), BF16),
        v_g1=((D,), F32),
        v_b1=((D,), F32),
        v_wq=((2, D, W), BF16),
        v_wk=((D, W), BF16),
        v_wv=((D, W), BF16),
        v_wo=((2, W, D), BF16),
        v_g2=((D,), F32),
        v_b2=((D,), F32),
        v_win=((D, F), BF16),
        v_wout=((F, D), BF16),
        v_ids=((2, LH, T), jnp.int32),
        v_masked=((M // 128, 128), jnp.int32),
        v_cot=((2, T, D), BF16),
        nrm=((T, D), BF16),
        nrm_sib=((T, W), BF16),
        q=((T, W), BF16),
        k=((T, W), BF16),
        v=((T, W), BF16),
        oht=((2, LH * SLOT, T), BF16),
        oh=((2, T, LH * SLOT), BF16),
        sums=((SENT, W + 128), BF16),
        rs=((2 * S, GROUP, W + 128), BF16),
        divisor=((GROUP, W), F32),
        ag1=((SLOT, W), BF16),
        dact=((T, F), F32),
        e=((LH * SLOT, T), F32),
        numer=((SENT, W + 128), BF16),
        stats=((SLOT, 128), F32),
        own_out=((GROUP, W), F32),
        ag2=((2, SLOT, W), BF16),
        own_lse=((GROUP, 128), F32),
        gat=((2, T, W), BF16),
        gat_sib=((T, W), BF16),
        resid=((T, D), F32),
        n2=((2, T, D), BF16),
        act=((T, F), BF16),
        dup=((T, F), BF16),
        act_sib=((T, F // 2), BF16),
        dup_sib=((T, F // 2), BF16),
        dn_send=((half, D), BF16),
        dn_recv=((half, D), BF16),
        dn_own=((half, D), F32),
        dres=((half, D), F32),
        dat=((T, D), BF16),
        dat_sib=((T, W), BF16),
        dc=((2, SENT, W), BF16),
        ag3=((SLOT, W), BF16),
        agdelta=((SLOT, 128), F32),
        pb=((LH * SLOT, T), BF16),
        dsb=((LH * SLOT, T), BF16),
        dcen=((SENT, W), BF16),
        ag4=((2, SLOT, W), BF16),
        dkv=((2, T, W), BF16),
        dkv_sib=((2, T, W), BF16),
        kv_send=((half, D), BF16),
        kv_recv=((half, D), BF16),
        dq=((2, half, W), BF16),
        norm_grads=((8, D), F32),
        norm_rs=((2 * S, 8, 128), F32),
        fp=((2, T, D), BF16),
        part_out=((F // 2, D), BF16),
        part_in=((D, F // 2), BF16),
        part_small=((3, W, W), BF16),
        ids_sib=((LH, T), jnp.int32),
    )
    steps = 2 * (n - 1) if ring else 1
    if ring:
        vmem["ring_wide"] = ((4, n - 1, D // 2 // n, D), BF16)
        vmem["ring_slim"] = ((3, n - 1, W // n, W), BF16)
        vmem["ring_n"] = ((n - 1, W // n, LH * SLOT), BF16)
        vmem["oht_sib"] = ((LH * SLOT, T), BF16)
        vmem["part_n"] = ((W, LH * SLOT), BF16)
        vmem["fin_n"] = ((W // n, LH * SLOT), BF16)
    else:
        vmem["dq_sib"] = ((T, W), BF16)
        vmem["part_q"] = ((W, W), BF16)
    sems = dict(
        load_sem=(14,),
        ex_send=(32,),
        ex_recv=(32,),
        sc_send=(5, GROUPS),
        sc_recv=(4,),
        sp_send=(5,),
        sp_recv=(5, GROUPS),
        pass_send=(2, GROUPS),
        pass_recv=(2, GROUPS),
        ring_send=(STREAMS, steps),
        ring_recv=(STREAMS, steps),
        norm_send=(D // 128 + 1, 2),
        norm_sem=(D // 128 + 1,),
    )
    names = list(inputs) + list(outputs) + list(vmem) + list(sems)
    results = pl.pallas_call(
        functools.partial(kernel, cfg, names),
        out_shape=[pltpu.VMEM(*o) for o in outputs.values()],
        in_specs=[pl.BlockSpec(memory_space=pl.ANY)] * len(inputs),
        out_specs=[pl.BlockSpec(memory_space=pltpu.VMEM)] * len(outputs),
        scratch_shapes=[pltpu.VMEM(*b) for b in vmem.values()] + [pltpu.SemaphoreType.DMA(b) for b in sems.values()],
        compiler_params=pltpu.CompilerParams(collective_id=0, has_side_effects=True, vmem_limit_bytes=(54 if ring else 55) * 2**20),
        name="block",
    )(*inputs.values())
    block, grad_tokens, norms, *grads = results
    if not ring:
        grads = lax.psum(grads, "seq")
    block, gain1, shift1, gain2, shift2, grad_tokens, *grads = widen(block, norms, [grad_tokens] + grads)
    grad_q, grad_k, grad_v, grad_o, grad_in, grad_out = grads
    return (
        block,
        grad_tokens,
        gain1,
        shift1,
        grad_q,
        grad_k,
        grad_v,
        grad_o,
        gain2,
        shift2,
        grad_in,
        grad_out,
    )


def widen(block, norms, arrays):
    D = norms.shape[1]
    tiles = [
        (i, k * size, size)
        for i, a in enumerate(arrays)
        for size in [a.shape[0] // max(2, a.shape[0] // 256)]
        for k in range(a.shape[0] // size)
    ]
    count = len(arrays)

    def kernel(*refs):
        block_in, norms_in, *rest = refs
        ins, rest = rest[:count], rest[count:]
        block_out, *rest = rest
        norm_outs, rest = rest[:4], rest[4:]
        outs, rest = rest[:count], rest[count:]
        flat, rest = rest[:4], rest[4:]
        wide, rest = rest[:count], rest[count:]
        sem_out, sem = rest
        stores = []
        for k, (i, at, size) in enumerate(tiles):

            def cast(j, i=i, at=at):
                rows = pl.ds(pl.multiple_of(at + j * 32, 32), 32)
                wide[i][rows, :] = ins[i][rows, :].astype(F32)

            loop(size // 32, cast)
            rows = pl.ds(at, size)
            stores.append(pltpu.make_async_copy(wide[i].at[rows], outs[i].at[rows], sem_out.at[k]))
            stores[-1].start()
        for k in range(4):
            flat[k][...] = norms_in[k, :]
            stores.append(pltpu.make_async_copy(flat[k], norm_outs[k], sem.at[k]))
            stores[-1].start()
        stores.append(pltpu.make_async_copy(block_in, block_out, sem.at[4]))
        stores[-1].start()
        for store in stores:
            store.wait()

    out_shape = [jax.ShapeDtypeStruct(block.shape, block.dtype)]
    out_shape += [jax.ShapeDtypeStruct((D,), F32)] * 4
    out_shape += [jax.ShapeDtypeStruct(a.shape, F32) for a in arrays]
    anywhere = pl.BlockSpec(memory_space=pl.ANY)
    return pl.pallas_call(
        kernel,
        out_shape=out_shape,
        in_specs=[pl.BlockSpec(memory_space=pltpu.VMEM)] * (count + 2),
        out_specs=[anywhere] * len(out_shape),
        scratch_shapes=[pltpu.VMEM((D,), F32)] * 4
        + [pltpu.VMEM(a.shape, F32) for a in arrays]
        + [pltpu.SemaphoreType.DMA((len(tiles),)), pltpu.SemaphoreType.DMA((5,))],
        compiler_params=pltpu.CompilerParams(vmem_limit_bytes=20 * 2**20),
        name="widen",
    )(block, norms, *arrays)


def solution(mesh):
    columns, rows = P(None, "head"), P("head", None)
    by_token = P("seq", None)
    return jax.shard_map(
        functools.partial(per_device, mesh.shape["seq"]),
        mesh=mesh,
        in_specs=(by_token, P(), P(), columns, columns, columns, rows, P(), P(), columns, rows, P("seq", "head"), P(), by_token),
        out_specs=(by_token, by_token, P(), P(), columns, columns, columns, rows, P(), P(), columns, rows),
        check_vma=False,
    )
```

```python
import functools
from types import SimpleNamespace

import jax
import jax.numpy as jnp
from jax import lax
from jax.experimental import pallas as pl
from jax.experimental.pallas import tpu as pltpu
from jax.sharding import PartitionSpec as P

CLUSTERS = 100
EPSILON = 1e-05
MESH = pl.DeviceIdType.MESH
F32 = jnp.float32
BF16 = jnp.bfloat16
SLOT = 128
GROUP = 16
GROUPS = -(-CLUSTERS // GROUP)
SENT = GROUPS * GROUP
STREAMS = 9


def mm(a, b):
    return lax.dot_general(a, b, (((1,), (0,)), ((), ())), preferred_element_type=F32)


def mm_nt(a, b):
    return lax.dot_general(a, b, (((1,), (1,)), ((), ())), preferred_element_type=F32)


def mm_tn(a, b):
    return lax.dot_general(a, b, (((0,), (0,)), ((), ())), preferred_element_type=F32)


def aligned(index, size):
    return pl.ds(pl.multiple_of(index, size), size)


def remote(src, dst, send_sem, recv_sem, device):
    return pltpu.make_async_remote_copy(
        src_ref=src, dst_ref=dst, send_sem=send_sem, recv_sem=recv_sem, device_id=device, device_id_type=MESH
    )


def loop(count, body):
    def step(i, carry):
        body(i)
        return carry

    lax.fori_loop(0, count, step, 0)


def normalize(values):
    centred = values - jnp.mean(values, axis=-1, keepdims=True)
    inverse = lax.rsqrt(jnp.mean(centred * centred, axis=-1, keepdims=True) + EPSILON)
    return centred * inverse, inverse


def normalize_back(grad, gain, scaled, inverse):
    inner = grad * gain
    return inverse * (
        inner - jnp.mean(inner, axis=-1, keepdims=True) - scaled * jnp.mean(inner * scaled, axis=-1, keepdims=True)
    )


ERFC = (
    0.27643095583919713,
    0.2770312983463117,
    0.2368366418089808,
    0.21634403047784398,
    -0.05751923336137985,
    0.34364725799951945,
    -0.5200124379554546,
    0.2829391760305868,
    -0.05569765451595309,
)


def normal_share(x, bell):
    t = 1.0 / (1.0 + (0.49 * 0.5**0.5) * jnp.abs(x))
    series = 0.5 * ERFC[-1]
    for factor in ERFC[-2::-1]:
        series = series * t + 0.5 * factor
    tail = series * t * bell
    return jnp.where(x < 0, tail, 1.0 - tail)


def fold_rows(values):
    return jnp.sum(values.reshape(values.shape[0] // 8, 8, values.shape[1]), axis=0)


def kernel(cfg, names, *all_refs):
    r = SimpleNamespace(**dict(zip(names, all_refs)))
    r.bout, r.gtok, r.norm_fin = r.o_block, r.o_tokens, r.o_norm
    r.fin_q, r.fin_k, r.fin_v, r.fin_o, r.fin_in, r.fin_out = r.o_q, r.o_k, r.o_v, r.o_o, r.o_in, r.o_out
    S, T, D, W, LH, F = cfg.S, cfg.T, cfg.D, cfg.W, cfg.LH, cfg.F
    pairs = LH // 2
    half = T // 2
    scale = (W // LH) ** (-0.5)
    ring = cfg.ring
    n = S // 2
    s = lax.axis_index("seq")
    h = lax.axis_index("head")
    oh = 1 - h
    core = lax.rem(s, 2)
    chip = lax.div(s, 2)
    me = s * 2 + h
    x_dev = (s, oh)
    sib_dev = (s + 1 - 2 * core, h)
    first = S // 4
    is_owner = jnp.logical_and(s >= first, s < first + GROUPS)
    group = s - first
    lanes = lax.broadcasted_iota(jnp.int32, (1, 128), 1)
    left = lanes < 64

    def fold(block):
        return jnp.where(left, block[:SLOT], block[SLOT:])

    def unfold(block):
        zero = jnp.zeros_like(block)
        return jnp.concatenate([jnp.where(left, block, zero), jnp.where(left, zero, block)], axis=0)

    def expand(stats):
        return jnp.concatenate(
            [jnp.where(left, stats[:, 2 * p : 2 * p + 1], stats[:, 2 * p + 1 : 2 * p + 2]) for p in range(pairs)], axis=1
        )

    def column(stats, p, at=0):
        return jnp.concatenate(
            [stats[:, at + 2 * p : at + 2 * p + 1], stats[:, at + 2 * p + 1 : at + 2 * p + 2]], axis=0
        )

    def place(columns, p, at=0):
        rows = columns.shape[0] // 2
        return jnp.where(lanes == at + 2 * p, columns[:rows], 0.0) + jnp.where(
            lanes == at + 2 * p + 1, columns[rows:], 0.0
        )

    def pair(p):
        return slice(p * 128, (p + 1) * 128)

    def pair_rows(p):
        return slice(p * 2 * SLOT, (p + 1) * 2 * SLOT)

    at_end = []

    loads = {}
    for i, name in enumerate(
        ["ids", "tok", "g1", "b1", "wq", "wo", "wk", "wv", "cot", "wout", "masked", "win", "g2", "b2"]
    ):
        dst = getattr(r, "v_" + name)
        dst = {"cot": lambda d: d.at[0], "wq": lambda d: d.at[h], "wo": lambda d: d.at[h], "ids": lambda d: d.at[h]}.get(
            name, lambda d: d
        )(dst)
        loads[name] = pltpu.make_async_copy(getattr(r, name), dst, r.load_sem.at[i])

    barrier = pltpu.get_barrier_semaphore()

    def greet(k):
        other = lax.rem(me + k + 1, 2 * S)
        pl.semaphore_signal(
            barrier, inc=1, device_id=(lax.div(other, 2), lax.rem(other, 2)), device_id_type=MESH
        )

    loop(2 * S - 1, greet)
    for load in loads.values():
        load.start()

    exchanges = {}

    def send(name, src, dst, device):
        i = len(exchanges)
        copy = remote(src, dst, r.ex_send.at[i], r.ex_recv.at[i], device)
        copy.start()
        exchanges[name] = copy
        at_end.append(copy.wait_send)

    def arrive(name):
        exchanges[name].wait_recv()

    counters = {"scatter": 0, "spread": 0}

    def scatter(src, dst, slot, plane):
        i = counters["scatter"]
        counters["scatter"] += 1

        def at(g):
            rows = pl.ds(g * GROUP, GROUP)
            mine = jnp.logical_and(s == first + g, h == plane)
            copy = remote(
                src.at[rows], dst.at[slot, :, cols], r.sc_send.at[i, g], r.sc_recv.at[cfg.scatter_of[i]], (first + g, plane)
            )
            return rows, mine, copy

        cols = pl.ds(0, src.shape[1])

        for g in range(GROUPS):
            rows, mine, copy = at(g)

            @pl.when(jnp.logical_not(mine))
            def _():
                copy.start()

            @pl.when(mine)
            def _():
                dst[slot, :, cols] = src[rows, :]

        def finish():
            for g in range(GROUPS):
                rows, mine, copy = at(g)

                @pl.when(jnp.logical_not(mine))
                def _():
                    copy.wait_send()

        at_end.append(finish)

    def gathered_at_owner(buf, count, width, i):
        block = buf.at[pl.ds(0, count - 1), :, pl.ds(0, width)]
        remote(block, block, r.sc_send.at[0, 0], r.sc_recv.at[i], x_dev).wait_recv()

    def spread(buf, i, width):
        rows = aligned(group * GROUP, GROUP)
        block = buf.at[rows]

        def to(k):
            copy = remote(block, block, r.sp_send.at[i], r.sp_recv.at[i, group], (lax.rem(s + k + 1, S), h))
            copy.start()

        loop(S - 1, to)

        def finish():
            @pl.when(is_owner)
            def _():
                block = r.rs.at[pl.ds(0, S - 1), :, pl.ds(0, width)]
                remote(block, block, r.sp_send.at[i], r.sp_recv.at[i, 0], x_dev).wait_send()

        at_end.append(finish)

    def spread_arrive(buf, i):
        for g in range(GROUPS):

            @pl.when(s != first + g)
            def _():
                block = buf.at[pl.ds(g * GROUP, GROUP)]
                remote(block, block, r.sp_send.at[i], r.sp_recv.at[i, g], x_dev).wait_recv()

    def spread_pass(buf, i, j):
        for g in range(GROUPS):
            block = buf.at[h, pl.ds(g * GROUP, GROUP)]

            @pl.when(s != first + g)
            def _():
                remote(block, block, r.sp_send.at[i], r.sp_recv.at[i, g], x_dev).wait_recv()

            copy = remote(block, block, r.pass_send.at[j, g], r.pass_recv.at[j, g], x_dev)
            copy.start()
            at_end.append(copy.wait_send)

    def pass_arrive(buf, j):
        for g in range(GROUPS):
            block = buf.at[oh, pl.ds(g * GROUP, GROUP)]
            remote(block, block, r.pass_send.at[j, g], r.pass_recv.at[j, g], x_dev).wait_recv()

    def total_of(buf, count, width):
        def add(i, acc):
            return acc + jnp.sum(buf[aligned(i * 16, 16), :, :width].astype(F32), axis=0)

        return lax.fori_loop(0, count // 16, add, jnp.zeros((GROUP, width), F32))

    def split(values):
        high = values.astype(BF16).astype(F32)
        return high, values - high

    z_count = n // 2
    z, y = lax.div(chip, 2), lax.rem(chip, 2)
    position = jnp.where(y == 0, z, n - 1 - z)

    def device_at(p):
        p = lax.rem(p + n, n)
        return (2 * jnp.where(p < z_count, 2 * p, 2 * (n - 1 - p) + 1) + core, h)

    streams = []
    ahead, behind = n // 2, n - 1 - n // 2

    def add_stream(name, part, fin_block, recv, shared=True, at=0, last=2 * ahead):
        i = len(streams)
        st = SimpleNamespace(name=name, i=i, part=part, fin=fin_block, turn=at, last=last)
        st.chunk = part.shape[0] // n
        st.recv = recv
        st.shared = shared
        st.ways = [(1, ahead, 0), (-1, behind, ahead)] if i % 2 == 0 else [(-1, ahead, 0), (1, behind, ahead)]
        if ring:
            streams.append(st)
            advance(st)
        else:
            st.fin(0, part.shape[0])[...] = part[...]
        return st

    def part_chunk(st, k):
        return st.part.at[pl.ds(pl.multiple_of(lax.rem(k + 2 * n, n) * st.chunk, 16), st.chunk)]

    def fin_chunk(st, k):
        return st.fin(lax.rem(k + 2 * n, n) * st.chunk, st.chunk)

    def sum_copy(st, way, t):
        sign, hops, slot = way
        src = part_chunk(st, position + sign * hops) if t == 0 else st.recv.at[slot + t - 1]
        return remote(
            src,
            st.recv.at[slot + t],
            r.ring_send.at[st.i, slot + t],
            r.ring_recv.at[st.i, slot + t],
            device_at(position + sign),
        )

    def pass_copy(st, way, t):
        sign, hops, slot = way
        block = fin_chunk(st, position - sign * t)
        return remote(
            block,
            block,
            r.ring_send.at[st.i, n - 1 + slot + t],
            r.ring_recv.at[st.i, n - 1 + slot + t],
            device_at(position + sign),
        )

    def start(copy):
        copy.start()
        at_end.append(copy.wait_send)

    def advance(st):
        t = st.turn
        st.turn += 1
        if t <= ahead:
            for way in st.ways:
                sign, hops, slot = way
                if 0 < t <= hops and st.recv is not None:
                    sum_copy(st, way, t - 1).wait_recv()
                    if t < hops:
                        came = st.recv[slot + t - 1].astype(F32) + part_chunk(st, position + sign * (hops - t))[...].astype(F32)
                        st.recv[slot + t - 1] = came.astype(BF16)
                if t < hops:
                    start(sum_copy(st, way, t))
            if t == ahead:
                if st.recv is not None:
                    total = part_chunk(st, position)[...].astype(F32)
                    for sign, hops, slot in st.ways:
                        total = total + st.recv[slot + hops - 1].astype(F32)
                    fin_chunk(st, position)[...] = total.astype(BF16)
                for way in st.ways if st.last > ahead else []:
                    start(pass_copy(st, way, 0))
        elif t <= 2 * ahead:
            u = t - ahead
            for way in st.ways:
                sign, hops, slot = way
                if u <= hops:
                    block = fin_chunk(st, position - sign * u)
                    remote(
                        block, block, r.ring_send.at[st.i, 0], r.ring_recv.at[st.i, n - 1 + slot + u - 1], x_dev
                    ).wait_recv()
                if u < hops:
                    start(pass_copy(st, way, u))
            if u == ahead and st.shared:
                whole = st.fin(0, st.part.shape[0])
                send(f"ring{st.i}", whole, whole, sib_dev)

    def tick(*wanted):
        for name in wanted:
            for st in streams:
                if st.name == name and st.turn <= st.last:
                    advance(st)

    def pending():
        return [st.name for st in streams if st.turn <= st.last]

    if not ring:
        for name in ["fin_out", "fin_in", "fin_k", "fin_v", "fin_q", "fin_o"]:
            ref = getattr(r, name)
            ref[...] = jnp.zeros_like(ref)

    def rows_of(ref, base, cols=None):
        def block(at, size):
            rows = pl.ds(pl.multiple_of(base + at, 16), size)
            return ref.at[rows] if cols is None else ref.at[rows, cols]

        return block

    r.ag1[...] = jnp.zeros_like(r.ag1)
    r.ag3[...] = jnp.zeros_like(r.ag3)
    r.ag2[...] = jnp.zeros_like(r.ag2)
    r.ag4[...] = jnp.zeros_like(r.ag4)
    r.agdelta[...] = jnp.zeros_like(r.agdelta)
    r.norm_grads[...] = jnp.zeros_like(r.norm_grads)

    def onehot_t(ids, out):
        rows = lax.broadcasted_iota(jnp.int32, (SLOT, T), 0)
        for j in range(LH):
            out[j * SLOT : (j + 1) * SLOT, :] = jnp.where(rows == ids[j : j + 1, :], 1.0, 0.0).astype(BF16)

    def onehot(x):
        onehot_t(r.v_ids[x], r.oht.at[x])
        for p in range(pairs):
            r.oh[x, :, pair_rows(p)] = r.oht[x, pair_rows(p), :].T

    def gain(ref):
        return ref[...].reshape(1, D)

    loads["ids"].wait()
    onehot(h)
    for name in ["g1", "b1", "tok"]:
        loads[name].wait()

    def first_norm(i):
        rows = aligned(i * 64, 64)
        scaled, _ = normalize(r.v_tok[rows, :].astype(F32))
        r.nrm[rows, :] = (scaled * gain(r.v_g1) + gain(r.v_b1)).astype(BF16)

    loop(T // 64, first_norm)
    loads["wq"].wait()

    def project(weight, out):
        def tile(i):
            rows = aligned(i * 256, 256)
            out[rows, :] = mm(r.nrm[rows, :], weight).astype(BF16)

        loop(T // 256, tile)

    project(r.v_wq[h], r.q)
    counts = jnp.zeros((SLOT, 128), F32)
    ones = jnp.ones((T, 128), BF16)
    for p in range(pairs):
        hot = r.oht[h, pair_rows(p), :]
        r.sums[:, pair(p)] = fold(mm(hot, r.q[:, pair(p)]))[:SENT].astype(BF16)
        counts = counts + place(mm(hot, ones)[:, :1], p)
    high = jnp.where(counts >= 256.0, 256.0, 0.0) + jnp.where(counts >= 512.0, 256.0, 0.0)
    r.sums[:, W:] = (high + pltpu.roll(counts - high, 8, 1))[:SENT].astype(BF16)

    pl.semaphore_wait(barrier, 2 * S - 1)
    scatter(r.sums, r.rs, s, h)
    send("ids", r.v_ids.at[h], r.v_ids.at[h], x_dev)
    loads["wo"].wait()
    wo_mine = pl.ds(pl.multiple_of(core * (W // 2), 16), W // 2)
    send("wo", r.v_wo.at[h, wo_mine], r.v_wo.at[h, wo_mine], x_dev)
    wq_mine = pl.ds(pl.multiple_of(core * W, 16), W)
    send("wq", r.v_wq.at[h, wq_mine], r.v_wq.at[h, wq_mine], x_dev)
    sib_half = pl.ds(pl.multiple_of((1 - core) * W, 128), W)
    own_half = pl.ds(pl.multiple_of(core * W, 128), W)
    loads["cot"].wait()
    send("cot", r.v_cot.at[0], r.v_cot.at[1], sib_dev)
    send("nrm", r.nrm.at[:, sib_half], r.nrm_sib, sib_dev)
    send("ids_sib", r.v_ids.at[h], r.ids_sib, sib_dev)

    loads["wk"].wait()
    project(r.v_wk[...], r.k)
    loads["wv"].wait()
    project(r.v_wv[...], r.v)
    loads["wout"].wait()

    def d_act(j):
        cols = aligned(j * 256, 256)
        r.dact[:, cols] = mm_nt(r.v_cot[0], r.v_wout[cols, :])

    loop(F // 256, d_act)
    if ring:
        arrive("nrm")
        arrive("ids_sib")
        onehot_t(r.ids_sib[...], r.oht_sib)
        nrm_t, nrm_sib_t = r.nrm[:, own_half].T, r.nrm_sib[...].T
        for p in range(pairs):
            tile = mm_nt(nrm_t, r.oht[h, pair_rows(p), :]) + mm_nt(nrm_sib_t, r.oht_sib[pair_rows(p), :])
            r.part_n[:, pair_rows(p)] = tile.astype(BF16)

    @pl.when(is_owner)
    def _():
        gathered_at_owner(r.rs, S, W + 128, 0)
        total = total_of(r.rs, S, W + 128)
        counts = total[:, W:]
        divisor = jnp.maximum(expand(counts + pltpu.roll(counts, 120, 1)), 1.0)
        r.divisor[...] = divisor
        r.ag1[aligned(group * GROUP, GROUP), :] = (total[:, :W] / divisor).astype(BF16)
        spread(r.ag1, 0, W)

    if ring:
        add_stream("n", r.part_n, lambda at, size: r.fin_n, r.ring_n, shared=False, last=ahead)
    arrive("ids")
    onehot(oh)
    arrive("wo")
    send("wo_sib", r.v_wo.at[oh, wo_mine], r.v_wo.at[oh, wo_mine], sib_dev)
    loads["masked"].wait()
    positions = s * T + lax.broadcasted_iota(jnp.int32, (1, T), 1)

    def mark(i, hits):
        keys = r.v_masked[aligned(i * 8, 8), :].T
        for j in range(8):
            found = jnp.where(keys[:, j : j + 1] == positions, 1.0, 0.0)
            hits = jnp.maximum(hits, jnp.max(found.reshape(16, 8, T), axis=0))
        return hits

    hits = lax.fori_loop(0, cfg.M // 1024, mark, jnp.zeros((8, T), F32))
    keep = 1.0 - jnp.max(hits, axis=0, keepdims=True)
    spread_arrive(r.ag1, 0)

    stats = jnp.zeros((SLOT, 128), F32)
    sent_stats = jnp.zeros((SLOT, 128), F32)
    for p in range(pairs):
        scores = mm_nt(unfold(r.ag1[:, pair(p)]), r.k[:, pair(p)]) * scale
        scores = jnp.where(keep > 0, scores, -1e30)
        high, low = split(jnp.max(scores, axis=1, keepdims=True))
        low = low.astype(BF16).astype(F32)
        top = high + low
        weights = jnp.where(keep > 0, jnp.exp(scores - top), 0.0)
        r.e[pair_rows(p), :] = weights
        total_high, total_low = split(jnp.sum(weights, axis=1, keepdims=True))
        r.numer[:, pair(p)] = fold(mm(weights.astype(BF16), r.v[:, pair(p)]))[:SENT].astype(BF16)
        stats = stats + place(top, p)
        sent_stats = sent_stats + place(high, p) + place(low, p, 8) + place(total_high, p, 16) + place(total_low, p, 24)
    r.stats[...] = stats
    r.numer[:, W:] = sent_stats[:SENT].astype(BF16)
    scatter(r.numer, r.rs, s, h)
    tick("n")

    @pl.when(is_owner)
    def _():
        gathered_at_owner(r.rs, S, W + 128, 1)

        used = lanes < LH

        def stats_of(i):
            theirs = r.rs[aligned(i * 16, 16), :, W:].astype(F32).reshape(16 * GROUP, 128)
            return theirs, (theirs + pltpu.roll(theirs, 120, 1)).reshape(16, GROUP, 128)

        def highest(i, acc):
            return jnp.maximum(acc, jnp.max(stats_of(i)[1], axis=0))

        top = lax.fori_loop(0, S // 16, highest, jnp.full((GROUP, 128), -3e38, F32))

        def add(i, carry):
            numer, total = carry
            theirs, tops = stats_of(i)
            weight = jnp.where(used, jnp.exp(tops - top), 0.0).reshape(16 * GROUP, 128)
            totals = weight * (pltpu.roll(theirs, 112, 1) + pltpu.roll(theirs, 104, 1))
            part = expand(weight) * r.rs[aligned(i * 16, 16), :, :W].astype(F32).reshape(16 * GROUP, W)
            return (
                numer + jnp.sum(part.reshape(16, GROUP, W), axis=0),
                total + jnp.sum(totals.reshape(16, GROUP, 128), axis=0),
            )

        numer, total = lax.fori_loop(
            0, S // 16, add, (jnp.zeros((GROUP, W), F32), jnp.zeros((GROUP, 128), F32))
        )
        total = jnp.where(used, total, 1.0)
        out = numer / expand(total)
        r.own_out[...] = out
        r.own_lse[...] = jnp.where(used, top + jnp.log(total), 0.0)
        r.ag2[h, aligned(group * GROUP, GROUP), :] = out.astype(BF16)
        spread(r.ag2.at[h], 1, W)
        block = r.ag2.at[h, aligned(group * GROUP, GROUP)]

        def across(k):
            remote(block, block, r.pass_send.at[0, 0], r.pass_recv.at[0, group], (lax.rem(s + k, S), oh)).start()

        loop(S, across)

    for name in ["win", "g2", "b2"]:
        loads[name].wait()
    arrive("wo_sib")
    arrive("wq")
    send("wq_sib", r.v_wq.at[oh, wq_mine], r.v_wq.at[oh, wq_mine], sib_dev)
    tick("n")
    spread_arrive(r.ag2.at[h], 1)

    def across_sent():
        @pl.when(is_owner)
        def _():
            block = r.rs.at[pl.ds(0, S), :, pl.ds(0, W)]
            remote(block, block, r.pass_send.at[0, 0], r.pass_recv.at[0, 0], x_dev).wait_send()

    at_end.append(across_sent)

    def gather(x):
        for p in range(pairs):
            r.gat[x, :, pair(p)] = mm(r.oh[x, :, pair_rows(p)], unfold(r.ag2[x, :, pair(p)])).astype(BF16)

    gather(h)
    pass_arrive(r.ag2, 0)
    gather(oh)

    def second_norm(i):
        rows = aligned(i * 128, 128)
        attn = mm(r.gat[0, rows, :], r.v_wo[0]) + mm(r.gat[1, rows, :], r.v_wo[1])
        resid = r.v_tok[rows, :].astype(F32) + attn
        r.resid[rows, :] = resid
        scaled, _ = normalize(resid)
        r.n2[0, rows, :] = (scaled * gain(r.v_g2) + gain(r.v_b2)).astype(BF16)

    loop(T // 128, second_norm)
    tick("n")
    send("n2", r.n2.at[0], r.n2.at[1], sib_dev)
    send("gat", r.gat.at[h], r.gat_sib, sib_dev)

    def feed_forward(base):
        rows = aligned(base, half)

        def tile(j):
            cols = aligned(j * 256, 256)
            up = mm(r.n2[0, rows, :], r.v_win[:, cols])
            bell = jnp.exp(up * up * -0.5)
            share = normal_share(up, bell)
            density = bell * 0.3989422804014327
            r.act[rows, cols] = (up * share).astype(BF16)
            r.dup[rows, cols] = (r.dact[rows, cols] * (share + up * density)).astype(BF16)

        loop(F // 256, tile)

    def d_normed2(base, out):
        rows = aligned(base, half)

        def tile(j):
            cols = aligned(j * 256, 256)
            out[:, cols] = mm_nt(r.dup[rows, :], r.v_win[cols, :]).astype(out.dtype)

        loop(D // 256, tile)

    sib_units = pl.ds(pl.multiple_of((1 - core) * (F // 2), 128), F // 2)
    own_units = pl.ds(pl.multiple_of(core * (F // 2), 128), F // 2)
    feed_forward(oh * half)
    feed_forward(h * half)
    send("act", r.act.at[:, sib_units], r.act_sib, sib_dev)
    d_normed2(oh * half, r.dn_send)
    send("dn", r.dn_send, r.dn_recv, x_dev)
    send("dup", r.dup.at[:, sib_units], r.dup_sib, sib_dev)
    tick("n")

    arrive("act")
    arrive("cot")

    for k in range(2):
        base = k * (D // 2)
        cols = pl.ds(pl.multiple_of(core * (F // 2) + base, 128), D // 2)
        tile = mm_tn(r.act[:, cols], r.v_cot[0]) + mm_tn(r.act_sib[:, pl.ds(base, D // 2)], r.v_cot[1])
        r.part_out[pl.ds(base, D // 2), :] = tile.astype(BF16)
        add_stream(
            f"out{k}", r.part_out.at[pl.ds(base, D // 2)], rows_of(r.fin_out, core * (F // 2) + base), ring and r.ring_wide.at[k]
        )
    tick("n")
    arrive("dup")
    arrive("n2")

    for k in range(2):
        base = k * (D // 2)
        cols = pl.ds(base, D // 2)
        tile = mm_tn(r.n2[0, :, cols], r.dup[:, own_units]) + mm_tn(r.n2[1, :, cols], r.dup_sib[...])
        r.part_in[cols, :] = tile.astype(BF16)
        add_stream(
            f"in{k}", r.part_in.at[cols], rows_of(r.fin_in, base, own_units), ring and r.ring_wide.at[2 + k]
        )

    def ffn_part(j):
        cols = aligned(j * 256, 256)
        r.fp[h, :, cols] = mm(r.act[...], r.v_wout[:, cols]).astype(BF16)

    d_normed2(h * half, r.dn_own)
    loop(D // 256, ffn_part)
    tick("n", "out0", "out1", "in0", "in1")

    arrive("dn")

    def second_norm_back(i, carry):
        gain_sum, shift_sum = carry
        rows = pl.ds(pl.multiple_of(h * half + i * 64, 64), 64)
        at = aligned(i * 64, 64)
        scaled, inverse = normalize(r.resid[rows, :])
        grad = r.dn_own[at, :] + r.dn_recv[at, :].astype(F32)
        d_resid = r.v_cot[0, rows, :].astype(F32) + normalize_back(grad, gain(r.v_g2), scaled, inverse)
        r.dres[at, :] = d_resid
        r.dat[rows, :] = d_resid.astype(BF16)
        return gain_sum + fold_rows(grad * scaled), shift_sum + fold_rows(grad)

    zero = jnp.zeros((8, D), F32)
    gain_sum, shift_sum = lax.fori_loop(0, half // 64, second_norm_back, (zero, zero))
    r.norm_grads[2:3, :] = jnp.sum(gain_sum, axis=0, keepdims=True)
    r.norm_grads[3:4, :] = jnp.sum(shift_sum, axis=0, keepdims=True)
    own_rows = aligned(h * half, half)
    other_rows = aligned(oh * half, half)
    for x in range(2):
        d_gathered = mm_nt(r.dat[own_rows, :], r.v_wo[x]).astype(BF16)
        for p in range(pairs):
            hot = r.oht[x, pair_rows(p), own_rows]
            r.dc[x, :, pair(p)] = fold(mm(hot, d_gathered[:, pair(p)]))[:SENT].astype(BF16)
    for x in range(2):
        scatter(r.dc.at[x], r.rs, me, x)
    send("dat", r.dat.at[own_rows], r.dat.at[own_rows], x_dev)

    send("fp_0", r.fp.at[h, own_rows], r.fp.at[h, own_rows], x_dev)
    tick("n", "out0", "out1")

    @pl.when(is_owner)
    def _():
        gathered_at_owner(r.rs, 2 * S, W, 2)
        rows = aligned(group * GROUP, GROUP)
        d_cluster = total_of(r.rs, 2 * S, W).astype(BF16)
        r.ag3[rows, :] = d_cluster
        spread(r.ag3, 2, W)
        product = d_cluster.astype(F32) * r.own_out[...]
        delta = pltpu.roll(r.own_lse[...], 8, 1)
        for p in range(pairs):
            block = product[:, pair(p)]
            delta = delta + jnp.where(
                lanes == 2 * p, jnp.sum(jnp.where(left, block, 0.0), axis=1, keepdims=True), 0.0
            )
            delta = delta + jnp.where(
                lanes == 2 * p + 1, jnp.sum(jnp.where(left, 0.0, block), axis=1, keepdims=True), 0.0
            )
        r.agdelta[rows, :] = delta
        spread(r.agdelta, 3, 256)

    tick("in0", "in1")
    spread_arrive(r.ag3, 2)
    spread_arrive(r.agdelta, 3)

    for p in range(pairs):
        d_probs = mm_nt(unfold(r.ag3[:, pair(p)]), r.v[:, pair(p)])
        factor = jnp.exp(column(r.stats[...], p) - column(r.agdelta[...], p, 8))
        probs = r.e[pair_rows(p), :] * factor
        r.pb[pair_rows(p), :] = probs.astype(BF16)
        d_scores = (probs * (d_probs - column(r.agdelta[...], p))).astype(BF16)
        r.dsb[pair_rows(p), :] = d_scores
        r.dcen[:, pair(p)] = fold(mm(d_scores, r.k[:, pair(p)]))[:SENT].astype(BF16)
    scatter(r.dcen, r.rs, s, h)

    for p in range(pairs):
        r.dkv[0, :, pair(p)] = (mm_tn(r.dsb[pair_rows(p), :], unfold(r.ag1[:, pair(p)])) * scale).astype(BF16)
        r.dkv[1, :, pair(p)] = mm_tn(r.pb[pair_rows(p), :], unfold(r.ag3[:, pair(p)])).astype(BF16)
    send("dkv", r.dkv, r.dkv_sib, sib_dev)

    def kv_part(rows):
        return mm_nt(r.dkv[0, rows, :], r.v_wk[...]) + mm_nt(r.dkv[1, rows, :], r.v_wv[...])

    r.kv_send[...] = kv_part(other_rows).astype(BF16)
    send("kv", r.kv_send, r.kv_recv, x_dev)
    arrive("dat")
    send("dat_sib", r.dat.at[:, sib_half], r.dat_sib, sib_dev)
    tick("n", "out0", "out1")

    tick("in0", "in1")
    arrive("dkv")
    if not ring:
        arrive("nrm")
    for i, name in enumerate(["k", "v"]):
        tile = mm_tn(r.nrm[:, own_half], r.dkv[i]) + mm_tn(r.nrm_sib[...], r.dkv_sib[i])
        r.part_small[i] = tile.astype(BF16)
        add_stream(name, r.part_small.at[i], rows_of(getattr(r, "fin_" + name), core * W), ring and r.ring_slim.at[i])
    tick("out0", "out1")
    arrive("gat")
    arrive("dat_sib")
    r.part_small[2] = (mm_tn(r.gat[h], r.dat[:, own_half]) + mm_tn(r.gat_sib[...], r.dat_sib[...])).astype(BF16)
    add_stream("o", r.part_small.at[2], rows_of(r.fin_o, 0, own_half), ring and r.ring_slim.at[2])
    r.dn_own[...] = kv_part(own_rows)
    @pl.when(is_owner)
    def _():
        gathered_at_owner(r.rs, S, W, 3)
        rows = aligned(group * GROUP, GROUP)
        r.ag4[h, rows, :] = (total_of(r.rs, S, W) * scale / r.divisor[...]).astype(BF16)
        spread(r.ag4.at[h], 4, W)

    tick("in0", "in1", "k", "v")

    spread_pass(r.ag4, 4, 1)
    tick(*pending())
    if ring:
        while "n" in pending():
            tick("n")
        size = W // n
        rows = pl.ds(pl.multiple_of(core * W + position * size, 16), size)
        for p in range(pairs):
            r.fin_q[rows, pair(p)] = mm(r.fin_n[:, pair_rows(p)], unfold(r.ag4[h, :, pair(p)])).astype(BF16)
        add_stream("q", r.fin_q.at[pl.ds(0, W)], rows_of(r.fin_q, core * W), None, at=ahead)
    else:
        for p in range(pairs):
            r.q[:, pair(p)] = mm(r.oh[h, :, pair_rows(p)], unfold(r.ag4[h, :, pair(p)])).astype(BF16)
        send("dq", r.q, r.dq_sib, sib_dev)
        arrive("dq")
        r.part_q[...] = (mm_tn(r.nrm[:, own_half], r.q[...]) + mm_tn(r.nrm_sib[...], r.dq_sib[...])).astype(BF16)
        add_stream("q", r.part_q, rows_of(r.fin_q, core * W), None)
    pass_arrive(r.ag4, 1)
    for x in range(2):
        for p in range(pairs):
            r.dq[x, :, pair(p)] = mm(r.oh[x, own_rows, pair_rows(p)], unfold(r.ag4[x, :, pair(p)])).astype(BF16)

    tick(*pending())
    arrive("kv")
    arrive("wq_sib")
    r.dn_own[...] += r.kv_recv[...].astype(F32) + mm_nt(r.dq[0], r.v_wq[0]) + mm_nt(r.dq[1], r.v_wq[1])

    def first_norm_back(i, carry):
        gain_sum, shift_sum = carry
        rows = pl.ds(pl.multiple_of(h * half + i * 64, 64), 64)
        at = aligned(i * 64, 64)
        scaled, inverse = normalize(r.v_tok[rows, :].astype(F32))
        grad = r.dn_own[at, :]
        grad_tokens = r.dres[at, :] + normalize_back(grad, gain(r.v_g1), scaled, inverse)
        r.gtok[rows, :] = grad_tokens.astype(BF16)
        return gain_sum + fold_rows(grad * scaled), shift_sum + fold_rows(grad)

    gain_sum, shift_sum = lax.fori_loop(0, half // 64, first_norm_back, (zero, zero))
    r.norm_grads[0:1, :] = jnp.sum(gain_sum, axis=0, keepdims=True)
    r.norm_grads[1:2, :] = jnp.sum(shift_sum, axis=0, keepdims=True)
    blocks = D // 128

    def norm_to(g, plane):
        cols = pl.ds(g * 128, 128)
        mine = jnp.logical_and(s == first + g, h == plane)
        copy = remote(
            r.norm_grads.at[:, cols], r.norm_rs.at[me], r.norm_send.at[g, plane], r.norm_sem.at[0], (first + g, plane)
        )
        return cols, mine, copy

    for plane in range(2):
        for g in range(blocks):
            cols, mine, copy = norm_to(g, plane)

            @pl.when(jnp.logical_not(mine))
            def _():
                copy.start()

            @pl.when(mine)
            def _():
                r.norm_rs[me] = r.norm_grads[:, cols]

    send("gtok", r.gtok.at[own_rows], r.gtok.at[own_rows], x_dev)
    send("fp_1", r.fp.at[h, other_rows], r.fp.at[h, other_rows], x_dev)
    tick(*pending())
    norm_owner = jnp.logical_and(s >= first, s < first + blocks)

    @pl.when(norm_owner)
    def _():
        block = r.norm_rs.at[pl.ds(0, 2 * S - 1)]
        remote(block, block, r.norm_send.at[0, 0], r.norm_sem.at[0], x_dev).wait_recv()

        def add(i, acc):
            return acc + r.norm_rs[i]

        cols = aligned(group * 128, 128)
        r.norm_fin[:, cols] = lax.fori_loop(0, 2 * S, add, jnp.zeros((8, 128), F32))
        block = r.norm_fin.at[:, cols]

        def to(k):
            remote(block, block, r.norm_send.at[blocks, 0], r.norm_sem.at[1 + group], (lax.rem(s + k + 1, S), h)).start()

        loop(S - 1, to)

    tick(*pending())
    for g in range(blocks):
        block = r.norm_fin.at[:, pl.ds(g * 128, 128)]

        @pl.when(s != first + g)
        def _():
            remote(block, block, r.norm_send.at[0, 0], r.norm_sem.at[1 + g], x_dev).wait_recv()

    while pending():
        tick(*pending())
    arrive("gtok")

    arrive("fp_0")
    arrive("fp_1")

    def block_out(i):
        rows = aligned(i * 64, 64)
        r.bout[rows, :] = (r.resid[rows, :] + r.fp[0, rows, :].astype(F32) + r.fp[1, rows, :].astype(F32)).astype(BF16)

    loop(T // 64, block_out)
    for st in streams:
        if st.shared:
            arrive(f"ring{st.i}")

    for finish in at_end:
        finish()
    for plane in range(2):
        for g in range(blocks):
            cols, mine, copy = norm_to(g, plane)

            @pl.when(jnp.logical_not(mine))
            def _():
                copy.wait_send()

    @pl.when(norm_owner)
    def _():
        block = r.norm_rs.at[pl.ds(0, S - 1)]
        remote(block, block, r.norm_send.at[blocks, 0], r.norm_sem.at[0], x_dev).wait_send()


def per_device(
    S,
    tokens,
    norm1_gain,
    norm1_shift,
    w_query,
    w_key,
    w_value,
    w_output,
    norm2_gain,
    norm2_shift,
    w_in,
    w_out,
    cluster_ids,
    masked_keys,
    cotangent,
):
    T, D = tokens.shape
    LH = cluster_ids.shape[1]
    W = w_query.shape[1]
    F = w_in.shape[1]
    n = S // 2
    ring = n <= 8
    cfg = SimpleNamespace(S=S, T=T, D=D, W=W, LH=LH, F=F, ring=ring, scatter_of=[0, 1, 2, 2, 3])

    M = -(-masked_keys.shape[0] // 1024) * 1024
    if M != masked_keys.shape[0]:
        masked_keys = jnp.pad(masked_keys, (0, M - masked_keys.shape[0]), constant_values=-1)
    cfg.M = M
    inputs = dict(
        tok=tokens,
        g1=norm1_gain,
        b1=norm1_shift,
        wq=w_query,
        wk=w_key,
        wv=w_value,
        wo=w_output,
        g2=norm2_gain,
        b2=norm2_shift,
        win=w_in,
        wout=w_out,
        ids=cluster_ids.T,
        masked=masked_keys.reshape(M // 128, 128),
        cot=cotangent,
    )
    outputs = dict(
        o_block=((T, D), BF16),
        o_tokens=((T, D), BF16),
        o_norm=((8, D), F32),
        o_q=((D, W), BF16),
        o_k=((D, W), BF16),
        o_v=((D, W), BF16),
        o_o=((W, D), BF16),
        o_in=((D, F), BF16),
        o_out=((F, D), BF16),
    )
    half = T // 2
    vmem = dict(
        v_tok=((T, D), BF16),
        v_g1=((D,), F32),
        v_b1=((D,), F32),
        v_wq=((2, D, W), BF16),
        v_wk=((D, W), BF16),
        v_wv=((D, W), BF16),
        v_wo=((2, W, D), BF16),
        v_g2=((D,), F32),
        v_b2=((D,), F32),
        v_win=((D, F), BF16),
        v_wout=((F, D), BF16),
        v_ids=((2, LH, T), jnp.int32),
        v_masked=((M // 128, 128), jnp.int32),
        v_cot=((2, T, D), BF16),
        nrm=((T, D), BF16),
        nrm_sib=((T, W), BF16),
        q=((T, W), BF16),
        k=((T, W), BF16),
        v=((T, W), BF16),
        oht=((2, LH * SLOT, T), BF16),
        oh=((2, T, LH * SLOT), BF16),
        sums=((SENT, W + 128), BF16),
        rs=((2 * S, GROUP, W + 128), BF16),
        divisor=((GROUP, W), F32),
        ag1=((SLOT, W), BF16),
        dact=((T, F), F32),
        e=((LH * SLOT, T), F32),
        numer=((SENT, W + 128), BF16),
        stats=((SLOT, 128), F32),
        own_out=((GROUP, W), F32),
        ag2=((2, SLOT, W), BF16),
        own_lse=((GROUP, 128), F32),
        gat=((2, T, W), BF16),
        gat_sib=((T, W), BF16),
        resid=((T, D), F32),
        n2=((2, T, D), BF16),
        act=((T, F), BF16),
        dup=((T, F), BF16),
        act_sib=((T, F // 2), BF16),
        dup_sib=((T, F // 2), BF16),
        dn_send=((half, D), BF16),
        dn_recv=((half, D), BF16),
        dn_own=((half, D), F32),
        dres=((half, D), F32),
        dat=((T, D), BF16),
        dat_sib=((T, W), BF16),
        dc=((2, SENT, W), BF16),
        ag3=((SLOT, W), BF16),
        agdelta=((SLOT, 128), F32),
        pb=((LH * SLOT, T), BF16),
        dsb=((LH * SLOT, T), BF16),
        dcen=((SENT, W), BF16),
        ag4=((2, SLOT, W), BF16),
        dkv=((2, T, W), BF16),
        dkv_sib=((2, T, W), BF16),
        kv_send=((half, D), BF16),
        kv_recv=((half, D), BF16),
        dq=((2, half, W), BF16),
        norm_grads=((8, D), F32),
        norm_rs=((2 * S, 8, 128), F32),
        fp=((2, T, D), BF16),
        part_out=((F // 2, D), BF16),
        part_in=((D, F // 2), BF16),
        part_small=((3, W, W), BF16),
        ids_sib=((LH, T), jnp.int32),
    )
    steps = 2 * (n - 1) if ring else 1
    if ring:
        vmem["ring_wide"] = ((4, n - 1, D // 2 // n, D), BF16)
        vmem["ring_slim"] = ((3, n - 1, W // n, W), BF16)
        vmem["ring_n"] = ((n - 1, W // n, LH * SLOT), BF16)
        vmem["oht_sib"] = ((LH * SLOT, T), BF16)
        vmem["part_n"] = ((W, LH * SLOT), BF16)
        vmem["fin_n"] = ((W // n, LH * SLOT), BF16)
    else:
        vmem["dq_sib"] = ((T, W), BF16)
        vmem["part_q"] = ((W, W), BF16)
    sems = dict(
        load_sem=(14,),
        ex_send=(32,),
        ex_recv=(32,),
        sc_send=(5, GROUPS),
        sc_recv=(4,),
        sp_send=(5,),
        sp_recv=(5, GROUPS),
        pass_send=(2, GROUPS),
        pass_recv=(2, GROUPS),
        ring_send=(STREAMS, steps),
        ring_recv=(STREAMS, steps),
        norm_send=(D // 128 + 1, 2),
        norm_sem=(D // 128 + 1,),
    )
    names = list(inputs) + list(outputs) + list(vmem) + list(sems)
    results = pl.pallas_call(
        functools.partial(kernel, cfg, names),
        out_shape=[pltpu.VMEM(*o) for o in outputs.values()],
        in_specs=[pl.BlockSpec(memory_space=pl.ANY)] * len(inputs),
        out_specs=[pl.BlockSpec(memory_space=pltpu.VMEM)] * len(outputs),
        scratch_shapes=[pltpu.VMEM(*b) for b in vmem.values()] + [pltpu.SemaphoreType.DMA(b) for b in sems.values()],
        compiler_params=pltpu.CompilerParams(collective_id=0, has_side_effects=True, vmem_limit_bytes=(54 if ring else 55) * 2**20),
        name="block",
    )(*inputs.values())
    block, grad_tokens, norms, *grads = results
    if not ring:
        grads = lax.psum(grads, "seq")
    block, gain1, shift1, gain2, shift2, grad_tokens, *grads = widen(block, norms, [grad_tokens] + grads)
    grad_q, grad_k, grad_v, grad_o, grad_in, grad_out = grads
    return (
        block,
        grad_tokens,
        gain1,
        shift1,
        grad_q,
        grad_k,
        grad_v,
        grad_o,
        gain2,
        shift2,
        grad_in,
        grad_out,
    )


def widen(block, norms, arrays):
    D = norms.shape[1]
    tiles = [
        (i, k * size, size)
        for i, a in enumerate(arrays)
        for size in [a.shape[0] // max(2, a.shape[0] // 256)]
        for k in range(a.shape[0] // size)
    ]
    count = len(arrays)

    def kernel(*refs):
        block_in, norms_in, *rest = refs
        ins, rest = rest[:count], rest[count:]
        block_out, *rest = rest
        norm_outs, rest = rest[:4], rest[4:]
        outs, rest = rest[:count], rest[count:]
        flat, rest = rest[:4], rest[4:]
        wide, rest = rest[:count], rest[count:]
        sem_out, sem = rest
        stores = []
        for k, (i, at, size) in enumerate(tiles):

            def cast(j, i=i, at=at):
                rows = pl.ds(pl.multiple_of(at + j * 32, 32), 32)
                wide[i][rows, :] = ins[i][rows, :].astype(F32)

            loop(size // 32, cast)
            rows = pl.ds(at, size)
            stores.append(pltpu.make_async_copy(wide[i].at[rows], outs[i].at[rows], sem_out.at[k]))
            stores[-1].start()
        for k in range(4):
            flat[k][...] = norms_in[k, :]
            stores.append(pltpu.make_async_copy(flat[k], norm_outs[k], sem.at[k]))
            stores[-1].start()
        stores.append(pltpu.make_async_copy(block_in, block_out, sem.at[4]))
        stores[-1].start()
        for store in stores:
            store.wait()

    out_shape = [jax.ShapeDtypeStruct(block.shape, block.dtype)]
    out_shape += [jax.ShapeDtypeStruct((D,), F32)] * 4
    out_shape += [jax.ShapeDtypeStruct(a.shape, F32) for a in arrays]
    anywhere = pl.BlockSpec(memory_space=pl.ANY)
    return pl.pallas_call(
        kernel,
        out_shape=out_shape,
        in_specs=[pl.BlockSpec(memory_space=pltpu.VMEM)] * (count + 2),
        out_specs=[anywhere] * len(out_shape),
        scratch_shapes=[pltpu.VMEM((D,), F32)] * 4
        + [pltpu.VMEM(a.shape, F32) for a in arrays]
        + [pltpu.SemaphoreType.DMA((len(tiles),)), pltpu.SemaphoreType.DMA((5,))],
        compiler_params=pltpu.CompilerParams(vmem_limit_bytes=20 * 2**20),
        name="widen",
    )(block, norms, *arrays)


def solution(mesh):
    columns, rows = P(None, "head"), P("head", None)
    by_token = P("seq", None)
    return jax.shard_map(
        functools.partial(per_device, mesh.shape["seq"]),
        mesh=mesh,
        in_specs=(by_token, P(), P(), columns, columns, columns, rows, P(), P(), columns, rows, P("seq", "head"), P(), by_token),
        out_specs=(by_token, by_token, P(), P(), columns, columns, columns, rows, P(), P(), columns, rows),
        check_vma=False,
    )
```
